32 devices in a mesh: dp: 4 (over y, x), seq: 8 (over z, core).
Axes of the slice: x: 2, y: 2, z: 4, core: 2. Of those that a mesh axis runs over, the one named last changes fastest.
Arguments:
- layer_input: bfloat16 [4, 1024, 2048], P('dp', 'seq'), may hold values from -6 to 6
- doc_lengths: int32 [4, 8], P('dp'), may hold values from 1 to 960, 1024 in all within a row
- language: int32 [4], P('dp'), may hold values from 0 to 6
- lang_table: bfloat16 [7, 2048], P(None, ('dp', 'seq')), may hold values from -3 to 3
- attn_norm_gain: bfloat16 [2048], P(('dp', 'seq')), may hold values from 0.5 to 1.5
- attn_norm_bias: bfloat16 [2048], P(('dp', 'seq')), may hold values from -3 to 3
- qkv_weight: bfloat16 [2048, 6144], P(('dp', 'seq')), may hold values from -0.125 to 0.125
- qkv_bias: bfloat16 [3, 2048], P(None, ('dp', 'seq')), may hold values from -0.119628906 to 0.119628906
- out_weight: bfloat16 [2048, 2048], P(('dp', 'seq')), may hold values from -2 to 2
- mlp_norm_gain: bfloat16 [2048], P(('dp', 'seq')), may hold values from 0.5 to 1.5
- mlp_norm_bias: bfloat16 [2048], P(('dp', 'seq')), may hold values from -3 to 3
- gate_weight: bfloat16 [2048, 5632], P(None, ('dp', 'seq')), may hold values from -0.125 to 0.125
- up_weight: bfloat16 [2048, 5632], P(None, ('dp', 'seq')), may hold values from -0.125 to 0.125
- down_weight: bfloat16 [5632, 2048], P(('dp', 'seq')), may hold values from -0.078125 to 0.078125
- cotangent: bfloat16 [4, 1024, 2048], P('dp', 'seq'), may hold values from -6 to 6
Outputs:
- layer_output: bfloat16 [4, 1024, 2048], P('dp', 'seq')
- grad_input: float32 [4, 1024, 2048], P('dp', 'seq')
- grad_lang_table: float32 [7, 2048], P(None, ('dp', 'seq'))
- grad_attn_norm_gain: float32 [2048], P(('dp', 'seq'))
- grad_attn_norm_bias: float32 [2048], P(('dp', 'seq'))
- grad_qkv_weight: float32 [2048, 6144], P(('dp', 'seq'))
- grad_qkv_bias: float32 [3, 2048], P(None, ('dp', 'seq'))
- grad_out_weight: float32 [2048, 2048], P(('dp', 'seq'))
- grad_mlp_norm_gain: float32 [2048], P(('dp', 'seq'))
- grad_mlp_norm_bias: float32 [2048], P(('dp', 'seq'))
- grad_gate_weight: float32 [2048, 5632], P(None, ('dp', 'seq'))
- grad_up_weight: float32 [2048, 5632], P(None, ('dp', 'seq'))
- grad_down_weight: float32 [5632, 2048], P(('dp', 'seq'))
The draws below stay inside these ranges and needn't reach their ends.
Inputs may be any that keep to these rules, and one draw needn't show every extreme that they name: `doc_lengths`: in each row the 8 lengths sum to 1024, and the longest is exactly 960.
All inputs are finite; a program needn't handle non-finite values.
Results may differ from the reference program's by a relative error of at most 0.015.
Values may be sent and summed in bfloat16 or wider, within the bound.
No kernel may reach another device: no remote copies, remote signals or barrier semaphores. Data moves between devices by JAX's collectives and lax.ppermute only.
A program may use at most 256 MiB of HBM per device.

```python
import math
from functools import partial
import jax
import jax.numpy as jnp
import numpy as np
from jax import lax

D = 2048
HEADS = 32
HEAD = 64
ROT = 16
FF = 5632
LANGS = 7
DOCS = 8
TOK_DEV = 128
LEN = 1024
ROWS = 4


def with_ends(result, rng, least, top_value):
    dims = result.shape
    index_at = [jax.random.randint(jax.random.fold_in(rng, axis), (), 0, dims[axis]) for axis in range(len(dims))]
    result = result.at[tuple(index_at)].set(least)
    longest = dims.index(max(dims))
    index_at[longest] = (index_at[longest] + 1) % dims[longest]
    return result.at[tuple(index_at)].set(top_value)


def block_levels(rng, extent, pieces, low, high):
    loudness, own = 1.0, jax.random.fold_in(rng, 6)
    for axis_at, parts in pieces:
        heights = jnp.exp(jax.random.uniform(jax.random.fold_in(own, axis_at), (parts,), jnp.float32, low / len(pieces), high / len(pieces)))
        loudness = loudness * jnp.repeat(heights, extent[axis_at] // parts).reshape([-1 if axis == axis_at else 1 for axis in range(len(extent))])
    return loudness


def profile(number_of, total, bound, lean):
    weights = [(1 << 20) // math.isqrt(standing ** lean) + 1 for standing in range(2, number_of + 1)]
    surplus, holding = total - bound - (number_of - 1), [1] * (number_of - 1)
    while surplus > 0:
        candidates = [i for i in range(number_of - 1) if holding[i] < bound]
        whole, left = sum([weights[i] for i in candidates]), surplus
        for i in candidates:
            addition = min(bound - holding[i], max(1, left * weights[i] // whole), surplus)
            holding[i] = holding[i] + addition
            surplus = surplus - addition
    return np.array([bound] + holding)


def ragged_sizes(key, count, total, bound, skew):
    if count == 2:
        one = jax.random.randint(key, (), max(1, total - bound), min(bound, total - 1) + 1)
        return jnp.stack([one, total - one])
    tallies = jnp.asarray(profile(count, total, bound, skew), jnp.int32)
    pairs = (count - 1) // 2
    giver, taker = tallies[1:1 + 2 * pairs:2], tallies[2:2 + 2 * pairs:2]
    room = jnp.minimum(giver - 1, bound - taker)
    passed = jax.random.randint(jax.random.fold_in(key, 1), (pairs,), 0, 1 << 20) % (room + 1)
    tallies = tallies.at[1:1 + 2 * pairs:2].set(giver - passed).at[2:2 + 2 * pairs:2].set(taker + passed)
    return tallies[jax.random.permutation(jax.random.fold_in(key, 2), count)]


def gaussian(key, extent, scale, limit, split=(), kind=jnp.bfloat16):
    array = jax.random.normal(key, extent, jnp.float32) * scale
    if len(split) > 0:
        array = block_levels(key, extent, split, -0.22, 0.18) * array
    return jnp.clip(array, min=-limit, max=limit).astype(kind)


def setup_inputs(seed: int = 0) -> dict:
    key_list = jax.random.split(jax.random.key(seed), 16)
    return {
        "layer_input": gaussian(key_list[0], (ROWS, LEN, D), 1.0, 6.0, ((0, 4), (1, 8))),
        "doc_lengths": jax.vmap(lambda own: ragged_sizes(own, DOCS, LEN, LEN - TOK_DEV // 2, 2))(jax.random.split(key_list[1], ROWS)).reshape((ROWS, DOCS)).astype(jnp.int32),
        "language": with_ends(jax.random.randint(key_list[2], (ROWS,), 0, LANGS), jax.random.fold_in(key_list[2], 1), 0, LANGS - 1).astype(jnp.int32),
        "lang_table": gaussian(key_list[3], (LANGS, D), 0.5, 3.0, ((1, 32),)),
        "attn_norm_gain": jnp.clip(1.0 + 0.1 * jax.random.normal(key_list[4], (D,), jnp.float32), 0.5, 1.5).astype(jnp.bfloat16),
        "attn_norm_bias": gaussian(key_list[5], (D,), 0.5, 3.0, ((0, 32),)),
        "qkv_weight": gaussian(key_list[6], (D, 3 * D), D ** -0.5, 0.125, ((0, 32),)),
        "qkv_bias": gaussian(key_list[7], (3, D), 0.02, 0.119628906, ((1, 32),)),
        "out_weight": gaussian(key_list[8], (D, D), (max(D * 4 // LEN, 1)) ** -0.5, 2.0, ((0, 32),)),
        "mlp_norm_gain": jnp.clip(1.0 + 0.1 * jax.random.normal(key_list[9], (D,), jnp.float32), 0.5, 1.5).astype(jnp.bfloat16),
        "mlp_norm_bias": gaussian(key_list[10], (D,), 0.5, 3.0, ((0, 32),)),
        "gate_weight": gaussian(key_list[11], (D, FF), D ** -0.5, 0.125, ((1, 32),)),
        "up_weight": gaussian(key_list[12], (D, FF), D ** -0.5, 0.125, ((1, 32),)),
        "down_weight": gaussian(key_list[13], (FF, D), FF ** -0.5, 0.078125, ((0, 32),)),
        "cotangent": gaussian(key_list[14], (ROWS, LEN, D), 1.0, 6.0, ((0, 4), (1, 8))),
    }


EPS = 1e-05
BASE = 10000.0
NEG = -1e+30
HIGH = lax.Precision.HIGHEST

@jax.custom_vjp
def low(v):
    return lax.optimization_barrier(v.astype(jnp.bfloat16)).astype(jnp.float32)

@jax.custom_vjp
def low_back(v):
    return v

def low_keep(v):
    return (low(v), None)

def low_pass(kept, grad):
    return (grad,)

def back_keep(v):
    return (v, None)

def back_low(kept, grad):
    return (low(grad),)
low.defvjp(low_keep, low_pass)
low_back.defvjp(back_keep, back_low)

def layer_norm(values, gain, bias):
    average = lax.optimization_barrier(jnp.mean(values, axis=-1, keepdims=True))
    centered = values - average
    variance = lax.optimization_barrier(jnp.mean(centered * centered, axis=-1, keepdims=True))
    return centered * lax.rsqrt(variance + EPS) * gain + bias

def row_tables(doc_lengths, length):
    ends = jnp.cumsum(doc_lengths).astype(jnp.int32)
    starts = ends - doc_lengths
    places = jnp.arange(length, dtype=jnp.int32)
    segment = lax.optimization_barrier(jnp.sum((places[:, None] >= ends[None, :]).astype(jnp.int32), axis=1))
    member = segment[:, None] == jnp.arange(ends.shape[0], dtype=jnp.int32)[None, :]
    offsets = lax.optimization_barrier(jnp.sum(jnp.where(member, starts[None, :], 0), axis=1))
    position = (places - offsets).astype(jnp.float32)
    half_rot = ROT // 2
    freq = BASE ** (-(2.0 * jnp.arange(half_rot, dtype=jnp.float32)) / ROT)
    angles = position[:, None] * freq[None, :]
    return (segment, jnp.cos(angles), jnp.sin(angles))

def rotate(values, cosines, sines, direction):
    half_rot = ROT // 2
    former = values[..., :half_rot]
    latter = values[..., half_rot:ROT]
    cos_part = cosines[:, None, :]
    sin_part = direction * sines[:, None, :]
    return jnp.concatenate([former * cos_part - latter * sin_part, latter * cos_part + former * sin_part, values[..., ROT:]], axis=-1)

def attend_head(allowed, trio):
    query, key_rows, value_rows = trio
    scores = low_back(jnp.dot(query, key_rows.T, precision=HIGH) * HEAD ** (-0.5))
    scores = jnp.where(allowed, scores, NEG)
    soft = jax.nn.softmax(scores, axis=-1)
    return jnp.dot(low(soft), value_rows, precision=HIGH)

def forward(language, tables, layer_input, lang_table, attn_norm_gain, attn_norm_bias, qkv_weight, qkv_bias, out_weight, mlp_norm_gain, mlp_norm_bias, gate_weight, up_weight, down_weight):
    resid_in = layer_input + jnp.take(lang_table, language, axis=0)[:, None, :]
    normed_attn = low(layer_norm(resid_in, attn_norm_gain, attn_norm_bias)).reshape(ROWS * LEN, D)
    projected = low_back(low(jnp.dot(normed_attn, qkv_weight, precision=HIGH) + qkv_bias.reshape(3 * D)))
    projected = projected.reshape(ROWS, LEN, 3, HEADS, HEAD)
    places = jnp.arange(LEN, dtype=jnp.int32)
    causal = places[None, :] <= places[:, None]
    contexts = []
    for row in range(ROWS):
        segment, cosines, sines = tables[row]
        allowed = causal & (segment[:, None] == segment[None, :])
        rot_query = low(rotate(projected[row, :, 0], cosines, sines, 1.0))
        rot_key = low(rotate(projected[row, :, 1], cosines, sines, 1.0))
        head_step = jax.checkpoint(partial(attend_head, allowed))
        per_head = lax.map(head_step, (jnp.swapaxes(rot_query, 0, 1), jnp.swapaxes(rot_key, 0, 1), jnp.swapaxes(projected[row, :, 2], 0, 1)))
        contexts.append(jnp.swapaxes(per_head, 0, 1).reshape(LEN, D))
    context = low_back(low(jnp.stack(contexts).reshape(ROWS * LEN, D)))
    attn_out = low_back(jnp.dot(context, out_weight, precision=HIGH)).reshape(ROWS, LEN, D)
    resid_mid = resid_in + attn_out
    normed_mlp = low(layer_norm(resid_mid, mlp_norm_gain, mlp_norm_bias)).reshape(ROWS * LEN, D)
    gate_values = low_back(jnp.dot(normed_mlp, gate_weight, precision=HIGH))
    up_values = low_back(jnp.dot(normed_mlp, up_weight, precision=HIGH))
    hidden = low(jax.nn.silu(gate_values) * up_values)
    mlp_out = low_back(jnp.dot(hidden, down_weight, precision=HIGH)).reshape(ROWS, LEN, D)
    return resid_mid + mlp_out

def reference(layer_input, doc_lengths, language, lang_table, attn_norm_gain, attn_norm_bias, qkv_weight, qkv_bias, out_weight, mlp_norm_gain, mlp_norm_bias, gate_weight, up_weight, down_weight, cotangent):
    tables = [row_tables(doc_lengths[row], LEN) for row in range(ROWS)]
    primals = (layer_input.astype(jnp.float32), lang_table.astype(jnp.float32), attn_norm_gain.astype(jnp.float32), attn_norm_bias.astype(jnp.float32), qkv_weight.astype(jnp.float32), qkv_bias.astype(jnp.float32), out_weight.astype(jnp.float32), mlp_norm_gain.astype(jnp.float32), mlp_norm_bias.astype(jnp.float32), gate_weight.astype(jnp.float32), up_weight.astype(jnp.float32), down_weight.astype(jnp.float32))
    output, pullback = jax.vjp(partial(forward, language, tables), *primals)
    grads = pullback(cotangent.astype(jnp.float32))
    return (output.astype(jnp.bfloat16), grads[0], grads[1], grads[2], grads[3], grads[4], grads[5], grads[6], grads[7], grads[8], grads[9], grads[10], grads[11])
```

```python
import jax
import jax.numpy as jnp
from jax import lax
from jax.sharding import PartitionSpec as P

D = 2048
HEADS = 32
HEAD = 64
ROT = 16
LANGS = 7


EPS = 1e-05
BASE = 10000.0
NEG = -1e30


def contract(left, right, left_dim, right_dim):
    return lax.dot_general(
        left, right, (((left_dim,), (right_dim,)), ((), ())), preferred_element_type=jnp.float32
    )


def norm_forward(values, gain, bias):
    average = jnp.mean(values, axis=-1, keepdims=True)
    centered = values - average
    variance = jnp.mean(centered * centered, axis=-1, keepdims=True)
    inverse = lax.rsqrt(variance + EPS)
    scaled = centered * inverse
    return (scaled * gain + bias, scaled, inverse)


def norm_backward(grad_normed, scaled, inverse, gain):
    grad_scaled = grad_normed * gain
    grad_values = inverse * (
        grad_scaled
        - jnp.mean(grad_scaled, axis=-1, keepdims=True)
        - scaled * jnp.mean(grad_scaled * scaled, axis=-1, keepdims=True)
    )
    return (grad_values, jnp.sum(grad_normed * scaled, axis=0), jnp.sum(grad_normed, axis=0))


def row_tables(doc_lengths, length):
    ends = jnp.cumsum(doc_lengths)
    starts = ends - doc_lengths
    places = jnp.arange(length, dtype=jnp.int32)
    segment = jnp.sum((places[:, None] >= ends[None, :]).astype(jnp.int32), axis=1)
    member = segment[:, None] == jnp.arange(ends.shape[0], dtype=jnp.int32)[None, :]
    offsets = jnp.sum(jnp.where(member, starts[None, :], 0), axis=1)
    position = (places - offsets).astype(jnp.float32)
    half_rot = ROT // 2
    freq = BASE ** (-(2.0 * jnp.arange(half_rot, dtype=jnp.float32)) / ROT)
    angles = position[:, None] * freq[None, :]
    return (segment, jnp.cos(angles), jnp.sin(angles))


def rotate(values, cosines, sines, direction):
    half_rot = ROT // 2
    former = values[..., :half_rot]
    latter = values[..., half_rot:ROT]
    cos_part = cosines[:, None, :]
    sin_part = direction * sines[:, None, :]
    return jnp.concatenate(
        [
            former * cos_part - latter * sin_part,
            latter * cos_part + former * sin_part,
            values[..., ROT:],
        ],
        axis=-1,
    )


def block_scores(query_block, key_heads, segment, index_query, index_key, block_rows):
    key_block = lax.dynamic_slice_in_dim(key_heads, index_key * block_rows, block_rows, 0)
    raw = jnp.einsum(
        "qhd,khd->hqk", query_block, key_block, preferred_element_type=jnp.float32
    ) * HEAD ** (-0.5)
    query_seg = lax.dynamic_slice_in_dim(segment, index_query * block_rows, block_rows, 0)
    key_seg = lax.dynamic_slice_in_dim(segment, index_key * block_rows, block_rows, 0)
    offsets = jnp.arange(block_rows, dtype=jnp.int32)
    allowed = (query_seg[:, None] == key_seg[None, :]) & (
        index_key * block_rows + offsets[None, :] <= index_query * block_rows + offsets[:, None]
    )
    allowed = allowed[None]
    return (jnp.where(allowed, raw, NEG), allowed, key_block)


def attention_forward(queries, key_heads, value_heads, segment):
    length, heads_here = (queries.shape[0], queries.shape[1])
    block_rows = min(512, length)

    def per_block(index_query):
        query_block = lax.dynamic_slice_in_dim(queries, index_query * block_rows, block_rows, 0)

        def gather_stats(index_key, carry):
            running, denominator = carry
            masked, allowed, unused = block_scores(
                query_block, key_heads, segment, index_query, index_key, block_rows
            )
            newest = jnp.maximum(running, jnp.max(masked, axis=-1))
            denominator = denominator * jnp.exp(running - newest) + jnp.sum(
                jnp.where(allowed, jnp.exp(masked - newest[..., None]), 0.0), axis=-1
            )
            return (newest, denominator)

        initial = (
            jnp.full((heads_here, block_rows), NEG, jnp.float32),
            jnp.zeros((heads_here, block_rows), jnp.float32),
        )
        running, denominator = lax.fori_loop(0, index_query + 1, gather_stats, initial)
        logsum = running + jnp.log(denominator)

        def weigh(index_key, accumulated):
            masked, allowed, unused = block_scores(
                query_block, key_heads, segment, index_query, index_key, block_rows
            )
            probabilities = jnp.where(allowed, jnp.exp(masked - logsum[..., None]), 0.0).astype(
                jnp.bfloat16
            )
            value_block = lax.dynamic_slice_in_dim(
                value_heads, index_key * block_rows, block_rows, 0
            )
            return accumulated + jnp.einsum(
                "hqk,khd->qhd", probabilities, value_block, preferred_element_type=jnp.float32
            )

        accumulated = lax.fori_loop(
            0, index_query + 1, weigh, jnp.zeros((block_rows, heads_here, HEAD), jnp.float32)
        )
        return (accumulated, logsum)

    context, logsum = lax.map(per_block, jnp.arange(length // block_rows, dtype=jnp.int32))
    return (context.reshape(length, heads_here, HEAD), logsum)


def attention_backward(queries, key_heads, value_heads, segment, context, logsum, grad_context):
    length, heads_here = (queries.shape[0], queries.shape[1])
    block_rows = min(512, length)
    deltas = jnp.sum(grad_context.astype(jnp.float32) * context, axis=-1)
    zeros_all = jnp.zeros((length, heads_here, HEAD), jnp.float32)

    def per_query(index_query, carry):
        grad_queries, grad_keys, grad_values = carry
        query_block = lax.dynamic_slice_in_dim(queries, index_query * block_rows, block_rows, 0)
        grad_block = lax.dynamic_slice_in_dim(grad_context, index_query * block_rows, block_rows, 0)
        delta_block = lax.dynamic_slice_in_dim(deltas, index_query * block_rows, block_rows, 0).T
        logsum_block = logsum[index_query]

        def per_key(index_key, inner):
            grad_query, grad_keys, grad_values = inner
            masked, allowed, key_block = block_scores(
                query_block, key_heads, segment, index_query, index_key, block_rows
            )
            soft = jnp.where(allowed, jnp.exp(masked - logsum_block[..., None]), 0.0)
            value_block = lax.dynamic_slice_in_dim(
                value_heads, index_key * block_rows, block_rows, 0
            )
            grad_soft = jnp.einsum(
                "qhd,khd->hqk", grad_block, value_block, preferred_element_type=jnp.float32
            )
            grad_scores = (soft * (grad_soft - delta_block[..., None])).astype(jnp.bfloat16)
            grad_query = grad_query + jnp.einsum(
                "hqk,khd->qhd", grad_scores, key_block, preferred_element_type=jnp.float32
            ) * HEAD ** (-0.5)
            key_part = jnp.einsum(
                "hqk,qhd->khd", grad_scores, query_block, preferred_element_type=jnp.float32
            ) * HEAD ** (-0.5)
            value_part = jnp.einsum(
                "hqk,qhd->khd",
                soft.astype(jnp.bfloat16),
                grad_block,
                preferred_element_type=jnp.float32,
            )
            offset = index_key * block_rows
            grad_keys = lax.dynamic_update_slice_in_dim(
                grad_keys,
                lax.dynamic_slice_in_dim(grad_keys, offset, block_rows, 0) + key_part,
                offset,
                0,
            )
            grad_values = lax.dynamic_update_slice_in_dim(
                grad_values,
                lax.dynamic_slice_in_dim(grad_values, offset, block_rows, 0) + value_part,
                offset,
                0,
            )
            return (grad_query, grad_keys, grad_values)

        initial = (jnp.zeros((block_rows, heads_here, HEAD), jnp.float32), grad_keys, grad_values)
        grad_query, grad_keys, grad_values = lax.fori_loop(0, index_query + 1, per_key, initial)
        grad_queries = lax.dynamic_update_slice_in_dim(
            grad_queries, grad_query, index_query * block_rows, 0
        )
        return (grad_queries, grad_keys, grad_values)

    return lax.fori_loop(0, length // block_rows, per_query, (zeros_all, zeros_all, zeros_all))


def gate_backward(gate_values, up_values, grad_hidden):
    sigmoid_gate = jax.nn.sigmoid(gate_values)
    silu_gate = gate_values * sigmoid_gate
    grad_gate = (
        grad_hidden * up_values * sigmoid_gate * (1.0 + gate_values * (1.0 - sigmoid_gate))
    ).astype(jnp.bfloat16)
    grad_up = (grad_hidden * silu_gate).astype(jnp.bfloat16)
    return (grad_gate, grad_up)


def permute(value, axis, offset):
    size = lax.axis_size(axis)
    return lax.ppermute(value, axis, [(i, i ^ offset) for i in range(size)])


def gather_dp(piece):
    return [piece] + [permute(piece, "dp", k) for k in range(1, lax.axis_size("dp"))]


def scatter_dp(pieces):
    total = pieces[0].astype(jnp.float32)
    for k in range(1, len(pieces)):
        total = total + permute(pieces[k].astype(jnp.bfloat16), "dp", k).astype(jnp.float32)
    return total


def gather_seq(piece):
    chips = lax.axis_size("seq") // 2
    same = [piece] + [permute(piece, "seq", 2 * k) for k in range(1, chips)]
    pieces = []
    for part in same:
        pieces += [part, permute(part, "seq", 1)]
    return pieces


def scatter_seq(terms):
    size = lax.axis_size("seq")
    block = terms.shape[0] // size
    stack = terms.reshape(size // 2, 2, block, terms.shape[1])
    pairs = stack[:, 0].astype(jnp.float32) + permute(
        stack[:, 1].astype(jnp.bfloat16), "seq", 1
    ).astype(jnp.float32)
    total = pairs[0]
    for k in range(1, size // 2):
        total = total + permute(pairs[k].astype(jnp.bfloat16), "seq", 2 * k).astype(jnp.float32)
    return total


def reorder(values, index, count):
    block = values.shape[0] // count
    result = jnp.zeros_like(values)
    for m in range(count):
        result = lax.dynamic_update_slice_in_dim(
            result, values[m * block : (m + 1) * block], (index ^ m) * block, 0
        )
    return result


def place(pieces, index):
    block = pieces[0].shape[0]
    result = jnp.zeros((block * len(pieces),) + pieces[0].shape[1:], pieces[0].dtype)
    for k, piece in enumerate(pieces):
        result = lax.dynamic_update_slice_in_dim(result, piece, (index ^ k) * block, 0)
    return result


def per_device(
    layer_input,
    doc_lengths,
    language,
    lang_table,
    attn_norm_gain,
    attn_norm_bias,
    qkv_weight,
    qkv_bias,
    out_weight,
    mlp_norm_gain,
    mlp_norm_bias,
    gate_weight,
    up_weight,
    down_weight,
    cotangent,
):
    tokens = layer_input.shape[1]
    groups = lax.axis_size("seq")
    rows = lax.axis_size("dp")
    devices = rows * groups
    at_dp = lax.axis_index("dp")
    at_seq = lax.axis_index("seq")
    length = tokens * groups
    heads_here = HEADS // groups
    local_width = heads_here * HEAD
    own = D // devices
    owner = [(i, (i % groups) * rows + i // groups) for i in range(devices)]
    back = [(b, a) for a, b in owner]
    small = jnp.concatenate(
        [
            lang_table,
            attn_norm_gain[None],
            attn_norm_bias[None],
            mlp_norm_gain[None],
            mlp_norm_bias[None],
            qkv_bias,
            jnp.broadcast_to(language.astype(jnp.bfloat16)[:, None], (1, own)),
            jnp.zeros((1, own), jnp.bfloat16),
        ],
        axis=0,
    )
    spread = lax.all_to_all(
        jnp.broadcast_to(small[None], (devices,) + small.shape),
        ("dp", "seq"),
        split_axis=0,
        concat_axis=0,
        tiled=True,
    )
    table = jnp.swapaxes(spread, 0, 1).reshape(small.shape[0], D).astype(jnp.float32)
    languages = spread[:, LANGS + 7, 0].astype(jnp.int32)
    gain_attn = table[LANGS]
    bias_attn = table[LANGS + 1]
    gain_mlp = table[LANGS + 2]
    bias_mlp = table[LANGS + 3]
    bias_qkv = lax.dynamic_slice_in_dim(
        table[LANGS + 4 : LANGS + 7], at_seq * local_width, local_width, 1
    ).reshape(3 * local_width)
    chooser = (jnp.arange(LANGS, dtype=jnp.int32) == language[0]).astype(jnp.float32)
    lang_row = jnp.sum(chooser[:, None] * table[:LANGS], axis=0)[None, :]
    qkv_part = lax.all_to_all(
        qkv_weight.reshape(own, 3, groups, local_width).transpose(2, 0, 1, 3).reshape(
            groups, own, 3 * local_width
        ),
        "seq",
        split_axis=0,
        concat_axis=0,
        tiled=True,
    ).reshape(groups * own, 3 * local_width)
    head_qkv = place(gather_dp(qkv_part), at_dp)
    head_out = place(gather_dp(lax.ppermute(out_weight, ("dp", "seq"), back)), at_dp)
    cols_gate = jnp.concatenate(gather_dp(gate_weight.T), axis=0)
    cols_up = jnp.concatenate(gather_dp(up_weight.T), axis=0)
    cols_down = jnp.concatenate(gather_dp(down_weight), axis=0)
    segment, cosines, sines = row_tables(doc_lengths[0], length)
    grad_out = cotangent[0]
    input_all = jnp.concatenate(gather_seq(layer_input[0]), axis=0)
    grad_all = jnp.concatenate(gather_seq(grad_out), axis=0)
    normed_all = norm_forward(input_all.astype(jnp.float32) + lang_row, gain_attn, bias_attn)[
        0
    ].astype(jnp.bfloat16)
    resid_in = layer_input[0].astype(jnp.float32) + lang_row
    unused, scaled_attn, inverse_attn = norm_forward(resid_in, gain_attn, bias_attn)
    projected = (
        jnp.dot(normed_all, head_qkv, preferred_element_type=jnp.float32) + bias_qkv
    ).astype(jnp.bfloat16)
    head_rows = reorder(projected, at_seq, groups).reshape(length, 3, heads_here, HEAD)
    rot_query = rotate(head_rows[:, 0].astype(jnp.float32), cosines, sines, 1.0).astype(
        jnp.bfloat16
    )
    rot_key = rotate(head_rows[:, 1].astype(jnp.float32), cosines, sines, 1.0).astype(jnp.bfloat16)
    value_heads = head_rows[:, 2]
    context, logsum = attention_forward(rot_query, rot_key, value_heads, segment)
    context_all = reorder(
        context.astype(jnp.bfloat16).reshape(length, local_width), at_seq, groups
    )
    resid_mid = resid_in + scatter_seq(
        jnp.dot(context_all, head_out, preferred_element_type=jnp.float32)
    )
    normed_mlp, scaled_mlp, inverse_mlp = norm_forward(resid_mid, gain_mlp, bias_mlp)
    rows_all = jnp.concatenate(gather_seq(normed_mlp.astype(jnp.bfloat16)), axis=0)
    gate_values = contract(rows_all, cols_gate, 1, 1)
    up_values = contract(rows_all, cols_up, 1, 1)
    hidden = (jax.nn.silu(gate_values) * up_values).astype(jnp.bfloat16)
    grad_hidden = contract(grad_all, cols_down, 1, 1)
    grad_gate, grad_up = gate_backward(gate_values, up_values, grad_hidden)
    grad_rows = contract(grad_gate, cols_gate, 1, 0) + contract(grad_up, cols_up, 1, 0)
    grad_normed_mlp = scatter_seq(grad_rows)
    mlp_out = scatter_seq(jnp.dot(hidden, cols_down, preferred_element_type=jnp.float32))
    layer_output = (resid_mid + mlp_out).astype(jnp.bfloat16)

    def to_owner(terms):
        return scatter_dp(jnp.split(terms.astype(jnp.bfloat16), rows, axis=0))

    out_gate = to_owner(contract(grad_gate, rows_all, 0, 0)).T
    out_up = to_owner(contract(grad_up, rows_all, 0, 0)).T
    out_down = to_owner(contract(hidden, grad_all, 0, 0))
    grad_mid_norm, grad_gain_mlp, grad_bias_mlp = norm_backward(
        grad_normed_mlp, scaled_mlp, inverse_mlp, gain_mlp
    )
    grad_mid = grad_out.astype(jnp.float32) + grad_mid_norm
    branch_all = jnp.concatenate(gather_seq(grad_mid.astype(jnp.bfloat16)), axis=0)
    grad_heads = reorder(
        contract(branch_all, head_out, 1, 1).astype(jnp.bfloat16), at_seq, groups
    ).reshape(length, heads_here, HEAD)
    grad_queries, grad_keys, grad_values = attention_backward(
        rot_query, rot_key, value_heads, segment, context, logsum, grad_heads
    )
    grad_query_raw = rotate(grad_queries, cosines, sines, -1.0).reshape(length, local_width)
    grad_key_raw = rotate(grad_keys, cosines, sines, -1.0).reshape(length, local_width)
    grad_stack = reorder(
        jnp.concatenate(
            [grad_query_raw, grad_key_raw, grad_values.reshape(length, local_width)], axis=1
        ).astype(jnp.bfloat16),
        at_seq,
        groups,
    )
    grad_normed_attn = scatter_seq(contract(grad_stack, head_qkv, 1, 1))
    grad_in_norm, grad_gain_attn, grad_bias_attn = norm_backward(
        grad_normed_attn, scaled_attn, inverse_attn, gain_attn
    )
    grad_input = grad_mid + grad_in_norm

    def dp_terms(terms):
        block = terms.shape[0] // rows
        return [
            lax.dynamic_slice_in_dim(terms, (at_dp ^ k) * block, block, 0) for k in range(rows)
        ]

    slice_summed = scatter_dp(dp_terms(contract(normed_all, grad_stack, 0, 0).astype(jnp.bfloat16)))
    grad_qkv_out = (
        lax.all_to_all(
            slice_summed.astype(jnp.bfloat16).reshape(groups, own, 3 * local_width),
            "seq",
            split_axis=0,
            concat_axis=0,
            tiled=True,
        )
        .reshape(groups, own, 3, local_width)
        .transpose(1, 2, 0, 3)
        .reshape(own, 3 * D)
        .astype(jnp.float32)
    )
    head_out_terms = scatter_dp(
        dp_terms(contract(context_all, branch_all, 0, 0).astype(jnp.bfloat16))
    )
    out_proj = lax.ppermute(head_out_terms, ("dp", "seq"), owner)
    grad_bias_qkv = jnp.sum(grad_stack.astype(jnp.float32), axis=0).reshape(3, local_width)
    terms = jnp.concatenate(
        [
            grad_gain_attn[None],
            grad_bias_attn[None],
            grad_gain_mlp[None],
            grad_bias_mlp[None],
            jnp.sum(grad_input, axis=0)[None],
            lax.dynamic_update_slice(
                jnp.zeros((3, D), jnp.float32), grad_bias_qkv, (0, at_seq * local_width)
            ),
        ],
        axis=0,
    )
    arrived = lax.all_to_all(
        terms.reshape(terms.shape[0], devices, own).swapaxes(0, 1),
        ("dp", "seq"),
        split_axis=0,
        concat_axis=0,
        tiled=True,
    )
    summed = jnp.sum(arrived, axis=0)
    members = (languages[:, None] == jnp.arange(LANGS, dtype=jnp.int32)[None, :]).astype(
        jnp.float32
    )
    lang_g = jnp.sum(members[:, :, None] * arrived[:, 4][:, None, :], axis=0)
    return (
        layer_output[None],
        grad_input[None],
        lang_g,
        summed[0],
        summed[1],
        grad_qkv_out,
        summed[5:8],
        out_proj,
        summed[2],
        summed[3],
        out_gate,
        out_up,
        out_down,
    )


def solution(mesh):
    placed = (
        P("dp", "seq", None),
        P("dp", None),
        P("dp"),
        P(None, ("dp", "seq")),
        P(("dp", "seq")),
        P(("dp", "seq")),
        P(("dp", "seq"), None),
        P(None, ("dp", "seq")),
        P(("dp", "seq"), None),
        P(("dp", "seq")),
        P(("dp", "seq")),
        P(None, ("dp", "seq")),
        P(None, ("dp", "seq")),
        P(("dp", "seq"), None),
        P("dp", "seq", None),
    )
    return jax.shard_map(
        per_device,
        mesh=mesh,
        in_specs=placed,
        out_specs=(
            P("dp", "seq", None),
            P("dp", "seq", None),
            P(None, ("dp", "seq")),
            P(("dp", "seq")),
            P(("dp", "seq")),
            P(("dp", "seq"), None),
            P(None, ("dp", "seq")),
            P(("dp", "seq"), None),
            P(("dp", "seq")),
            P(("dp", "seq")),
            P(None, ("dp", "seq")),
            P(None, ("dp", "seq")),
            P(("dp", "seq"), None),
        ),
        check_vma=False,
    )
```

```python
import jax
import jax.numpy as jnp
from jax import lax
from jax.experimental import pallas as pl
from jax.experimental.pallas import tpu as pltpu
from jax.sharding import PartitionSpec as P

D = 2048
HEADS = 32
HEAD = 64
ROT = 16
LANGS = 7


EPS = 1e-05
BASE = 10000.0
NEG = -1e30


def contract(left, right, left_dim, right_dim):
    return lax.dot_general(
        left, right, (((left_dim,), (right_dim,)), ((), ())), preferred_element_type=jnp.float32
    )


def norm_forward(values, gain, bias):
    average = jnp.mean(values, axis=-1, keepdims=True)
    centered = values - average
    variance = jnp.mean(centered * centered, axis=-1, keepdims=True)
    inverse = lax.rsqrt(variance + EPS)
    scaled = centered * inverse
    return (scaled * gain + bias, scaled, inverse)


def norm_backward(grad_normed, scaled, inverse, gain):
    grad_scaled = grad_normed * gain
    grad_values = inverse * (
        grad_scaled
        - jnp.mean(grad_scaled, axis=-1, keepdims=True)
        - scaled * jnp.mean(grad_scaled * scaled, axis=-1, keepdims=True)
    )
    return (grad_values, jnp.sum(grad_normed * scaled, axis=0), jnp.sum(grad_normed, axis=0))


def row_tables(doc_lengths, length):
    ends = jnp.cumsum(doc_lengths)
    starts = ends - doc_lengths
    places = jnp.arange(length, dtype=jnp.int32)
    segment = jnp.sum((places[:, None] >= ends[None, :]).astype(jnp.int32), axis=1)
    member = segment[:, None] == jnp.arange(ends.shape[0], dtype=jnp.int32)[None, :]
    offsets = jnp.sum(jnp.where(member, starts[None, :], 0), axis=1)
    position = (places - offsets).astype(jnp.float32)
    half_rot = ROT // 2
    freq = BASE ** (-(2.0 * jnp.arange(half_rot, dtype=jnp.float32)) / ROT)
    angles = position[:, None] * freq[None, :]
    return (offsets, jnp.cos(angles), jnp.sin(angles))


def head_lanes(shape, dim, head):
    place = lax.broadcasted_iota(jnp.int32, shape, dim)
    return (place >= head * HEAD) & (place < (head + 1) * HEAD)


def turn(values, tables, direction):
    lanes = values.shape[1]
    cosines, sines_former, sines_latter = tables
    after = pltpu.roll(values, lanes - ROT // 2, 1)
    before = pltpu.roll(values, ROT // 2, 1)
    return values * cosines + direction * (before * sines_latter - after * sines_former)


def allowed_pairs(first_ref, start, block, keys):
    key_at = lax.broadcasted_iota(jnp.int32, (keys, block), 0)
    query_at = start + lax.broadcasted_iota(jnp.int32, (keys, block), 1)
    return (key_at >= first_ref[:, pl.ds(start, block)]) & (key_at <= query_at)


def over_blocks(length, block, step):
    count = length // block
    if count <= 4:
        for i in range(count):
            step(i * block, (i + 1) * block)
    else:

        def body(i, carry):
            step(pl.multiple_of(i * block, block), length)
            return carry

        lax.fori_loop(0, count, body, 0)


def forward_kernel(
    qkv_ref, cos_ref, former_ref, latter_ref, first_ref,
    query_ref, key_ref, context_ref, logsum_ref, value_t,
):
    length, width = query_ref.shape
    lanes = cos_ref.shape[1]
    block = min(256, length)
    tables = (cos_ref[...], former_ref[...], latter_ref[...])
    for group in range(width // lanes):
        part = slice(group * lanes, (group + 1) * lanes)

        def columns(c):
            begin = c * width + group * lanes
            return qkv_ref[:, begin : begin + lanes].astype(jnp.float32)

        query_ref[:, part] = turn(columns(0), tables, 1.0).astype(jnp.bfloat16)
        key_ref[:, part] = turn(columns(1), tables, 1.0).astype(jnp.bfloat16)
        value_t[...] = columns(2).T.astype(jnp.bfloat16)

        def step(start, keys):
            queries = query_ref[pl.ds(start, block), part].astype(jnp.float32) * HEAD ** (-0.5)
            allowed = allowed_pairs(first_ref, start, block, keys)
            found = []
            for head in range(lanes // HEAD):
                own = jnp.where(head_lanes(queries.shape, 1, head), queries, 0.0)
                scores = contract(key_ref[0:keys, part], own.astype(jnp.bfloat16), 1, 1)
                scores = jnp.where(allowed, scores, NEG)
                most = jnp.max(scores, axis=0, keepdims=True)
                weights = jnp.exp(scores - most)
                total = jnp.sum(weights, axis=0, keepdims=True)
                probs = (weights * (1.0 / total)).astype(jnp.bfloat16)
                logsum_ref[
                    pl.ds(group * (lanes // HEAD) + head, 1), pl.ds(start, block)
                ] = most + jnp.log(total)
                context = contract(value_t[:, 0:keys], probs, 1, 0)
                found.append(context[head * HEAD : (head + 1) * HEAD])
            context_ref[pl.ds(start, block), part] = (
                jnp.concatenate(found, axis=0).T.astype(jnp.bfloat16)
            )

        over_blocks(length, block, step)


def backward_kernel(
    query_ref, key_ref, qkv_ref, context_grad_ref, logsum_ref, cos_ref, former_ref, latter_ref,
    first_ref, grad_ref, key_t, grad_query, grad_key, grad_value,
):
    length, width = query_ref.shape
    lanes = cos_ref.shape[1]
    block = min(256, length)
    scale = HEAD ** (-0.5)
    tables = (cos_ref[...], former_ref[...], latter_ref[...])
    for group in range(width // lanes):
        part = slice(group * lanes, (group + 1) * lanes)
        value_part = slice(2 * width + group * lanes, 2 * width + (group + 1) * lanes)
        key_t[...] = key_ref[:, part].astype(jnp.float32).T.astype(jnp.bfloat16)
        grad_key[...] = jnp.zeros_like(grad_key)
        grad_value[...] = jnp.zeros_like(grad_value)

        def step(start, keys):
            queries = query_ref[pl.ds(start, block), part].astype(jnp.float32) * scale
            grads = context_grad_ref[pl.ds(start, block), part].astype(jnp.float32)
            allowed = allowed_pairs(first_ref, start, block, keys)
            found = []
            for head in range(lanes // HEAD):
                mine = head_lanes(queries.shape, 1, head)
                own_query = jnp.where(mine, queries, 0.0).astype(jnp.bfloat16)
                own_grad = jnp.where(mine, grads, 0.0).astype(jnp.bfloat16)
                scores = contract(key_ref[0:keys, part], own_query, 1, 1)
                logsum = logsum_ref[
                    pl.ds(group * (lanes // HEAD) + head, 1), pl.ds(start, block)
                ]
                soft = jnp.exp(jnp.where(allowed, scores, NEG) - logsum)
                grad_soft = contract(qkv_ref[0:keys, value_part], own_grad, 1, 1)
                weighed = soft * grad_soft
                delta = jnp.sum(weighed, axis=0, keepdims=True)
                grad_scores = (weighed - soft * delta).astype(jnp.bfloat16)
                grad_value[0:keys] += contract(soft.astype(jnp.bfloat16), own_grad, 1, 0)
                grad_key[0:keys] += contract(grad_scores, own_query, 1, 0)
                turned = contract(key_t[:, 0:keys], grad_scores, 1, 0)
                found.append(turned[head * HEAD : (head + 1) * HEAD])
            grad_query[pl.ds(start, block), :] = jnp.concatenate(found, axis=0).T * scale

        over_blocks(length, block, step)
        for c, grads in ((0, grad_query), (1, grad_key)):
            begin = c * width + group * lanes
            grad_ref[:, begin : begin + lanes] = turn(grads[...], tables, -1.0).astype(
                jnp.bfloat16
            )
        grad_ref[:, value_part] = grad_value[...].astype(jnp.bfloat16)


def rotation_tables(cosines, sines, lanes):
    length = cosines.shape[0]
    rest = jnp.ones((length, HEAD - ROT), jnp.float32)
    none = jnp.zeros_like(sines)
    heads = lanes // HEAD
    return (
        jnp.tile(jnp.concatenate([cosines, cosines, rest], axis=1), (1, heads)),
        jnp.tile(jnp.concatenate([sines, none, 0.0 * rest], axis=1), (1, heads)),
        jnp.tile(jnp.concatenate([none, sines, 0.0 * rest], axis=1), (1, heads)),
    )


VMEM_BYTES = 48 * 1024 * 1024


def attention_forward(projected, tables, first):
    length, width = projected.shape[0], projected.shape[1] // 3
    lanes = tables[0].shape[1]
    rows = jax.ShapeDtypeStruct((length, width), jnp.bfloat16)
    return pl.pallas_call(
        forward_kernel,
        out_shape=(
            rows,
            rows,
            rows,
            jax.ShapeDtypeStruct((width // HEAD, length), jnp.float32),
        ),
        scratch_shapes=[pltpu.VMEM((lanes, length), jnp.bfloat16)],
        compiler_params=pltpu.CompilerParams(vmem_limit_bytes=VMEM_BYTES),
        cost_estimate=pl.CostEstimate(
            flops=4 * length * length * width,
            bytes_accessed=12 * length * width,
            transcendentals=length * length * width // HEAD,
        ),
        name="attention_forward",
    )(projected, *tables, first)


def attention_backward(queries, key_heads, projected, grad_context, logsum, tables, first):
    length, width = queries.shape
    lanes = tables[0].shape[1]
    return pl.pallas_call(
        backward_kernel,
        out_shape=jax.ShapeDtypeStruct((length, 3 * width), jnp.bfloat16),
        scratch_shapes=[
            pltpu.VMEM((lanes, length), jnp.bfloat16),
            pltpu.VMEM((length, lanes), jnp.float32),
            pltpu.VMEM((length, lanes), jnp.float32),
            pltpu.VMEM((length, lanes), jnp.float32),
        ],
        compiler_params=pltpu.CompilerParams(vmem_limit_bytes=VMEM_BYTES),
        cost_estimate=pl.CostEstimate(
            flops=10 * length * length * width,
            bytes_accessed=18 * length * width,
            transcendentals=length * length * width // HEAD,
        ),
        name="attention_backward",
    )(queries, key_heads, projected, grad_context, logsum, *tables, first)


def gate_backward(gate_values, up_values, grad_hidden):
    sigmoid_gate = jax.nn.sigmoid(gate_values)
    silu_gate = gate_values * sigmoid_gate
    grad_gate = (
        grad_hidden * up_values * sigmoid_gate * (1.0 + gate_values * (1.0 - sigmoid_gate))
    ).astype(jnp.bfloat16)
    grad_up = (grad_hidden * silu_gate).astype(jnp.bfloat16)
    return (grad_gate, grad_up)


def permute(value, axis, offset):
    size = lax.axis_size(axis)
    return lax.ppermute(value, axis, [(i, i ^ offset) for i in range(size)])


def gather_dp(piece):
    return [piece] + [permute(piece, "dp", k) for k in range(1, lax.axis_size("dp"))]


def scatter_dp(pieces):
    total = pieces[0].astype(jnp.float32)
    for k in range(1, len(pieces)):
        total = total + permute(pieces[k].astype(jnp.bfloat16), "dp", k).astype(jnp.float32)
    return total


def gather_seq(piece):
    return lax.all_gather(piece, "seq", axis=0, tiled=True)


def scatter_seq(terms):
    return lax.psum_scatter(
        terms.astype(jnp.bfloat16), "seq", scatter_dimension=0, tiled=True
    ).astype(jnp.float32)


def after(value, *others):
    return lax.optimization_barrier((value,) + others)[0]


def place(pieces, index):
    block = pieces[0].shape[0]
    result = jnp.zeros((block * len(pieces),) + pieces[0].shape[1:], pieces[0].dtype)
    for k, piece in enumerate(pieces):
        result = lax.dynamic_update_slice_in_dim(result, piece, (index ^ k) * block, 0)
    return result


def per_device(
    layer_input,
    doc_lengths,
    language,
    lang_table,
    attn_norm_gain,
    attn_norm_bias,
    qkv_weight,
    qkv_bias,
    out_weight,
    mlp_norm_gain,
    mlp_norm_bias,
    gate_weight,
    up_weight,
    down_weight,
    cotangent,
):
    tokens = layer_input.shape[1]
    groups = lax.axis_size("seq")
    rows = lax.axis_size("dp")
    devices = rows * groups
    at_dp = lax.axis_index("dp")
    at_seq = lax.axis_index("seq")
    length = tokens * groups
    heads_here = HEADS // groups
    local_width = heads_here * HEAD
    own = D // devices
    owner = [(i, (i % groups) * rows + i // groups) for i in range(devices)]
    back = [(b, a) for a, b in owner]
    small = jnp.concatenate(
        [
            lang_table,
            attn_norm_gain[None],
            attn_norm_bias[None],
            mlp_norm_gain[None],
            mlp_norm_bias[None],
            qkv_bias,
            jnp.broadcast_to(language.astype(jnp.bfloat16)[:, None], (1, own)),
            jnp.zeros((1, own), jnp.bfloat16),
        ],
        axis=0,
    )
    spread = lax.all_to_all(
        jnp.broadcast_to(small[None], (devices,) + small.shape),
        ("dp", "seq"),
        split_axis=0,
        concat_axis=0,
        tiled=True,
    )
    table = jnp.swapaxes(spread, 0, 1).reshape(small.shape[0], D).astype(jnp.float32)
    languages = spread[:, LANGS + 7, 0].astype(jnp.int32)
    gain_attn = table[LANGS]
    bias_attn = table[LANGS + 1]
    gain_mlp = table[LANGS + 2]
    bias_mlp = table[LANGS + 3]
    bias_qkv = lax.dynamic_slice_in_dim(
        table[LANGS + 4 : LANGS + 7], at_seq * local_width, local_width, 1
    ).reshape(3 * local_width)
    chooser = (jnp.arange(LANGS, dtype=jnp.int32) == language[0]).astype(jnp.float32)
    lang_row = jnp.sum(chooser[:, None] * table[:LANGS], axis=0)[None, :]
    qkv_part = lax.all_to_all(
        qkv_weight.reshape(own, 3, groups, local_width).transpose(2, 0, 1, 3).reshape(
            groups, own, 3 * local_width
        ),
        "seq",
        split_axis=0,
        concat_axis=0,
        tiled=True,
    ).reshape(groups * own, 3 * local_width)
    head_qkv = place(gather_dp(qkv_part), at_dp)
    head_out = place(gather_dp(lax.ppermute(out_weight, ("dp", "seq"), back)), at_dp)
    cols_gate = jnp.concatenate(gather_dp(gate_weight.T), axis=0)
    cols_up = jnp.concatenate(gather_dp(up_weight.T), axis=0)
    cols_down = jnp.concatenate(gather_dp(down_weight), axis=0)
    offsets, cosines, sines = row_tables(doc_lengths[0], length)
    tables = rotation_tables(cosines, sines, min(128, local_width))
    first = offsets[None, :]
    grad_out = cotangent[0]
    input_all = gather_seq(layer_input[0])
    grad_all = gather_seq(after(grad_out, input_all))
    normed_all = norm_forward(input_all.astype(jnp.float32) + lang_row, gain_attn, bias_attn)[
        0
    ].astype(jnp.bfloat16)
    resid_in = layer_input[0].astype(jnp.float32) + lang_row
    unused, scaled_attn, inverse_attn = norm_forward(resid_in, gain_attn, bias_attn)
    projected = (
        jnp.dot(normed_all, head_qkv, preferred_element_type=jnp.float32) + bias_qkv
    ).astype(jnp.bfloat16)
    rot_query, rot_key, context_all, logsum = attention_forward(projected, tables, first)
    resid_mid = resid_in + scatter_seq(
        jnp.dot(context_all, head_out, preferred_element_type=jnp.float32)
    )
    normed_mlp, scaled_mlp, inverse_mlp = norm_forward(resid_mid, gain_mlp, bias_mlp)
    rows_all = gather_seq(normed_mlp.astype(jnp.bfloat16))
    gate_values = contract(rows_all, cols_gate, 1, 1)
    up_values = contract(rows_all, cols_up, 1, 1)
    hidden = (jax.nn.silu(gate_values) * up_values).astype(jnp.bfloat16)
    grad_hidden = contract(grad_all, cols_down, 1, 1)
    grad_gate, grad_up = gate_backward(gate_values, up_values, grad_hidden)
    grad_rows = contract(grad_gate, cols_gate, 1, 0) + contract(grad_up, cols_up, 1, 0)
    grad_normed_mlp = scatter_seq(grad_rows)
    def to_owner(terms):
        return scatter_dp(jnp.split(terms.astype(jnp.bfloat16), rows, axis=0))

    out_gate = to_owner(contract(grad_gate, rows_all, 0, 0)).T
    out_up = to_owner(contract(grad_up, rows_all, 0, 0)).T
    out_down = to_owner(contract(hidden, grad_all, 0, 0))
    grad_mid_norm, grad_gain_mlp, grad_bias_mlp = norm_backward(
        grad_normed_mlp, scaled_mlp, inverse_mlp, gain_mlp
    )
    grad_mid = grad_out.astype(jnp.float32) + grad_mid_norm
    branch_all = gather_seq(grad_mid.astype(jnp.bfloat16))
    mlp_terms = jnp.dot(hidden, cols_down, preferred_element_type=jnp.float32)
    mlp_out = scatter_seq(after(mlp_terms.astype(jnp.bfloat16), branch_all))
    layer_output = (resid_mid + mlp_out).astype(jnp.bfloat16)
    grad_heads = contract(branch_all, head_out, 1, 1).astype(jnp.bfloat16)
    grad_stack = attention_backward(
        rot_query, rot_key, projected, grad_heads, logsum, tables, first
    )
    grad_normed_attn = scatter_seq(contract(grad_stack, head_qkv, 1, 1))
    grad_in_norm, grad_gain_attn, grad_bias_attn = norm_backward(
        grad_normed_attn, scaled_attn, inverse_attn, gain_attn
    )
    grad_input = grad_mid + grad_in_norm

    def dp_terms(terms):
        block = terms.shape[0] // rows
        return [
            lax.dynamic_slice_in_dim(terms, (at_dp ^ k) * block, block, 0) for k in range(rows)
        ]

    slice_summed = scatter_dp(dp_terms(contract(normed_all, grad_stack, 0, 0).astype(jnp.bfloat16)))
    grad_qkv_out = (
        lax.all_to_all(
            slice_summed.astype(jnp.bfloat16).reshape(groups, own, 3 * local_width),
            "seq",
            split_axis=0,
            concat_axis=0,
            tiled=True,
        )
        .reshape(groups, own, 3, local_width)
        .transpose(1, 2, 0, 3)
        .reshape(own, 3 * D)
        .astype(jnp.float32)
    )
    head_out_terms = scatter_dp(
        dp_terms(contract(context_all, branch_all, 0, 0).astype(jnp.bfloat16))
    )
    out_proj = lax.ppermute(head_out_terms, ("dp", "seq"), owner)
    grad_bias_qkv = jnp.sum(grad_stack.astype(jnp.float32), axis=0).reshape(3, local_width)
    terms = jnp.concatenate(
        [
            grad_gain_attn[None],
            grad_bias_attn[None],
            grad_gain_mlp[None],
            grad_bias_mlp[None],
            jnp.sum(grad_input, axis=0)[None],
            lax.dynamic_update_slice(
                jnp.zeros((3, D), jnp.float32), grad_bias_qkv, (0, at_seq * local_width)
            ),
        ],
        axis=0,
    )
    arrived = lax.all_to_all(
        terms.reshape(terms.shape[0], devices, own).swapaxes(0, 1),
        ("dp", "seq"),
        split_axis=0,
        concat_axis=0,
        tiled=True,
    )
    summed = jnp.sum(arrived, axis=0)
    members = (languages[:, None] == jnp.arange(LANGS, dtype=jnp.int32)[None, :]).astype(
        jnp.float32
    )
    lang_g = jnp.sum(members[:, :, None] * arrived[:, 4][:, None, :], axis=0)
    return (
        layer_output[None],
        grad_input[None],
        lang_g,
        summed[0],
        summed[1],
        grad_qkv_out,
        summed[5:8],
        out_proj,
        summed[2],
        summed[3],
        out_gate,
        out_up,
        out_down,
    )


def solution(mesh):
    placed = (
        P("dp", "seq", None),
        P("dp", None),
        P("dp"),
        P(None, ("dp", "seq")),
        P(("dp", "seq")),
        P(("dp", "seq")),
        P(("dp", "seq"), None),
        P(None, ("dp", "seq")),
        P(("dp", "seq"), None),
        P(("dp", "seq")),
        P(("dp", "seq")),
        P(None, ("dp", "seq")),
        P(None, ("dp", "seq")),
        P(("dp", "seq"), None),
        P("dp", "seq", None),
    )
    return jax.shard_map(
        per_device,
        mesh=mesh,
        in_specs=placed,
        out_specs=(
            P("dp", "seq", None),
            P("dp", "seq", None),
            P(None, ("dp", "seq")),
            P(("dp", "seq")),
            P(("dp", "seq")),
            P(("dp", "seq"), None),
            P(None, ("dp", "seq")),
            P(("dp", "seq"), None),
            P(("dp", "seq")),
            P(("dp", "seq")),
            P(None, ("dp", "seq")),
            P(None, ("dp", "seq")),
            P(("dp", "seq"), None),
        ),
        check_vma=False,
    )
```

```python
import jax
import jax.numpy as jnp
from jax import lax
from jax.experimental import pallas as pl
from jax.experimental.pallas import tpu as pltpu
from jax.sharding import PartitionSpec as P

D = 2048
HEADS = 32
HEAD = 64
ROT = 16
LANGS = 7


EPS = 1e-05
BASE = 10000.0
NEG = -1e30


def contract(left, right, left_dim, right_dim):
    return lax.dot_general(
        left, right, (((left_dim,), (right_dim,)), ((), ())), preferred_element_type=jnp.float32
    )


def norm_forward(values, gain, bias):
    average = jnp.mean(values, axis=-1, keepdims=True)
    centered = values - average
    variance = jnp.mean(centered * centered, axis=-1, keepdims=True)
    inverse = lax.rsqrt(variance + EPS)
    scaled = centered * inverse
    return (scaled * gain + bias, scaled, inverse)


def norm_backward(grad_normed, scaled, inverse, gain):
    grad_scaled = grad_normed * gain
    grad_values = inverse * (
        grad_scaled
        - jnp.mean(grad_scaled, axis=-1, keepdims=True)
        - scaled * jnp.mean(grad_scaled * scaled, axis=-1, keepdims=True)
    )
    return (grad_values, jnp.sum(grad_normed * scaled, axis=0), jnp.sum(grad_normed, axis=0))


def row_tables(doc_lengths, length):
    ends = jnp.cumsum(doc_lengths)
    starts = ends - doc_lengths
    places = jnp.arange(length, dtype=jnp.int32)
    segment = jnp.sum((places[:, None] >= ends[None, :]).astype(jnp.int32), axis=1)
    member = segment[:, None] == jnp.arange(ends.shape[0], dtype=jnp.int32)[None, :]
    offsets = jnp.sum(jnp.where(member, starts[None, :], 0), axis=1)
    position = (places - offsets).astype(jnp.float32)
    half_rot = ROT // 2
    freq = BASE ** (-(2.0 * jnp.arange(half_rot, dtype=jnp.float32)) / ROT)
    angles = position[:, None] * freq[None, :]
    return (offsets, jnp.cos(angles), jnp.sin(angles))


def head_lanes(shape, dim, head):
    place = lax.broadcasted_iota(jnp.int32, shape, dim)
    return (place >= head * HEAD) & (place < (head + 1) * HEAD)


def turn(values, tables, direction):
    lanes = values.shape[1]
    cosines, sines_former, sines_latter = tables
    after = pltpu.roll(values, lanes - ROT // 2, 1)
    before = pltpu.roll(values, ROT // 2, 1)
    return values * cosines + direction * (before * sines_latter - after * sines_former)


def allowed_pairs(first_ref, start, block, keys):
    key_at = lax.broadcasted_iota(jnp.int32, (keys, block), 0)
    query_at = start + lax.broadcasted_iota(jnp.int32, (keys, block), 1)
    return (key_at >= first_ref[:, pl.ds(start, block)]) & (key_at <= query_at)


def over_blocks(length, block, step):
    count = length // block
    if count <= 4:
        for i in range(count):
            step(i * block, (i + 1) * block)
    else:

        def body(i, carry):
            step(pl.multiple_of(i * block, block), length)
            return carry

        lax.fori_loop(0, count, body, 0)


def forward_kernel(
    qkv_ref, cos_ref, former_ref, latter_ref, first_ref,
    query_ref, key_ref, context_ref, logsum_ref, value_t,
):
    length, width = query_ref.shape
    lanes = cos_ref.shape[1]
    block = min(256, length)
    tables = (cos_ref[...], former_ref[...], latter_ref[...])
    for group in range(width // lanes):
        part = slice(group * lanes, (group + 1) * lanes)

        def columns(c):
            begin = c * width + group * lanes
            return qkv_ref[:, begin : begin + lanes].astype(jnp.float32)

        query_ref[:, part] = turn(columns(0), tables, 1.0).astype(jnp.bfloat16)
        key_ref[:, part] = turn(columns(1), tables, 1.0).astype(jnp.bfloat16)
        value_t[...] = columns(2).T.astype(jnp.bfloat16)

        def step(start, keys):
            queries = query_ref[pl.ds(start, block), part].astype(jnp.float32) * HEAD ** (-0.5)
            allowed = allowed_pairs(first_ref, start, block, keys)
            found = []
            for head in range(lanes // HEAD):
                own = jnp.where(head_lanes(queries.shape, 1, head), queries, 0.0)
                scores = contract(key_ref[0:keys, part], own.astype(jnp.bfloat16), 1, 1)
                scores = jnp.where(allowed, scores, NEG)
                most = jnp.max(scores, axis=0, keepdims=True)
                weights = jnp.exp(scores - most)
                total = jnp.sum(weights, axis=0, keepdims=True)
                probs = (weights * (1.0 / total)).astype(jnp.bfloat16)
                logsum_ref[
                    pl.ds(group * (lanes // HEAD) + head, 1), pl.ds(start, block)
                ] = most + jnp.log(total)
                context = contract(value_t[:, 0:keys], probs, 1, 0)
                found.append(context[head * HEAD : (head + 1) * HEAD])
            context_ref[pl.ds(start, block), part] = (
                jnp.concatenate(found, axis=0).T.astype(jnp.bfloat16)
            )

        over_blocks(length, block, step)


def backward_kernel(
    query_ref, key_ref, qkv_ref, context_grad_ref, logsum_ref, cos_ref, former_ref, latter_ref,
    first_ref, grad_ref, key_t, grad_query, grad_key, grad_value,
):
    length, width = query_ref.shape
    lanes = cos_ref.shape[1]
    block = min(256, length)
    scale = HEAD ** (-0.5)
    tables = (cos_ref[...], former_ref[...], latter_ref[...])
    for group in range(width // lanes):
        part = slice(group * lanes, (group + 1) * lanes)
        value_part = slice(2 * width + group * lanes, 2 * width + (group + 1) * lanes)
        key_t[...] = key_ref[:, part].astype(jnp.float32).T.astype(jnp.bfloat16)
        grad_key[...] = jnp.zeros_like(grad_key)
        grad_value[...] = jnp.zeros_like(grad_value)

        def step(start, keys):
            queries = query_ref[pl.ds(start, block), part].astype(jnp.float32) * scale
            grads = context_grad_ref[pl.ds(start, block), part].astype(jnp.float32)
            allowed = allowed_pairs(first_ref, start, block, keys)
            found = []
            for head in range(lanes // HEAD):
                mine = head_lanes(queries.shape, 1, head)
                own_query = jnp.where(mine, queries, 0.0).astype(jnp.bfloat16)
                own_grad = jnp.where(mine, grads, 0.0).astype(jnp.bfloat16)
                scores = contract(key_ref[0:keys, part], own_query, 1, 1)
                logsum = logsum_ref[
                    pl.ds(group * (lanes // HEAD) + head, 1), pl.ds(start, block)
                ]
                soft = jnp.exp(jnp.where(allowed, scores, NEG) - logsum)
                grad_soft = contract(qkv_ref[0:keys, value_part], own_grad, 1, 1)
                weighed = soft * grad_soft
                delta = jnp.sum(weighed, axis=0, keepdims=True)
                grad_scores = (weighed - soft * delta).astype(jnp.bfloat16)
                grad_value[0:keys] += contract(soft.astype(jnp.bfloat16), own_grad, 1, 0)
                grad_key[0:keys] += contract(grad_scores, own_query, 1, 0)
                turned = contract(key_t[:, 0:keys], grad_scores, 1, 0)
                found.append(turned[head * HEAD : (head + 1) * HEAD])
            grad_query[pl.ds(start, block), :] = jnp.concatenate(found, axis=0).T * scale

        over_blocks(length, block, step)
        for c, grads in ((0, grad_query), (1, grad_key)):
            begin = c * width + group * lanes
            grad_ref[:, begin : begin + lanes] = turn(grads[...], tables, -1.0).astype(
                jnp.bfloat16
            )
        grad_ref[:, value_part] = grad_value[...].astype(jnp.bfloat16)


def rotation_tables(cosines, sines, lanes):
    length = cosines.shape[0]
    rest = jnp.ones((length, HEAD - ROT), jnp.float32)
    none = jnp.zeros_like(sines)
    heads = lanes // HEAD
    return (
        jnp.tile(jnp.concatenate([cosines, cosines, rest], axis=1), (1, heads)),
        jnp.tile(jnp.concatenate([sines, none, 0.0 * rest], axis=1), (1, heads)),
        jnp.tile(jnp.concatenate([none, sines, 0.0 * rest], axis=1), (1, heads)),
    )


VMEM_BYTES = 48 * 1024 * 1024


def attention_forward(projected, tables, first):
    length, width = projected.shape[0], projected.shape[1] // 3
    lanes = tables[0].shape[1]
    rows = jax.ShapeDtypeStruct((length, width), jnp.bfloat16)
    return pl.pallas_call(
        forward_kernel,
        out_shape=(
            rows,
            rows,
            rows,
            jax.ShapeDtypeStruct((width // HEAD, length), jnp.float32),
        ),
        scratch_shapes=[pltpu.VMEM((lanes, length), jnp.bfloat16)],
        compiler_params=pltpu.CompilerParams(vmem_limit_bytes=VMEM_BYTES),
        cost_estimate=pl.CostEstimate(
            flops=4 * length * length * width,
            bytes_accessed=12 * length * width,
            transcendentals=length * length * width // HEAD,
        ),
        name="attention_forward",
    )(projected, *tables, first)


def attention_backward(queries, key_heads, projected, grad_context, logsum, tables, first):
    length, width = queries.shape
    lanes = tables[0].shape[1]
    return pl.pallas_call(
        backward_kernel,
        out_shape=jax.ShapeDtypeStruct((length, 3 * width), jnp.bfloat16),
        scratch_shapes=[
            pltpu.VMEM((lanes, length), jnp.bfloat16),
            pltpu.VMEM((length, lanes), jnp.float32),
            pltpu.VMEM((length, lanes), jnp.float32),
            pltpu.VMEM((length, lanes), jnp.float32),
        ],
        compiler_params=pltpu.CompilerParams(vmem_limit_bytes=VMEM_BYTES),
        cost_estimate=pl.CostEstimate(
            flops=10 * length * length * width,
            bytes_accessed=18 * length * width,
            transcendentals=length * length * width // HEAD,
        ),
        name="attention_backward",
    )(queries, key_heads, projected, grad_context, logsum, *tables, first)


def gate_backward(gate_values, up_values, grad_hidden):
    sigmoid_gate = jax.nn.sigmoid(gate_values)
    silu_gate = gate_values * sigmoid_gate
    grad_gate = (
        grad_hidden * up_values * sigmoid_gate * (1.0 + gate_values * (1.0 - sigmoid_gate))
    ).astype(jnp.bfloat16)
    grad_up = (grad_hidden * silu_gate).astype(jnp.bfloat16)
    return (grad_gate, grad_up)


def permute(value, axis, offset):
    size = lax.axis_size(axis)
    return lax.ppermute(value, axis, [(i, i ^ offset) for i in range(size)])


def gather_dp(piece):
    return [piece] + [permute(piece, "dp", k) for k in range(1, lax.axis_size("dp"))]


def scatter_dp(pieces):
    total = pieces[0].astype(jnp.float32)
    for k in range(1, len(pieces)):
        total = total + permute(pieces[k].astype(jnp.bfloat16), "dp", k).astype(jnp.float32)
    return total


def total(parts):
    result = parts[0].astype(jnp.float32)
    for piece in parts[1:]:
        result = result + piece.astype(jnp.float32)
    return result


def gather_seq(piece):
    return lax.all_gather(piece, "seq", axis=0, tiled=True)


def scatter_seq(terms):
    return lax.psum_scatter(
        terms.astype(jnp.bfloat16), "seq", scatter_dimension=0, tiled=True
    ).astype(jnp.float32)


def after(value, *others):
    return lax.optimization_barrier((value,) + others)[0]


def place(pieces, index):
    block = pieces[0].shape[0]
    result = jnp.zeros((block * len(pieces),) + pieces[0].shape[1:], pieces[0].dtype)
    for k, piece in enumerate(pieces):
        result = lax.dynamic_update_slice_in_dim(result, piece, (index ^ k) * block, 0)
    return result


def per_device(
    layer_input,
    doc_lengths,
    language,
    lang_table,
    attn_norm_gain,
    attn_norm_bias,
    qkv_weight,
    qkv_bias,
    out_weight,
    mlp_norm_gain,
    mlp_norm_bias,
    gate_weight,
    up_weight,
    down_weight,
    cotangent,
):
    tokens = layer_input.shape[1]
    groups = lax.axis_size("seq")
    rows = lax.axis_size("dp")
    devices = rows * groups
    at_dp = lax.axis_index("dp")
    at_seq = lax.axis_index("seq")
    length = tokens * groups
    heads_here = HEADS // groups
    local_width = heads_here * HEAD
    own = D // devices
    whole_heads = own % HEAD == 0
    deal = (rows, groups, own) if whole_heads else (1, groups, local_width)
    at_deal = (0, 0, at_seq, 0)
    owner = [(i, (i % groups) * rows + i // groups) for i in range(devices)]
    back = [(b, a) for a, b in owner]

    def to_heads(values):
        count = values.shape[0]
        return lax.dynamic_slice(
            values.reshape((count,) + deal), at_deal, (count, deal[0], 1, deal[2])
        ).reshape(count, local_width)

    def from_heads(values):
        count = values.shape[0]
        return lax.dynamic_update_slice(
            jnp.zeros((count,) + deal, values.dtype),
            values.reshape(count, deal[0], 1, deal[2]),
            at_deal,
        ).reshape(count, D)

    phase = lax.optimization_barrier
    grad_out = cotangent[0]
    half = D // 2

    def to_owner(terms):
        return scatter_dp(jnp.split(terms, rows, axis=0))

    def dp_terms(terms):
        block = terms.shape[0] // rows
        return [
            lax.dynamic_slice_in_dim(terms, (at_dp ^ k) * block, block, 0) for k in range(rows)
        ]

    small = jnp.concatenate(
        [
            lang_table,
            attn_norm_gain[None],
            attn_norm_bias[None],
            mlp_norm_gain[None],
            mlp_norm_bias[None],
            qkv_bias,
            jnp.broadcast_to(language.astype(jnp.bfloat16)[:, None], (1, own)),
        ],
        axis=0,
    )
    ride = 8
    riders = jnp.zeros((ride * 3 * local_width,), jnp.bfloat16)
    riders = lax.dynamic_update_slice(riders, small.reshape(-1), (0,))
    part = lax.all_to_all(
        jnp.concatenate(
            [
                qkv_weight.reshape((own, 3) + deal)
                .transpose(3, 0, 1, 2, 4)
                .reshape(groups, own, 3 * local_width),
                jnp.broadcast_to(
                    riders.reshape(1, ride, 3 * local_width), (groups, ride, 3 * local_width)
                ),
            ],
            axis=1,
        ),
        "seq",
        split_axis=0,
        concat_axis=0,
        tiled=True,
    )
    part, own_input = phase((part, layer_input[0]))
    input_all = gather_seq(own_input)
    spread = place(gather_dp(part[:, own:].reshape(groups, -1)), at_dp)
    head_qkv = place(gather_dp(part[:, :own].reshape(groups * own, 3 * local_width)), at_dp)
    spread = spread[:, : small.size].reshape((devices,) + small.shape)
    table = jnp.swapaxes(spread, 0, 1).reshape(small.shape[0], D).astype(jnp.float32)
    languages = spread[:, LANGS + 7, 0].astype(jnp.int32)
    gain_attn = table[LANGS]
    bias_attn = table[LANGS + 1]
    gain_mlp = table[LANGS + 2]
    bias_mlp = table[LANGS + 3]
    bias_qkv = to_heads(table[LANGS + 4 : LANGS + 7]).reshape(3 * local_width)
    chooser = (jnp.arange(LANGS, dtype=jnp.int32) == language[0]).astype(jnp.float32)
    lang_row = jnp.sum(chooser[:, None] * table[:LANGS], axis=0)[None, :]
    offsets, cosines, sines = row_tables(doc_lengths[0], length)
    tables = rotation_tables(cosines, sines, min(128, local_width))
    first = offsets[None, :]
    resid_in = layer_input[0].astype(jnp.float32) + lang_row
    unused, scaled_attn, inverse_attn = norm_forward(resid_in, gain_attn, bias_attn)
    input_all, head_qkv, out_rows, tables, first, resid_in, grad_first, gate_rows = phase(
        (
            input_all,
            head_qkv,
            out_weight,
            tables,
            first,
            resid_in,
            grad_out[:, :half],
            gate_weight.T,
        )
    )
    if not whole_heads:
        out_rows = lax.ppermute(out_rows, ("dp", "seq"), back)
    head_out = place(gather_dp(out_rows), at_dp)
    gate_pieces = [gate_rows, permute(gate_rows, "dp", 1), permute(gate_rows, "dp", 2)]
    grad_all_first = gather_seq(grad_first)
    normed_all, scaled_all, inverse_all = norm_forward(
        input_all.astype(jnp.float32) + lang_row, gain_attn, bias_attn
    )
    normed_all = normed_all.astype(jnp.bfloat16)
    projected = (
        jnp.dot(normed_all, head_qkv, preferred_element_type=jnp.float32) + bias_qkv
    ).astype(jnp.bfloat16)
    rot_query, rot_key, context_all, logsum = attention_forward(projected, tables, first)
    out_terms = jnp.dot(context_all, head_out, preferred_element_type=jnp.float32).astype(
        jnp.bfloat16
    )
    out_terms, grad_all_first, gate_pieces = phase((out_terms, grad_all_first, gate_pieces))
    attn_out = scatter_seq(out_terms)
    cols_gate = jnp.concatenate(gate_pieces + [permute(gate_pieces[0], "dp", 3)], axis=0)
    cols_up = jnp.concatenate(gather_dp(after(up_weight.T, cols_gate)), axis=0)
    attn_out, cols_gate, cols_up, down_rows = phase((attn_out, cols_gate, cols_up, down_weight))
    cols_down = jnp.concatenate(gather_dp(down_rows), axis=0)
    resid_mid = resid_in + attn_out
    normed_mlp, scaled_mlp, inverse_mlp = norm_forward(resid_mid, gain_mlp, bias_mlp)
    rows_all = gather_seq(normed_mlp.astype(jnp.bfloat16))
    grad_hidden = contract(grad_all_first, cols_down[:, :half], 1, 1)
    rows_all, cols_down, grad_hidden, grad_second = phase(
        (rows_all, cols_down, grad_hidden, grad_out[:, half:])
    )
    grad_all_second = gather_seq(grad_second)
    gate_values = contract(rows_all, cols_gate, 1, 1)
    up_values = contract(rows_all, cols_up, 1, 1)
    hidden = (jax.nn.silu(gate_values) * up_values).astype(jnp.bfloat16)
    grad_hidden = grad_hidden + contract(grad_all_second, cols_down[:, half:], 1, 1)
    grad_gate, grad_up = gate_backward(gate_values, up_values, grad_hidden)
    grad_rows = (
        contract(grad_gate, cols_gate, 1, 0) + contract(grad_up, cols_up, 1, 0)
    ).astype(jnp.bfloat16)
    grad_rows, grad_gate, grad_up, hidden = phase((grad_rows, grad_gate, grad_up, hidden))
    grad_normed_mlp = scatter_seq(grad_rows)
    out_gate = to_owner(contract(grad_gate, rows_all, 0, 0).astype(jnp.bfloat16))
    up_terms = contract(grad_up, rows_all, 0, 0).astype(jnp.bfloat16)
    mlp_first = contract(hidden, cols_down[:, :half], 1, 0).astype(jnp.bfloat16)
    mlp_second = contract(hidden, cols_down[:, half:], 1, 0).astype(jnp.bfloat16)
    down_terms = jnp.concatenate(
        [contract(hidden, grad_all_first, 0, 0), contract(hidden, grad_all_second, 0, 0)], axis=1
    ).astype(jnp.bfloat16)
    grad_normed_mlp, out_gate, up_terms, mlp_first, mlp_second, down_terms = phase(
        (grad_normed_mlp, out_gate, up_terms, mlp_first, mlp_second, down_terms)
    )
    grad_mid_norm, grad_gain_mlp, grad_bias_mlp = norm_backward(
        grad_normed_mlp, scaled_mlp, inverse_mlp, gain_mlp
    )
    grad_mid = grad_out.astype(jnp.float32) + grad_mid_norm
    branch_all = gather_seq(grad_mid.astype(jnp.bfloat16))
    out_up = to_owner(up_terms)
    branch_all, out_up, mlp_first, down_terms = phase((branch_all, out_up, mlp_first, down_terms))
    mlp_out_first = scatter_seq(mlp_first)
    down_pieces = jnp.split(down_terms, rows, axis=0)
    down_arrived = [permute(down_pieces[k], "dp", k) for k in range(1, rows - 1)]
    grad_heads = contract(branch_all, head_out, 1, 1).astype(jnp.bfloat16)
    grad_stack = attention_backward(
        rot_query, rot_key, projected, grad_heads, logsum, tables, first
    )
    slice_terms = contract(normed_all, grad_stack, 0, 0).astype(jnp.bfloat16)
    attn_terms = contract(grad_stack, head_qkv, 1, 1).astype(jnp.bfloat16)
    (
        attn_terms,
        slice_terms,
        mlp_out_first,
        grad_stack,
        branch_all,
        down_arrived,
        down_pieces,
        input_all,
    ) = phase(
        (
            attn_terms,
            slice_terms,
            mlp_out_first,
            grad_stack,
            branch_all,
            down_arrived,
            down_pieces,
            input_all,
        )
    )
    grad_normed_attn = scatter_seq(attn_terms)
    slice_pieces = dp_terms(slice_terms)
    slice_arrived = [permute(slice_pieces[k], "dp", k) for k in range(1, rows - 1)]
    unused, scaled_all, inverse_all = norm_forward(
        input_all.astype(jnp.float32) + lang_row, gain_attn, bias_attn
    )
    grad_in_terms, grad_gain_attn, grad_bias_attn = norm_backward(
        attn_terms.astype(jnp.float32), scaled_all, inverse_all, gain_attn
    )
    grad_input_sum = jnp.sum(grad_mid, axis=0) + jnp.sum(grad_in_terms, axis=0)
    grad_bias_qkv = jnp.sum(grad_stack.astype(jnp.float32), axis=0).reshape(3, local_width)
    terms = jnp.concatenate(
        [
            grad_gain_attn[None],
            grad_bias_attn[None],
            grad_gain_mlp[None],
            grad_bias_mlp[None],
            grad_input_sum[None],
            from_heads(grad_bias_qkv),
        ],
        axis=0,
    )
    head_out_terms = dp_terms(contract(context_all, branch_all, 0, 0).astype(jnp.bfloat16))
    terms, head_out_terms, slice_arrived, slice_pieces = phase(
        (terms, head_out_terms, slice_arrived, slice_pieces)
    )
    slice_arrived = slice_arrived + [permute(slice_pieces[-1], "dp", rows - 1)]
    out_arrived = [permute(head_out_terms[k], "dp", k) for k in range(1, rows)]

    slice_summed = total([slice_pieces[0]] + slice_arrived).astype(jnp.bfloat16)
    arrived = lax.all_to_all(
        terms.reshape(terms.shape[0], devices, own).swapaxes(0, 1),
        ("dp", "seq"),
        split_axis=0,
        concat_axis=0,
        tiled=True,
    )
    out_arrived, mlp_second, arrived, slice_summed, grad_normed_attn, down_arrived, down_pieces = (
        phase(
            (
                out_arrived,
                mlp_second,
                arrived,
                slice_summed,
                grad_normed_attn,
                down_arrived,
                down_pieces,
            )
        )
    )
    grad_qkv_out = (
        lax.all_to_all(
            slice_summed.reshape(groups, own, 3 * local_width),
            "seq",
            split_axis=0,
            concat_axis=0,
            tiled=True,
        )
        .reshape(groups, own, 3, deal[0], deal[2])
        .transpose(1, 2, 3, 0, 4)
        .reshape(own, 3 * D)
        .astype(jnp.float32)
    )
    mlp_out = jnp.concatenate([mlp_out_first, scatter_seq(mlp_second)], axis=1)
    out_proj = total([head_out_terms[0]] + out_arrived)
    if not whole_heads:
        out_proj = lax.ppermute(out_proj, ("dp", "seq"), owner)
    out_down = total(
        [down_pieces[0]] + down_arrived + [permute(down_pieces[-1], "dp", rows - 1)]
    )
    layer_output = (resid_mid + mlp_out).astype(jnp.bfloat16)
    grad_input = grad_mid + norm_backward(
        grad_normed_attn, scaled_attn, inverse_attn, gain_attn
    )[0]
    summed = jnp.sum(arrived, axis=0)
    members = (languages[:, None] == jnp.arange(LANGS, dtype=jnp.int32)[None, :]).astype(
        jnp.float32
    )
    lang_g = jnp.sum(members[:, :, None] * arrived[:, 4][:, None, :], axis=0)
    return (
        layer_output[None],
        grad_input[None],
        lang_g,
        summed[0],
        summed[1],
        grad_qkv_out,
        summed[5:8],
        out_proj,
        summed[2],
        summed[3],
        out_gate.T,
        out_up.T,
        out_down,
    )


def solution(mesh):
    placed = (
        P("dp", "seq", None),
        P("dp", None),
        P("dp"),
        P(None, ("dp", "seq")),
        P(("dp", "seq")),
        P(("dp", "seq")),
        P(("dp", "seq"), None),
        P(None, ("dp", "seq")),
        P(("dp", "seq"), None),
        P(("dp", "seq")),
        P(("dp", "seq")),
        P(None, ("dp", "seq")),
        P(None, ("dp", "seq")),
        P(("dp", "seq"), None),
        P("dp", "seq", None),
    )
    return jax.shard_map(
        per_device,
        mesh=mesh,
        in_specs=placed,
        out_specs=(
            P("dp", "seq", None),
            P("dp", "seq", None),
            P(None, ("dp", "seq")),
            P(("dp", "seq")),
            P(("dp", "seq")),
            P(("dp", "seq"), None),
            P(None, ("dp", "seq")),
            P(("dp", "seq"), None),
            P(("dp", "seq")),
            P(("dp", "seq")),
            P(None, ("dp", "seq")),
            P(None, ("dp", "seq")),
            P(("dp", "seq"), None),
        ),
        check_vma=False,
    )
```

```python
import jax
import jax.numpy as jnp
from jax import lax
from jax.experimental import pallas as pl
from jax.experimental.pallas import tpu as pltpu
from jax.sharding import PartitionSpec as P

D = 2048
HEADS = 32
HEAD = 64
ROT = 16
LANGS = 7


EPS = 1e-05
BASE = 10000.0
NEG = -1e30


def contract(left, right, left_dim, right_dim):
    return lax.dot_general(
        left, right, (((left_dim,), (right_dim,)), ((), ())), preferred_element_type=jnp.float32
    )


def norm_forward(values, gain, bias):
    average = jnp.mean(values, axis=-1, keepdims=True)
    centered = values - average
    variance = jnp.mean(centered * centered, axis=-1, keepdims=True)
    inverse = lax.rsqrt(variance + EPS)
    scaled = centered * inverse
    return (scaled * gain + bias, scaled, inverse)


def norm_backward(grad_normed, scaled, inverse, gain):
    grad_scaled = grad_normed * gain
    grad_values = inverse * (
        grad_scaled
        - jnp.mean(grad_scaled, axis=-1, keepdims=True)
        - scaled * jnp.mean(grad_scaled * scaled, axis=-1, keepdims=True)
    )
    return (grad_values, jnp.sum(grad_normed * scaled, axis=0), jnp.sum(grad_normed, axis=0))


def row_tables(doc_lengths, length):
    ends = jnp.cumsum(doc_lengths)
    starts = ends - doc_lengths
    places = jnp.arange(length, dtype=jnp.int32)
    segment = jnp.sum((places[:, None] >= ends[None, :]).astype(jnp.int32), axis=1)
    member = segment[:, None] == jnp.arange(ends.shape[0], dtype=jnp.int32)[None, :]
    offsets = jnp.sum(jnp.where(member, starts[None, :], 0), axis=1)
    position = (places - offsets).astype(jnp.float32)
    half_rot = ROT // 2
    freq = BASE ** (-(2.0 * jnp.arange(half_rot, dtype=jnp.float32)) / ROT)
    angles = position[:, None] * freq[None, :]
    return (offsets, jnp.cos(angles), jnp.sin(angles))


def head_lanes(shape, dim, head):
    place = lax.broadcasted_iota(jnp.int32, shape, dim)
    return (place >= head * HEAD) & (place < (head + 1) * HEAD)


def turn(values, tables, direction):
    lanes = values.shape[1]
    cosines, sines_former, sines_latter = tables
    after = pltpu.roll(values, lanes - ROT // 2, 1)
    before = pltpu.roll(values, ROT // 2, 1)
    return values * cosines + direction * (before * sines_latter - after * sines_former)


def allowed_pairs(first_ref, start, block, keys):
    key_at = lax.broadcasted_iota(jnp.int32, (keys, block), 0)
    query_at = start + lax.broadcasted_iota(jnp.int32, (keys, block), 1)
    return (key_at >= first_ref[:, pl.ds(start, block)]) & (key_at <= query_at)


def over_blocks(length, block, step):
    count = length // block
    if count <= 4:
        for i in range(count):
            step(i * block, (i + 1) * block)
    else:

        def body(i, carry):
            step(pl.multiple_of(i * block, block), length)
            return carry

        lax.fori_loop(0, count, body, 0)


def forward_kernel(
    qkv_ref, cos_ref, former_ref, latter_ref, first_ref,
    query_ref, key_ref, context_ref, logsum_ref, value_t,
):
    length, width = query_ref.shape
    lanes = cos_ref.shape[1]
    block = min(256, length)
    tables = (cos_ref[...], former_ref[...], latter_ref[...])
    for group in range(width // lanes):
        part = slice(group * lanes, (group + 1) * lanes)

        def columns(c):
            begin = c * width + group * lanes
            return qkv_ref[:, begin : begin + lanes].astype(jnp.float32)

        query_ref[:, part] = turn(columns(0), tables, 1.0).astype(jnp.bfloat16)
        key_ref[:, part] = turn(columns(1), tables, 1.0).astype(jnp.bfloat16)
        value_t[...] = columns(2).T.astype(jnp.bfloat16)

        def step(start, keys):
            queries = query_ref[pl.ds(start, block), part].astype(jnp.float32) * HEAD ** (-0.5)
            allowed = allowed_pairs(first_ref, start, block, keys)
            found = []
            for head in range(lanes // HEAD):
                own = jnp.where(head_lanes(queries.shape, 1, head), queries, 0.0)
                scores = contract(key_ref[0:keys, part], own.astype(jnp.bfloat16), 1, 1)
                scores = jnp.where(allowed, scores, NEG)
                most = jnp.max(scores, axis=0, keepdims=True)
                weights = jnp.exp(scores - most)
                total = jnp.sum(weights, axis=0, keepdims=True)
                probs = (weights * (1.0 / total)).astype(jnp.bfloat16)
                logsum_ref[
                    pl.ds(group * (lanes // HEAD) + head, 1), pl.ds(start, block)
                ] = most + jnp.log(total)
                context = contract(value_t[:, 0:keys], probs, 1, 0)
                found.append(context[head * HEAD : (head + 1) * HEAD])
            context_ref[pl.ds(start, block), part] = (
                jnp.concatenate(found, axis=0).T.astype(jnp.bfloat16)
            )

        over_blocks(length, block, step)


def backward_kernel(
    query_ref, key_ref, qkv_ref, context_grad_ref, logsum_ref, cos_ref, former_ref, latter_ref,
    first_ref, grad_ref, key_t, grad_query, grad_key, grad_value,
):
    length, width = query_ref.shape
    lanes = cos_ref.shape[1]
    block = min(256, length)
    scale = HEAD ** (-0.5)
    tables = (cos_ref[...], former_ref[...], latter_ref[...])
    for group in range(width // lanes):
        part = slice(group * lanes, (group + 1) * lanes)
        value_part = slice(2 * width + group * lanes, 2 * width + (group + 1) * lanes)
        key_t[...] = key_ref[:, part].astype(jnp.float32).T.astype(jnp.bfloat16)
        grad_key[...] = jnp.zeros_like(grad_key)
        grad_value[...] = jnp.zeros_like(grad_value)

        def step(start, keys):
            queries = query_ref[pl.ds(start, block), part].astype(jnp.float32) * scale
            grads = context_grad_ref[pl.ds(start, block), part].astype(jnp.float32)
            allowed = allowed_pairs(first_ref, start, block, keys)
            found = []
            for head in range(lanes // HEAD):
                mine = head_lanes(queries.shape, 1, head)
                own_query = jnp.where(mine, queries, 0.0).astype(jnp.bfloat16)
                own_grad = jnp.where(mine, grads, 0.0).astype(jnp.bfloat16)
                scores = contract(key_ref[0:keys, part], own_query, 1, 1)
                logsum = logsum_ref[
                    pl.ds(group * (lanes // HEAD) + head, 1), pl.ds(start, block)
                ]
                soft = jnp.exp(jnp.where(allowed, scores, NEG) - logsum)
                grad_soft = contract(qkv_ref[0:keys, value_part], own_grad, 1, 1)
                weighed = soft * grad_soft
                delta = jnp.sum(weighed, axis=0, keepdims=True)
                grad_scores = (weighed - soft * delta).astype(jnp.bfloat16)
                grad_value[0:keys] += contract(soft.astype(jnp.bfloat16), own_grad, 1, 0)
                grad_key[0:keys] += contract(grad_scores, own_query, 1, 0)
                turned = contract(key_t[:, 0:keys], grad_scores, 1, 0)
                found.append(turned[head * HEAD : (head + 1) * HEAD])
            grad_query[pl.ds(start, block), :] = jnp.concatenate(found, axis=0).T * scale

        over_blocks(length, block, step)
        for c, grads in ((0, grad_query), (1, grad_key)):
            begin = c * width + group * lanes
            grad_ref[:, begin : begin + lanes] = turn(grads[...], tables, -1.0).astype(
                jnp.bfloat16
            )
        grad_ref[:, value_part] = grad_value[...].astype(jnp.bfloat16)


def columns_kernel(part_refs, out_ref, deal, width):
    row = 0
    for ref in part_refs:
        groups, rows = ref.shape[0], ref.shape[1]
        for c in range(3):
            for d in range(0, deal, 2):
                for s in range(0, groups, 2):
                    begin = c * deal * HEAD + d * HEAD
                    left = ref[s, :, begin : begin + 2 * HEAD].astype(jnp.float32)
                    right = ref[s + 1, :, begin : begin + 2 * HEAD].astype(jnp.float32)
                    lower = lax.broadcasted_iota(jnp.int32, left.shape, 1) < HEAD
                    out = c * width + d * groups * HEAD + s * HEAD
                    out_ref[row : row + rows, out : out + 2 * HEAD] = jnp.where(
                        lower, left, pltpu.roll(right, HEAD, 1)
                    )
                    out = out + groups * HEAD
                    out_ref[row : row + rows, out : out + 2 * HEAD] = jnp.where(
                        lower, pltpu.roll(left, HEAD, 1), right
                    )
        row += rows


def columns_in_place(parts, deal):
    rows = sum(part.shape[1] for part in parts)
    width = parts[0].shape[0] * deal * HEAD

    def kernel(*refs):
        columns_kernel(refs[:-1], refs[-1], deal, width)

    return pl.pallas_call(
        kernel,
        out_shape=jax.ShapeDtypeStruct((rows, 3 * width), jnp.float32),
        compiler_params=pltpu.CompilerParams(vmem_limit_bytes=VMEM_BYTES),
        name="columns_in_place",
    )(*parts)


def deal_kernel(weight_ref, riders_ref, out_ref, deal):
    groups = out_ref.shape[0]
    rows, width = weight_ref.shape[0], weight_ref.shape[1] // 3
    for c in range(3):
        for d in range(0, deal, 2):
            for s in range(0, groups, 2):
                begin = c * width + d * groups * HEAD + s * HEAD
                upper = weight_ref[:, begin : begin + 2 * HEAD].astype(jnp.float32)
                begin = begin + groups * HEAD
                after = weight_ref[:, begin : begin + 2 * HEAD].astype(jnp.float32)
                lower = lax.broadcasted_iota(jnp.int32, upper.shape, 1) < HEAD
                out = c * deal * HEAD + d * HEAD
                out_ref[s, 0:rows, out : out + 2 * HEAD] = jnp.where(
                    lower, upper, pltpu.roll(after, HEAD, 1)
                ).astype(jnp.bfloat16)
                out_ref[s + 1, 0:rows, out : out + 2 * HEAD] = jnp.where(
                    lower, pltpu.roll(upper, HEAD, 1), after
                ).astype(jnp.bfloat16)
    for s in range(groups):
        out_ref[s, rows:, :] = riders_ref[...]


def deal_columns(weight, riders, groups, deal):
    def kernel(*refs):
        deal_kernel(*refs, deal)

    return pl.pallas_call(
        kernel,
        out_shape=jax.ShapeDtypeStruct(
            (groups, weight.shape[0] + riders.shape[0], riders.shape[1]), jnp.bfloat16
        ),
        compiler_params=pltpu.CompilerParams(vmem_limit_bytes=VMEM_BYTES),
        name="deal_columns",
    )(weight, riders)


def rotation_tables(cosines, sines, lanes):
    length = cosines.shape[0]
    rest = jnp.ones((length, HEAD - ROT), jnp.float32)
    none = jnp.zeros_like(sines)
    heads = lanes // HEAD
    return (
        jnp.tile(jnp.concatenate([cosines, cosines, rest], axis=1), (1, heads)),
        jnp.tile(jnp.concatenate([sines, none, 0.0 * rest], axis=1), (1, heads)),
        jnp.tile(jnp.concatenate([none, sines, 0.0 * rest], axis=1), (1, heads)),
    )


VMEM_BYTES = 48 * 1024 * 1024


def attention_forward(projected, tables, first):
    length, width = projected.shape[0], projected.shape[1] // 3
    lanes = tables[0].shape[1]
    rows = jax.ShapeDtypeStruct((length, width), jnp.bfloat16)
    return pl.pallas_call(
        forward_kernel,
        out_shape=(
            rows,
            rows,
            rows,
            jax.ShapeDtypeStruct((width // HEAD, length), jnp.float32),
        ),
        scratch_shapes=[pltpu.VMEM((lanes, length), jnp.bfloat16)],
        compiler_params=pltpu.CompilerParams(vmem_limit_bytes=VMEM_BYTES),
        cost_estimate=pl.CostEstimate(flops=1, bytes_accessed=1, transcendentals=1),
        name="attention_forward",
    )(projected, *tables, first)


def attention_backward(queries, key_heads, projected, grad_context, logsum, tables, first):
    length, width = queries.shape
    lanes = tables[0].shape[1]
    return pl.pallas_call(
        backward_kernel,
        out_shape=jax.ShapeDtypeStruct((length, 3 * width), jnp.bfloat16),
        scratch_shapes=[
            pltpu.VMEM((lanes, length), jnp.bfloat16),
            pltpu.VMEM((length, lanes), jnp.float32),
            pltpu.VMEM((length, lanes), jnp.float32),
            pltpu.VMEM((length, lanes), jnp.float32),
        ],
        compiler_params=pltpu.CompilerParams(vmem_limit_bytes=VMEM_BYTES),
        cost_estimate=pl.CostEstimate(flops=1, bytes_accessed=1, transcendentals=1),
        name="attention_backward",
    )(queries, key_heads, projected, grad_context, logsum, *tables, first)


def gate_backward(gate_values, up_values, grad_hidden):
    sigmoid_gate = jax.nn.sigmoid(gate_values)
    silu_gate = gate_values * sigmoid_gate
    grad_gate = (
        grad_hidden * up_values * sigmoid_gate * (1.0 + gate_values * (1.0 - sigmoid_gate))
    ).astype(jnp.bfloat16)
    grad_up = (grad_hidden * silu_gate).astype(jnp.bfloat16)
    return (grad_gate, grad_up)


def permute(value, axis, offset):
    size = lax.axis_size(axis)
    return lax.ppermute(value, axis, [(i, i ^ offset) for i in range(size)])


def gather_dp(piece):
    return [piece] + [permute(piece, "dp", k) for k in range(1, lax.axis_size("dp"))]


def near_dp(piece):
    return [piece, permute(piece, "dp", 1), permute(piece, "dp", 2)]


def corner_dp(pieces):
    middle = pieces[0].shape[0] // 2
    return jnp.concatenate(
        [permute(pieces[2][:middle], "dp", 1), permute(pieces[1][middle:], "dp", 2)], axis=0
    )


def send_corner(pieces):
    middle = pieces[0].shape[0] // 2
    return (permute(pieces[3][:middle], "dp", 2), permute(pieces[3][middle:], "dp", 1))


def add_corner(pieces, corner):
    middle = pieces[0].shape[0] // 2
    first = total([pieces[1][:middle], corner[0]]).astype(jnp.bfloat16)
    second = total([pieces[2][middle:], corner[1]]).astype(jnp.bfloat16)
    return [
        jnp.concatenate([first, pieces[1][middle:]], axis=0),
        jnp.concatenate([pieces[2][:middle], second], axis=0),
    ]


def send_near(pieces, corner):
    first, second = add_corner(pieces, corner)
    return [permute(first, "dp", 1), permute(second, "dp", 2)]


def total(parts):
    result = parts[0].astype(jnp.float32)
    for piece in parts[1:]:
        result = result + piece.astype(jnp.float32)
    return result


def gather_seq(piece):
    return lax.all_gather(piece, "seq", axis=0, tiled=True)


def scatter_seq(terms):
    return lax.psum_scatter(
        terms.astype(jnp.bfloat16), "seq", scatter_dimension=0, tiled=True
    ).astype(jnp.float32)


def after(value, *others):
    return lax.optimization_barrier((value,) + others)[0]


def place(pieces, index):
    block = pieces[0].shape[0]
    result = jnp.zeros((block * len(pieces),) + pieces[0].shape[1:], pieces[0].dtype)
    for k, piece in enumerate(pieces):
        result = lax.dynamic_update_slice_in_dim(result, piece, (index ^ k) * block, 0)
    return result


def per_device(
    layer_input,
    doc_lengths,
    language,
    lang_table,
    attn_norm_gain,
    attn_norm_bias,
    qkv_weight,
    qkv_bias,
    out_weight,
    mlp_norm_gain,
    mlp_norm_bias,
    gate_weight,
    up_weight,
    down_weight,
    cotangent,
):
    tokens = layer_input.shape[1]
    groups = lax.axis_size("seq")
    rows = lax.axis_size("dp")
    devices = rows * groups
    at_dp = lax.axis_index("dp")
    at_seq = lax.axis_index("seq")
    length = tokens * groups
    heads_here = HEADS // groups
    local_width = heads_here * HEAD
    own = D // devices
    whole_heads = own % HEAD == 0
    deal = (rows, groups, own) if whole_heads else (1, groups, local_width)
    at_deal = (0, 0, at_seq, 0)
    owner = [(i, (i % groups) * rows + i // groups) for i in range(devices)]
    back = [(b, a) for a, b in owner]

    def to_heads(values):
        count = values.shape[0]
        return lax.dynamic_slice(
            values.reshape((count,) + deal), at_deal, (count, deal[0], 1, deal[2])
        ).reshape(count, local_width)

    def from_heads(values):
        count = values.shape[0]
        return lax.dynamic_update_slice(
            jnp.zeros((count,) + deal, values.dtype),
            values.reshape(count, deal[0], 1, deal[2]),
            at_deal,
        ).reshape(count, D)

    phase = lax.optimization_barrier
    grad_out = cotangent[0]

    def dp_terms(terms):
        block = terms.shape[0] // rows
        return [
            lax.dynamic_slice_in_dim(terms, (at_dp ^ k) * block, block, 0) for k in range(rows)
        ]

    small = jnp.concatenate(
        [
            lang_table,
            attn_norm_gain[None],
            attn_norm_bias[None],
            mlp_norm_gain[None],
            mlp_norm_bias[None],
            qkv_bias,
            jnp.broadcast_to(language.astype(jnp.bfloat16)[:, None], (1, own)),
        ],
        axis=0,
    )
    ride = 16
    riders = jnp.zeros((ride * 3 * local_width,), jnp.bfloat16)
    riders = lax.dynamic_update_slice(riders, small.reshape(-1), (0,))
    riders = riders.reshape(ride, 3 * local_width)
    if whole_heads and rows % 2 == 0:
        dealt = deal_columns(qkv_weight, riders, groups, rows)
    else:
        dealt = jnp.concatenate(
            [
                qkv_weight.reshape((own, 3) + deal)
                .transpose(3, 0, 1, 2, 4)
                .reshape(groups, own, 3 * local_width),
                jnp.broadcast_to(riders[None], (groups,) + riders.shape),
            ],
            axis=1,
        )
    part = lax.all_to_all(dealt, "seq", split_axis=0, concat_axis=0, tiled=True)
    chips = groups // 2
    input_all = gather_seq(layer_input[0])
    spread = place(gather_dp(part[:, own:].reshape(groups, -1)), at_dp)
    qkv_pieces = near_dp(part[:, :own].reshape(groups * own, 3 * local_width))
    input_all, spread, grad_far = phase((input_all, spread, grad_out))
    grad_pieces = [grad_out] + [permute(grad_far, "seq", 2 * k) for k in range(1, chips)]
    spread = spread[:, : small.size].reshape((devices,) + small.shape)
    table = jnp.swapaxes(spread, 0, 1).reshape(small.shape[0], D).astype(jnp.float32)
    languages = spread[:, LANGS + 7, 0].astype(jnp.int32)
    gain_attn = table[LANGS]
    bias_attn = table[LANGS + 1]
    gain_mlp = table[LANGS + 2]
    bias_mlp = table[LANGS + 3]
    bias_qkv = to_heads(table[LANGS + 4 : LANGS + 7]).reshape(3 * local_width)
    chooser = (jnp.arange(LANGS, dtype=jnp.int32) == language[0]).astype(jnp.float32)
    lang_row = jnp.sum(chooser[:, None] * table[:LANGS], axis=0)[None, :]
    offsets, cosines, sines = row_tables(doc_lengths[0], length)
    tables = rotation_tables(cosines, sines, min(128, local_width))
    first = offsets[None, :]
    resid_in = layer_input[0].astype(jnp.float32) + lang_row
    unused, scaled_attn, inverse_attn = norm_forward(resid_in, gain_attn, bias_attn)
    normed_all = norm_forward(input_all.astype(jnp.float32) + lang_row, gain_attn, bias_attn)[
        0
    ].astype(jnp.bfloat16)
    qkv_pieces, tables, first, resid_in = phase((qkv_pieces, tables, first, resid_in))
    head_qkv = place(qkv_pieces + [corner_dp(qkv_pieces)], at_dp)
    head_qkv, normed_all, out_rows, gate_rows = phase(
        (head_qkv, normed_all, out_weight, gate_weight.T)
    )
    if not whole_heads:
        out_rows = lax.ppermute(out_rows, ("dp", "seq"), back)
    head_out = place(gather_dp(out_rows), at_dp)
    gate_pieces = near_dp(gate_rows)
    projected = (
        jnp.dot(normed_all, head_qkv, preferred_element_type=jnp.float32) + bias_qkv
    ).astype(jnp.bfloat16)
    rot_query, rot_key, context_all, logsum = attention_forward(projected, tables, first)
    out_terms = jnp.dot(context_all, head_out, preferred_element_type=jnp.float32).astype(
        jnp.bfloat16
    )
    out_terms, grad_pieces, gate_pieces, up_rows = phase(
        (out_terms, grad_pieces, gate_pieces, up_weight.T)
    )
    attn_out = scatter_seq(out_terms)
    gate_pieces = gate_pieces + [corner_dp(gate_pieces)]
    up_pieces = near_dp(up_rows)
    mates = permute(jnp.concatenate(grad_pieces, axis=0), "seq", 1)
    gate_pieces, up_pieces, mates = phase((gate_pieces, up_pieces, mates))
    up_pieces = up_pieces + [corner_dp(up_pieces)]
    mates = jnp.split(mates, chips, axis=0)
    grad_all = place([piece for pair in zip(grad_pieces, mates) for piece in pair], at_seq)
    attn_out, up_pieces, grad_all, down_rows = phase((attn_out, up_pieces, grad_all, down_weight))
    resid_mid = resid_in + attn_out
    normed_mlp, scaled_mlp, inverse_mlp = norm_forward(resid_mid, gain_mlp, bias_mlp)
    rows_all = gather_seq(normed_mlp.astype(jnp.bfloat16))
    down_pieces = near_dp(down_rows)
    down_pieces = phase(down_pieces)
    cols_down = jnp.concatenate(down_pieces + [corner_dp(down_pieces)], axis=0)
    cols_gate = jnp.concatenate(gate_pieces, axis=0)
    cols_up = jnp.concatenate(up_pieces, axis=0)
    grad_hidden = contract(grad_all, cols_down, 1, 1)
    rows_all, cols_down, cols_gate, cols_up, grad_hidden = phase(
        (rows_all, cols_down, cols_gate, cols_up, grad_hidden)
    )
    gate_values = contract(rows_all, cols_gate, 1, 1)
    up_values = contract(rows_all, cols_up, 1, 1)
    hidden = (jax.nn.silu(gate_values) * up_values).astype(jnp.bfloat16)
    grad_gate, grad_up = gate_backward(gate_values, up_values, grad_hidden)
    grad_rows = (
        contract(grad_gate, cols_gate, 1, 0) + contract(grad_up, cols_up, 1, 0)
    ).astype(jnp.bfloat16)
    grad_rows, grad_gate, grad_up, hidden = phase((grad_rows, grad_gate, grad_up, hidden))
    grad_normed_mlp = scatter_seq(grad_rows)
    gate_terms = jnp.split(
        contract(grad_gate, rows_all, 0, 0).astype(jnp.bfloat16), rows, axis=0
    )
    gate_corner = send_corner(gate_terms)
    mlp_terms = (
        contract(hidden, cols_down, 1, 0).astype(jnp.bfloat16).reshape(chips, 2, tokens, D)
    )
    mlp_other = permute(
        lax.dynamic_index_in_dim(mlp_terms, 1 - at_seq % 2, 1, keepdims=False), "seq", 1
    )
    up_terms = contract(grad_up, rows_all, 0, 0).astype(jnp.bfloat16)
    gate_corner, gate_terms, mlp_terms, mlp_other, up_terms = phase(
        (gate_corner, gate_terms, mlp_terms, mlp_other, up_terms)
    )
    gate_near = send_near(gate_terms, gate_corner)
    mlp_pairs = total(
        [lax.dynamic_index_in_dim(mlp_terms, at_seq % 2, 1, keepdims=False), mlp_other]
    ).astype(jnp.bfloat16)
    down_terms = contract(hidden, grad_all, 0, 0).astype(jnp.bfloat16)
    mlp_pieces = [
        lax.dynamic_index_in_dim(mlp_pairs, (at_seq // 2) ^ k, 0, keepdims=False)
        for k in range(chips)
    ]
    grad_normed_mlp, gate_near, up_terms, mlp_pieces, down_terms = phase(
        (grad_normed_mlp, gate_near, up_terms, mlp_pieces, down_terms)
    )
    out_gate = total([gate_terms[0], *gate_near])
    grad_mid_norm, grad_gain_mlp, grad_bias_mlp = norm_backward(
        grad_normed_mlp, scaled_mlp, inverse_mlp, gain_mlp
    )
    grad_mid = grad_out.astype(jnp.float32) + grad_mid_norm
    branch_all = gather_seq(grad_mid.astype(jnp.bfloat16))
    up_terms = jnp.split(up_terms, rows, axis=0)
    down_terms = jnp.split(down_terms, rows, axis=0)
    up_corner = send_corner(up_terms)
    mlp_sums = [permute(mlp_pieces[1], "seq", 2)]
    up_corner, up_terms, down_terms = phase((up_corner, up_terms, down_terms))
    up_near = send_near(up_terms, up_corner)
    down_corner = send_corner(down_terms)
    down_terms = down_terms[:1] + add_corner(down_terms, down_corner)
    branch_all, up_near, mlp_sums, mlp_pieces, down_terms = phase(
        (branch_all, up_near, mlp_sums, mlp_pieces, down_terms)
    )
    out_up = total([up_terms[0], *up_near])
    mlp_sums = mlp_sums + [permute(mlp_pieces[k], "seq", 2 * k) for k in range(2, chips - 1)]
    down_near = [permute(down_terms[1], "dp", 1), permute(down_terms[2], "dp", 2)]
    grad_heads = contract(branch_all, head_out, 1, 1).astype(jnp.bfloat16)
    grad_stack = attention_backward(
        rot_query, rot_key, projected, grad_heads, logsum, tables, first
    )
    grad_stack, down_near = phase((grad_stack, down_near))
    slice_terms = contract(normed_all, grad_stack, 0, 0).astype(jnp.bfloat16)
    attn_terms = contract(grad_stack, head_qkv, 1, 1).astype(jnp.bfloat16)
    slice_pieces = dp_terms(slice_terms)
    attn_terms, slice_pieces, grad_stack, branch_all, mlp_sums, mlp_pieces, input_all = phase(
        (attn_terms, slice_pieces, grad_stack, branch_all, mlp_sums, mlp_pieces, input_all)
    )
    mlp_sums = mlp_sums + [permute(mlp_pieces[-1], "seq", 2 * (chips - 1))]
    out_down = total([down_terms[0], *down_near])
    half = D // 2
    attn_first = scatter_seq(attn_terms[:, :half])
    attn_second = scatter_seq(attn_terms[:, half:])
    slice_corner = send_corner(slice_pieces)
    unused, scaled_all, inverse_all = norm_forward(
        input_all.astype(jnp.float32) + lang_row, gain_attn, bias_attn
    )
    grad_in_terms, grad_gain_attn, grad_bias_attn = norm_backward(
        attn_terms.astype(jnp.float32), scaled_all, inverse_all, gain_attn
    )
    grad_input_sum = jnp.sum(grad_mid, axis=0) + jnp.sum(grad_in_terms, axis=0)
    grad_bias_qkv = jnp.sum(grad_stack.astype(jnp.float32), axis=0).reshape(3, local_width)
    terms = jnp.concatenate(
        [
            grad_gain_attn[None],
            grad_bias_attn[None],
            grad_gain_mlp[None],
            grad_bias_mlp[None],
            grad_input_sum[None],
            from_heads(grad_bias_qkv),
        ],
        axis=0,
    )
    head_out_terms = dp_terms(contract(context_all, branch_all, 0, 0).astype(jnp.bfloat16))
    terms, head_out_terms, slice_corner, slice_pieces, mlp_sums = phase(
        (terms, head_out_terms, slice_corner, slice_pieces, mlp_sums)
    )
    slice_near = send_near(slice_pieces, slice_corner)
    arrived = lax.all_to_all(
        terms.reshape(terms.shape[0], devices, own).swapaxes(0, 1),
        ("dp", "seq"),
        split_axis=0,
        concat_axis=0,
        tiled=True,
    )
    attn_first, arrived, slice_near, head_out_terms = phase(
        (attn_first, arrived, slice_near, head_out_terms)
    )
    home = lax.all_to_all(
        total([slice_pieces[0], *slice_near])
        .astype(jnp.bfloat16)
        .reshape(groups, own, 3 * local_width),
        "seq",
        split_axis=0,
        concat_axis=0,
        tiled=True,
    )
    out_arrived = [permute(head_out_terms[k], "dp", k) for k in range(1, rows)]
    home, out_arrived, attn_second = phase((home, out_arrived, attn_second))
    grad_normed_attn = jnp.concatenate([attn_first, attn_second], axis=1)
    if whole_heads and rows % 2 == 0:
        grad_qkv_out = columns_in_place([home], rows)
    else:
        grad_qkv_out = (
            home.reshape(groups, own, 3, deal[0], deal[2])
            .transpose(1, 2, 3, 0, 4)
            .reshape(own, 3 * D)
            .astype(jnp.float32)
        )
    out_proj = total([head_out_terms[0]] + out_arrived)
    if not whole_heads:
        out_proj = lax.ppermute(out_proj, ("dp", "seq"), owner)
    mlp_out = total([mlp_pieces[0]] + mlp_sums)
    layer_output = (resid_mid + mlp_out).astype(jnp.bfloat16)
    grad_input = grad_mid + norm_backward(
        grad_normed_attn, scaled_attn, inverse_attn, gain_attn
    )[0]
    summed = jnp.sum(arrived, axis=0)
    members = (languages[:, None] == jnp.arange(LANGS, dtype=jnp.int32)[None, :]).astype(
        jnp.float32
    )
    lang_g = jnp.sum(members[:, :, None] * arrived[:, 4][:, None, :], axis=0)
    return (
        layer_output[None],
        grad_input[None],
        lang_g,
        summed[0],
        summed[1],
        grad_qkv_out,
        summed[5:8],
        out_proj,
        summed[2],
        summed[3],
        out_gate.T,
        out_up.T,
        out_down,
    )


def solution(mesh):
    placed = (
        P("dp", "seq", None),
        P("dp", None),
        P("dp"),
        P(None, ("dp", "seq")),
        P(("dp", "seq")),
        P(("dp", "seq")),
        P(("dp", "seq"), None),
        P(None, ("dp", "seq")),
        P(("dp", "seq"), None),
        P(("dp", "seq")),
        P(("dp", "seq")),
        P(None, ("dp", "seq")),
        P(None, ("dp", "seq")),
        P(("dp", "seq"), None),
        P("dp", "seq", None),
    )
    return jax.shard_map(
        per_device,
        mesh=mesh,
        in_specs=placed,
        out_specs=(
            P("dp", "seq", None),
            P("dp", "seq", None),
            P(None, ("dp", "seq")),
            P(("dp", "seq")),
            P(("dp", "seq")),
            P(("dp", "seq"), None),
            P(None, ("dp", "seq")),
            P(("dp", "seq"), None),
            P(("dp", "seq")),
            P(("dp", "seq")),
            P(None, ("dp", "seq")),
            P(None, ("dp", "seq")),
            P(("dp", "seq"), None),
        ),
        check_vma=False,
    )
```

```python
import jax
import jax.numpy as jnp
from jax import lax
from jax.experimental import pallas as pl
from jax.experimental.pallas import tpu as pltpu
from jax.sharding import PartitionSpec as P

D = 2048
HEADS = 32
HEAD = 64
ROT = 16
LANGS = 7


EPS = 1e-05
BASE = 10000.0
NEG = -1e30


def contract(left, right, left_dim, right_dim):
    return lax.dot_general(
        left, right, (((left_dim,), (right_dim,)), ((), ())), preferred_element_type=jnp.float32
    )


def norm_forward(values, gain, bias):
    average = jnp.mean(values, axis=-1, keepdims=True)
    centered = values - average
    variance = jnp.mean(centered * centered, axis=-1, keepdims=True)
    inverse = lax.rsqrt(variance + EPS)
    scaled = centered * inverse
    return (scaled * gain + bias, scaled, inverse)


def norm_backward(grad_normed, scaled, inverse, gain):
    grad_scaled = grad_normed * gain
    grad_values = inverse * (
        grad_scaled
        - jnp.mean(grad_scaled, axis=-1, keepdims=True)
        - scaled * jnp.mean(grad_scaled * scaled, axis=-1, keepdims=True)
    )
    return (grad_values, jnp.sum(grad_normed * scaled, axis=0), jnp.sum(grad_normed, axis=0))


def row_tables(doc_lengths, length):
    ends = jnp.cumsum(doc_lengths)
    starts = ends - doc_lengths
    places = jnp.arange(length, dtype=jnp.int32)
    segment = jnp.sum((places[:, None] >= ends[None, :]).astype(jnp.int32), axis=1)
    member = segment[:, None] == jnp.arange(ends.shape[0], dtype=jnp.int32)[None, :]
    offsets = jnp.sum(jnp.where(member, starts[None, :], 0), axis=1)
    position = (places - offsets).astype(jnp.float32)
    half_rot = ROT // 2
    freq = BASE ** (-(2.0 * jnp.arange(half_rot, dtype=jnp.float32)) / ROT)
    angles = position[:, None] * freq[None, :]
    return (offsets, jnp.cos(angles), jnp.sin(angles))


def head_lanes(shape, dim, head):
    place = lax.broadcasted_iota(jnp.int32, shape, dim)
    return (place >= head * HEAD) & (place < (head + 1) * HEAD)


def turn(values, tables, direction):
    lanes = values.shape[1]
    cosines, sines_former, sines_latter = tables
    after = pltpu.roll(values, lanes - ROT // 2, 1)
    before = pltpu.roll(values, ROT // 2, 1)
    return values * cosines + direction * (before * sines_latter - after * sines_former)


def allowed_pairs(first_ref, start, block, keys):
    key_at = lax.broadcasted_iota(jnp.int32, (keys, block), 0)
    query_at = start + lax.broadcasted_iota(jnp.int32, (keys, block), 1)
    return (key_at >= first_ref[:, pl.ds(start, block)]) & (key_at <= query_at)


def over_blocks(length, block, step):
    count = length // block
    if count <= 4:
        for i in range(count):
            step(i * block, (i + 1) * block)
    else:

        def body(i, carry):
            step(pl.multiple_of(i * block, block), length)
            return carry

        lax.fori_loop(0, count, body, 0)


def forward_kernel(
    qkv_ref, cos_ref, former_ref, latter_ref, first_ref,
    query_ref, key_ref, context_ref, logsum_ref, value_t,
):
    length, width = query_ref.shape
    lanes = cos_ref.shape[1]
    block = min(256, length)
    tables = (cos_ref[...], former_ref[...], latter_ref[...])
    for group in range(width // lanes):
        part = slice(group * lanes, (group + 1) * lanes)

        def columns(c):
            begin = c * width + group * lanes
            return qkv_ref[:, begin : begin + lanes].astype(jnp.float32)

        query_ref[:, part] = turn(columns(0), tables, 1.0).astype(jnp.bfloat16)
        key_ref[:, part] = turn(columns(1), tables, 1.0).astype(jnp.bfloat16)
        value_t[...] = columns(2).T.astype(jnp.bfloat16)

        def step(start, keys):
            queries = query_ref[pl.ds(start, block), part].astype(jnp.float32) * HEAD ** (-0.5)
            allowed = allowed_pairs(first_ref, start, block, keys)
            found = []
            for head in range(lanes // HEAD):
                own = jnp.where(head_lanes(queries.shape, 1, head), queries, 0.0)
                scores = contract(key_ref[0:keys, part], own.astype(jnp.bfloat16), 1, 1)
                scores = jnp.where(allowed, scores, NEG)
                most = jnp.max(scores, axis=0, keepdims=True)
                weights = jnp.exp(scores - most)
                total = jnp.sum(weights, axis=0, keepdims=True)
                probs = (weights * (1.0 / total)).astype(jnp.bfloat16)
                logsum_ref[
                    pl.ds(group * (lanes // HEAD) + head, 1), pl.ds(start, block)
                ] = most + jnp.log(total)
                context = contract(value_t[:, 0:keys], probs, 1, 0)
                found.append(context[head * HEAD : (head + 1) * HEAD])
            context_ref[pl.ds(start, block), part] = (
                jnp.concatenate(found, axis=0).T.astype(jnp.bfloat16)
            )

        over_blocks(length, block, step)


def backward_kernel(
    query_ref, key_ref, qkv_ref, context_grad_ref, logsum_ref, cos_ref, former_ref, latter_ref,
    first_ref, grad_ref, key_t, grad_query, grad_key, grad_value,
):
    length, width = query_ref.shape
    lanes = cos_ref.shape[1]
    block = min(256, length)
    scale = HEAD ** (-0.5)
    tables = (cos_ref[...], former_ref[...], latter_ref[...])
    for group in range(width // lanes):
        part = slice(group * lanes, (group + 1) * lanes)
        value_part = slice(2 * width + group * lanes, 2 * width + (group + 1) * lanes)
        key_t[...] = key_ref[:, part].astype(jnp.float32).T.astype(jnp.bfloat16)
        grad_key[...] = jnp.zeros_like(grad_key)
        grad_value[...] = jnp.zeros_like(grad_value)

        def step(start, keys):
            queries = query_ref[pl.ds(start, block), part].astype(jnp.float32) * scale
            grads = context_grad_ref[pl.ds(start, block), part].astype(jnp.float32)
            allowed = allowed_pairs(first_ref, start, block, keys)
            found = []
            for head in range(lanes // HEAD):
                mine = head_lanes(queries.shape, 1, head)
                own_query = jnp.where(mine, queries, 0.0).astype(jnp.bfloat16)
                own_grad = jnp.where(mine, grads, 0.0).astype(jnp.bfloat16)
                scores = contract(key_ref[0:keys, part], own_query, 1, 1)
                logsum = logsum_ref[
                    pl.ds(group * (lanes // HEAD) + head, 1), pl.ds(start, block)
                ]
                soft = jnp.exp(jnp.where(allowed, scores, NEG) - logsum)
                grad_soft = contract(qkv_ref[0:keys, value_part], own_grad, 1, 1)
                weighed = soft * grad_soft
                delta = jnp.sum(weighed, axis=0, keepdims=True)
                grad_scores = (weighed - soft * delta).astype(jnp.bfloat16)
                grad_value[0:keys] += contract(soft.astype(jnp.bfloat16), own_grad, 1, 0)
                grad_key[0:keys] += contract(grad_scores, own_query, 1, 0)
                turned = contract(key_t[:, 0:keys], grad_scores, 1, 0)
                found.append(turned[head * HEAD : (head + 1) * HEAD])
            grad_query[pl.ds(start, block), :] = jnp.concatenate(found, axis=0).T * scale

        over_blocks(length, block, step)
        for c, grads in ((0, grad_query), (1, grad_key)):
            begin = c * width + group * lanes
            grad_ref[:, begin : begin + lanes] = turn(grads[...], tables, -1.0).astype(
                jnp.bfloat16
            )
        grad_ref[:, value_part] = grad_value[...].astype(jnp.bfloat16)


def columns_kernel(part_refs, out_ref, deal, width):
    row = 0
    for ref in part_refs:
        groups, rows = ref.shape[0], ref.shape[1]
        for c in range(3):
            for d in range(0, deal, 2):
                for s in range(0, groups, 2):
                    begin = c * deal * HEAD + d * HEAD
                    left = ref[s, :, begin : begin + 2 * HEAD].astype(jnp.float32)
                    right = ref[s + 1, :, begin : begin + 2 * HEAD].astype(jnp.float32)
                    lower = lax.broadcasted_iota(jnp.int32, left.shape, 1) < HEAD
                    out = c * width + d * groups * HEAD + s * HEAD
                    out_ref[row : row + rows, out : out + 2 * HEAD] = jnp.where(
                        lower, left, pltpu.roll(right, HEAD, 1)
                    )
                    out = out + groups * HEAD
                    out_ref[row : row + rows, out : out + 2 * HEAD] = jnp.where(
                        lower, pltpu.roll(left, HEAD, 1), right
                    )
        row += rows


def columns_in_place(parts, deal):
    rows = sum(part.shape[1] for part in parts)
    width = parts[0].shape[0] * deal * HEAD

    def kernel(*refs):
        columns_kernel(refs[:-1], refs[-1], deal, width)

    return pl.pallas_call(
        kernel,
        out_shape=jax.ShapeDtypeStruct((rows, 3 * width), jnp.float32),
        compiler_params=pltpu.CompilerParams(vmem_limit_bytes=VMEM_BYTES),
        name="columns_in_place",
    )(*parts)


def deal_kernel(weight_ref, riders_ref, out_ref, deal):
    groups = out_ref.shape[0]
    rows, width = weight_ref.shape[0], weight_ref.shape[1] // 3
    for c in range(3):
        for d in range(0, deal, 2):
            for s in range(0, groups, 2):
                begin = c * width + d * groups * HEAD + s * HEAD
                upper = weight_ref[:, begin : begin + 2 * HEAD].astype(jnp.float32)
                begin = begin + groups * HEAD
                after = weight_ref[:, begin : begin + 2 * HEAD].astype(jnp.float32)
                lower = lax.broadcasted_iota(jnp.int32, upper.shape, 1) < HEAD
                out = c * deal * HEAD + d * HEAD
                out_ref[s, 0:rows, out : out + 2 * HEAD] = jnp.where(
                    lower, upper, pltpu.roll(after, HEAD, 1)
                ).astype(jnp.bfloat16)
                out_ref[s + 1, 0:rows, out : out + 2 * HEAD] = jnp.where(
                    lower, pltpu.roll(upper, HEAD, 1), after
                ).astype(jnp.bfloat16)
    for s in range(groups):
        out_ref[s, rows:, :] = riders_ref[...]


def deal_columns(weight, riders, groups, deal):
    def kernel(*refs):
        deal_kernel(*refs, deal)

    return pl.pallas_call(
        kernel,
        out_shape=jax.ShapeDtypeStruct(
            (groups, weight.shape[0] + riders.shape[0], riders.shape[1]), jnp.bfloat16
        ),
        compiler_params=pltpu.CompilerParams(vmem_limit_bytes=VMEM_BYTES),
        name="deal_columns",
    )(weight, riders)


SMALL_COST = pl.CostEstimate(flops=1, bytes_accessed=1, transcendentals=1)


def norm_sums_kernel(values_ref, terms_ref, lang_ref, gain_ref, out_ref):
    @pl.when(pl.program_id(0) == 0)
    def clear():
        out_ref[...] = jnp.zeros_like(out_ref)

    values = values_ref[...].astype(jnp.float32) + lang_ref[...]
    terms = terms_ref[...].astype(jnp.float32)
    unused, scaled, inverse = norm_forward(values, 1.0, 0.0)
    grad_values, gain_sum, bias_sum = norm_backward(terms, scaled, inverse, gain_ref[...])
    out_ref[0:1] += gain_sum[None]
    out_ref[1:2] += bias_sum[None]
    out_ref[2:3] += jnp.sum(grad_values, axis=0, keepdims=True)


def norm_sums(values, terms, lang_row, gain):
    length, width = values.shape
    block = min(256, length)
    rows = pl.BlockSpec((block, width), lambda i: (i, 0))
    whole = pl.BlockSpec((1, width), lambda i: (0, 0))
    return pl.pallas_call(
        norm_sums_kernel,
        grid=(length // block,),
        in_specs=[rows, rows, whole, whole],
        out_specs=pl.BlockSpec((8, width), lambda i: (0, 0)),
        out_shape=jax.ShapeDtypeStruct((8, width), jnp.float32),
        compiler_params=pltpu.CompilerParams(vmem_limit_bytes=VMEM_BYTES),
        cost_estimate=SMALL_COST,
        name="norm_sums",
    )(values, terms, lang_row, gain[None])


def rotation_tables(cosines, sines, lanes):
    length = cosines.shape[0]
    rest = jnp.ones((length, HEAD - ROT), jnp.float32)
    none = jnp.zeros_like(sines)
    heads = lanes // HEAD
    return (
        jnp.tile(jnp.concatenate([cosines, cosines, rest], axis=1), (1, heads)),
        jnp.tile(jnp.concatenate([sines, none, 0.0 * rest], axis=1), (1, heads)),
        jnp.tile(jnp.concatenate([none, sines, 0.0 * rest], axis=1), (1, heads)),
    )


VMEM_BYTES = 48 * 1024 * 1024


def attention_forward(projected, tables, first):
    length, width = projected.shape[0], projected.shape[1] // 3
    lanes = tables[0].shape[1]
    rows = jax.ShapeDtypeStruct((length, width), jnp.bfloat16)
    return pl.pallas_call(
        forward_kernel,
        out_shape=(
            rows,
            rows,
            rows,
            jax.ShapeDtypeStruct((width // HEAD, length), jnp.float32),
        ),
        scratch_shapes=[pltpu.VMEM((lanes, length), jnp.bfloat16)],
        compiler_params=pltpu.CompilerParams(vmem_limit_bytes=VMEM_BYTES),
        cost_estimate=SMALL_COST,
        name="attention_forward",
    )(projected, *tables, first)


def attention_backward(queries, key_heads, projected, grad_context, logsum, tables, first):
    length, width = queries.shape
    lanes = tables[0].shape[1]
    return pl.pallas_call(
        backward_kernel,
        out_shape=jax.ShapeDtypeStruct((length, 3 * width), jnp.bfloat16),
        scratch_shapes=[
            pltpu.VMEM((lanes, length), jnp.bfloat16),
            pltpu.VMEM((length, lanes), jnp.float32),
            pltpu.VMEM((length, lanes), jnp.float32),
            pltpu.VMEM((length, lanes), jnp.float32),
        ],
        compiler_params=pltpu.CompilerParams(vmem_limit_bytes=VMEM_BYTES),
        cost_estimate=SMALL_COST,
        name="attention_backward",
    )(queries, key_heads, projected, grad_context, logsum, *tables, first)


def gate_backward(gate_values, up_values, grad_hidden):
    sigmoid_gate = jax.nn.sigmoid(gate_values)
    silu_gate = gate_values * sigmoid_gate
    grad_gate = (
        grad_hidden * up_values * sigmoid_gate * (1.0 + gate_values * (1.0 - sigmoid_gate))
    ).astype(jnp.bfloat16)
    grad_up = (grad_hidden * silu_gate).astype(jnp.bfloat16)
    return (grad_gate, grad_up)


def permute(value, axis, offset):
    size = lax.axis_size(axis)
    return lax.ppermute(value, axis, [(i, i ^ offset) for i in range(size)])


def gather_dp(piece):
    return [piece] + [permute(piece, "dp", k) for k in range(1, lax.axis_size("dp"))]


def scatter_dp(pieces):
    return total([pieces[0]] + [permute(pieces[k], "dp", k) for k in range(1, len(pieces))])


def near_dp(piece):
    return [piece, permute(piece, "dp", 1), permute(piece, "dp", 2)]


def corner_dp(pieces):
    middle = pieces[0].shape[0] // 2
    return jnp.concatenate(
        [permute(pieces[2][:middle], "dp", 1), permute(pieces[1][middle:], "dp", 2)], axis=0
    )


def send_corner(pieces):
    middle = pieces[0].shape[0] // 2
    return (permute(pieces[3][:middle], "dp", 2), permute(pieces[3][middle:], "dp", 1))


def add_corner(pieces, corner):
    middle = pieces[0].shape[0] // 2
    first = total([pieces[1][:middle], corner[0]]).astype(jnp.bfloat16)
    second = total([pieces[2][middle:], corner[1]]).astype(jnp.bfloat16)
    return [
        jnp.concatenate([first, pieces[1][middle:]], axis=0),
        jnp.concatenate([pieces[2][:middle], second], axis=0),
    ]


def send_near(pieces, corner):
    first, second = add_corner(pieces, corner)
    return [permute(first, "dp", 1), permute(second, "dp", 2)]


def total(parts):
    result = parts[0].astype(jnp.float32)
    for piece in parts[1:]:
        result = result + piece.astype(jnp.float32)
    return result


def gather_seq(piece):
    return lax.all_gather(piece, "seq", axis=0, tiled=True)


def scatter_seq(terms):
    return lax.psum_scatter(
        terms.astype(jnp.bfloat16), "seq", scatter_dimension=0, tiled=True
    ).astype(jnp.float32)


def after(value, *others):
    return lax.optimization_barrier((value,) + others)[0]


def place(pieces, index):
    block = pieces[0].shape[0]
    result = jnp.zeros((block * len(pieces),) + pieces[0].shape[1:], pieces[0].dtype)
    for k, piece in enumerate(pieces):
        result = lax.dynamic_update_slice_in_dim(result, piece, (index ^ k) * block, 0)
    return result


def per_device(
    layer_input,
    doc_lengths,
    language,
    lang_table,
    attn_norm_gain,
    attn_norm_bias,
    qkv_weight,
    qkv_bias,
    out_weight,
    mlp_norm_gain,
    mlp_norm_bias,
    gate_weight,
    up_weight,
    down_weight,
    cotangent,
):
    tokens = layer_input.shape[1]
    groups = lax.axis_size("seq")
    rows = lax.axis_size("dp")
    devices = rows * groups
    at_dp = lax.axis_index("dp")
    at_seq = lax.axis_index("seq")
    length = tokens * groups
    heads_here = HEADS // groups
    local_width = heads_here * HEAD
    own = D // devices
    whole_heads = own % HEAD == 0
    deal = (rows, groups, own) if whole_heads else (1, groups, local_width)
    at_deal = (0, 0, at_seq, 0)
    owner = [(i, (i % groups) * rows + i // groups) for i in range(devices)]
    back = [(b, a) for a, b in owner]

    def to_heads(values):
        count = values.shape[0]
        return lax.dynamic_slice(
            values.reshape((count,) + deal), at_deal, (count, deal[0], 1, deal[2])
        ).reshape(count, local_width)

    def from_heads(values):
        count = values.shape[0]
        return lax.dynamic_update_slice(
            jnp.zeros((count,) + deal, values.dtype),
            values.reshape(count, deal[0], 1, deal[2]),
            at_deal,
        ).reshape(count, D)

    phase = lax.optimization_barrier
    grad_out = cotangent[0]

    def dp_terms(terms):
        block = terms.shape[0] // rows
        return [
            lax.dynamic_slice_in_dim(terms, (at_dp ^ k) * block, block, 0) for k in range(rows)
        ]

    small = jnp.concatenate(
        [
            lang_table,
            attn_norm_gain[None],
            attn_norm_bias[None],
            mlp_norm_gain[None],
            mlp_norm_bias[None],
            qkv_bias,
        ],
        axis=0,
    )
    ride = 16
    riders = jnp.zeros((ride * 3 * local_width,), jnp.bfloat16)
    riders = lax.dynamic_update_slice(riders, small.reshape(-1), (0,))
    riders = riders.reshape(ride, 3 * local_width)
    if whole_heads and rows % 2 == 0:
        dealt = deal_columns(qkv_weight, riders, groups, rows)
    else:
        dealt = jnp.concatenate(
            [
                qkv_weight.reshape((own, 3) + deal)
                .transpose(3, 0, 1, 2, 4)
                .reshape(groups, own, 3 * local_width),
                jnp.broadcast_to(riders[None], (groups,) + riders.shape),
            ],
            axis=1,
        )
    part = lax.all_to_all(dealt, "seq", split_axis=0, concat_axis=0, tiled=True)
    chips = groups // 2
    input_all = gather_seq(layer_input[0])
    spread = place(gather_dp(part[:, own:].reshape(groups, -1)), at_dp)
    qkv_pieces = near_dp(part[:, :own].reshape(groups * own, 3 * local_width))
    input_all, spread, grad_far = phase((input_all, spread, grad_out))
    grad_pieces = [permute(grad_far, "seq", 2 * k) for k in range(2, chips)]
    spread = spread[:, : small.size].reshape((devices,) + small.shape)
    table = jnp.swapaxes(spread, 0, 1).reshape(small.shape[0], D).astype(jnp.float32)
    gain_attn = table[LANGS]
    bias_attn = table[LANGS + 1]
    gain_mlp = table[LANGS + 2]
    bias_mlp = table[LANGS + 3]
    bias_qkv = to_heads(table[LANGS + 4 : LANGS + 7]).reshape(3 * local_width)
    chooser = (jnp.arange(LANGS, dtype=jnp.int32) == language[0]).astype(jnp.float32)
    lang_row = jnp.sum(chooser[:, None] * table[:LANGS], axis=0)[None, :]
    offsets, cosines, sines = row_tables(doc_lengths[0], length)
    tables = rotation_tables(cosines, sines, min(128, local_width))
    first = offsets[None, :]
    resid_in = layer_input[0].astype(jnp.float32) + lang_row
    unused, scaled_attn, inverse_attn = norm_forward(resid_in, gain_attn, bias_attn)
    normed_all = norm_forward(input_all.astype(jnp.float32) + lang_row, gain_attn, bias_attn)[
        0
    ].astype(jnp.bfloat16)
    qkv_pieces, tables, first, resid_in = phase((qkv_pieces, tables, first, resid_in))
    head_qkv = place(qkv_pieces + [corner_dp(qkv_pieces)], at_dp)
    head_qkv, normed_all, out_rows = phase((head_qkv, normed_all, out_weight))
    if not whole_heads:
        out_rows = lax.ppermute(out_rows, ("dp", "seq"), back)
    head_out = place(gather_dp(out_rows), at_dp)
    projected = (
        jnp.dot(normed_all, head_qkv, preferred_element_type=jnp.float32) + bias_qkv
    ).astype(jnp.bfloat16)
    rot_query, rot_key, context_all, logsum = attention_forward(projected, tables, first)
    out_terms = jnp.dot(context_all, head_out, preferred_element_type=jnp.float32).astype(
        jnp.bfloat16
    )
    out_terms, grad_pieces, gate_rows, grad_near = phase(
        (out_terms, grad_pieces, gate_weight.T, grad_out)
    )
    attn_out = scatter_seq(out_terms)
    gate_pieces = near_dp(gate_rows)
    near = permute(grad_near, "seq", 2)
    gate_pieces, near, up_rows = phase((gate_pieces, near, up_weight.T))
    grad_pieces = [grad_out, near, *grad_pieces]
    gate_pieces = gate_pieces + [corner_dp(gate_pieces)]
    up_pieces = near_dp(up_rows)
    mates = permute(jnp.concatenate(grad_pieces, axis=0), "seq", 1)
    mates = jnp.split(mates, chips, axis=0)
    grad_all = place([piece for pair in zip(grad_pieces, mates) for piece in pair], at_seq)
    attn_out, gate_pieces, up_pieces, grad_all, down_rows = phase(
        (attn_out, gate_pieces, up_pieces, grad_all, down_weight)
    )
    resid_mid = resid_in + attn_out
    normed_mlp, scaled_mlp, inverse_mlp = norm_forward(resid_mid, gain_mlp, bias_mlp)
    rows_all = gather_seq(normed_mlp.astype(jnp.bfloat16))
    up_pieces = up_pieces + [corner_dp(up_pieces)]
    down_pieces = near_dp(down_rows)
    down_pieces, up_pieces = phase((down_pieces, up_pieces))
    cols_down = jnp.concatenate(down_pieces + [corner_dp(down_pieces)], axis=0)
    cols_gate = jnp.concatenate(gate_pieces, axis=0)
    cols_up = jnp.concatenate(up_pieces, axis=0)
    grad_hidden = contract(grad_all, cols_down, 1, 1)
    rows_all, cols_down, cols_gate, cols_up, grad_hidden = phase(
        (rows_all, cols_down, cols_gate, cols_up, grad_hidden)
    )
    gate_values = contract(rows_all, cols_gate, 1, 1)
    up_values = contract(rows_all, cols_up, 1, 1)
    hidden = (jax.nn.silu(gate_values) * up_values).astype(jnp.bfloat16)
    grad_gate, grad_up = gate_backward(gate_values, up_values, grad_hidden)
    grad_rows = (
        contract(grad_gate, cols_gate, 1, 0) + contract(grad_up, cols_up, 1, 0)
    ).astype(jnp.bfloat16)
    grad_rows, grad_gate, grad_up, hidden = phase((grad_rows, grad_gate, grad_up, hidden))
    grad_normed_mlp = scatter_seq(grad_rows)
    gate_terms = jnp.split(
        contract(grad_gate, rows_all, 0, 0).astype(jnp.bfloat16), rows, axis=0
    )
    gate_corner = send_corner(gate_terms)
    mlp_terms = (
        contract(hidden, cols_down, 1, 0).astype(jnp.bfloat16).reshape(chips, 2, tokens, D)
    )
    mlp_other = permute(
        lax.dynamic_index_in_dim(mlp_terms, 1 - at_seq % 2, 1, keepdims=False), "seq", 1
    )
    up_terms = contract(grad_up, rows_all, 0, 0).astype(jnp.bfloat16)
    gate_corner, gate_terms, mlp_terms, mlp_other, up_terms = phase(
        (gate_corner, gate_terms, mlp_terms, mlp_other, up_terms)
    )
    gate_near = send_near(gate_terms, gate_corner)
    mlp_pairs = total(
        [lax.dynamic_index_in_dim(mlp_terms, at_seq % 2, 1, keepdims=False), mlp_other]
    ).astype(jnp.bfloat16)
    down_terms = contract(hidden, grad_all, 0, 0).astype(jnp.bfloat16)
    mlp_pieces = [
        lax.dynamic_index_in_dim(mlp_pairs, (at_seq // 2) ^ k, 0, keepdims=False)
        for k in range(chips)
    ]
    grad_normed_mlp, gate_near, up_terms, mlp_pieces, down_terms = phase(
        (grad_normed_mlp, gate_near, up_terms, mlp_pieces, down_terms)
    )
    out_gate = total([gate_terms[0], *gate_near])
    grad_mid_norm, grad_gain_mlp, grad_bias_mlp = norm_backward(
        grad_normed_mlp, scaled_mlp, inverse_mlp, gain_mlp
    )
    grad_mid = grad_out.astype(jnp.float32) + grad_mid_norm
    branch_all = gather_seq(grad_mid.astype(jnp.bfloat16))
    up_terms = jnp.split(up_terms, rows, axis=0)
    down_terms = jnp.split(down_terms, rows, axis=0)
    up_corner = send_corner(up_terms)
    mlp_sums = [permute(mlp_pieces[1], "seq", 2)]
    up_corner, up_terms, down_terms = phase((up_corner, up_terms, down_terms))
    up_near = send_near(up_terms, up_corner)
    down_corner = send_corner(down_terms)
    down_terms = down_terms[:1] + add_corner(down_terms, down_corner)
    branch_all, up_near, mlp_sums, mlp_pieces, down_terms = phase(
        (branch_all, up_near, mlp_sums, mlp_pieces, down_terms)
    )
    out_up = total([up_terms[0], *up_near])
    mlp_sums = mlp_sums + [permute(mlp_pieces[k], "seq", 2 * k) for k in range(2, chips - 1)]
    middle = tokens // 2
    mlp_half = permute(mlp_pieces[-1][:middle], "seq", 2 * (chips - 1))
    down_near = [permute(down_terms[1], "dp", 1), permute(down_terms[2], "dp", 2)]
    grad_heads = contract(branch_all, head_out, 1, 1).astype(jnp.bfloat16)
    grad_stack = attention_backward(
        rot_query, rot_key, projected, grad_heads, logsum, tables, first
    )
    grad_stack, down_near = phase((grad_stack, down_near))
    slice_terms = contract(normed_all, grad_stack, 0, 0).astype(jnp.bfloat16)
    attn_terms = contract(grad_stack, head_qkv, 1, 1).astype(jnp.bfloat16)
    slice_pieces = dp_terms(slice_terms)
    attn_terms, slice_pieces, grad_stack, branch_all, mlp_sums, mlp_half, mlp_pieces = phase(
        (attn_terms, slice_pieces, grad_stack, branch_all, mlp_sums, mlp_half, mlp_pieces)
    )
    grad_normed_attn = scatter_seq(attn_terms)
    slice_arrived = [permute(slice_pieces[k], "dp", k) for k in range(1, rows)]
    mlp_last = permute(mlp_pieces[-1][middle:], "seq", 2 * (chips - 1))
    sums = norm_sums(input_all, attn_terms, lang_row, gain_attn)
    sums, slice_arrived, mlp_sums, mlp_last, down_near, grad_stack, branch_all = phase(
        (sums, slice_arrived, mlp_sums, mlp_last, down_near, grad_stack, branch_all)
    )
    out_pieces = dp_terms(contract(context_all, branch_all, 0, 0).astype(jnp.bfloat16))
    out_arrived = [permute(out_pieces[k], "dp", k) for k in range(1, rows)]
    home = lax.all_to_all(
        total([slice_pieces[0], *slice_arrived])
        .astype(jnp.bfloat16)
        .reshape(groups, own, 3 * local_width),
        "seq",
        split_axis=0,
        concat_axis=0,
        tiled=True,
    )
    grad_bias_qkv = jnp.sum(grad_stack.astype(jnp.float32), axis=0).reshape(3, local_width)
    terms = jnp.concatenate(
        [
            sums[:2],
            grad_gain_mlp[None],
            grad_bias_mlp[None],
            from_heads(grad_bias_qkv),
            chooser[:, None] * (jnp.sum(grad_mid, axis=0) + sums[2])[None],
        ],
        axis=0,
    )
    count = terms.shape[0]

    def sum_small(values, axis, index):
        parts = [
            lax.dynamic_index_in_dim(values, index ^ k, 0, keepdims=False)
            for k in range(values.shape[0])
        ]
        return total([parts[0]] + [permute(parts[k], axis, k) for k in range(1, len(parts))])

    terms = terms.reshape(count, rows, groups, own).transpose(1, 2, 0, 3)
    terms, out_arrived = phase((sum_small(terms, "dp", at_dp), out_arrived))
    summed = sum_small(terms, "seq", at_seq)
    home, grad_normed_attn, out_arrived = phase((home, grad_normed_attn, out_arrived))
    out_proj = total([out_pieces[0], *out_arrived])
    out_down = total([down_terms[0], *down_near])
    if whole_heads and rows % 2 == 0:
        grad_qkv_out = columns_in_place([home], rows)
    else:
        grad_qkv_out = (
            home.reshape(groups, own, 3, deal[0], deal[2])
            .transpose(1, 2, 3, 0, 4)
            .reshape(own, 3 * D)
            .astype(jnp.float32)
        )
    if not whole_heads:
        out_proj = lax.ppermute(out_proj, ("dp", "seq"), owner)
    mlp_last = jnp.concatenate([mlp_half, mlp_last], axis=0)
    mlp_out = total([mlp_pieces[0], *mlp_sums, mlp_last])
    layer_output = (resid_mid + mlp_out).astype(jnp.bfloat16)
    grad_input = grad_mid + norm_backward(
        grad_normed_attn, scaled_attn, inverse_attn, gain_attn
    )[0]
    return (
        layer_output[None],
        grad_input[None],
        summed[7:],
        summed[0],
        summed[1],
        grad_qkv_out,
        summed[4:7],
        out_proj,
        summed[2],
        summed[3],
        out_gate.T,
        out_up.T,
        out_down,
    )


def solution(mesh):
    placed = (
        P("dp", "seq", None),
        P("dp", None),
        P("dp"),
        P(None, ("dp", "seq")),
        P(("dp", "seq")),
        P(("dp", "seq")),
        P(("dp", "seq"), None),
        P(None, ("dp", "seq")),
        P(("dp", "seq"), None),
        P(("dp", "seq")),
        P(("dp", "seq")),
        P(None, ("dp", "seq")),
        P(None, ("dp", "seq")),
        P(("dp", "seq"), None),
        P("dp", "seq", None),
    )
    return jax.shard_map(
        per_device,
        mesh=mesh,
        in_specs=placed,
        out_specs=(
            P("dp", "seq", None),
            P("dp", "seq", None),
            P(None, ("dp", "seq")),
            P(("dp", "seq")),
            P(("dp", "seq")),
            P(("dp", "seq"), None),
            P(None, ("dp", "seq")),
            P(("dp", "seq"), None),
            P(("dp", "seq")),
            P(("dp", "seq")),
            P(None, ("dp", "seq")),
            P(None, ("dp", "seq")),
            P(("dp", "seq"), None),
        ),
        check_vma=False,
    )
```

```python
import jax
import jax.numpy as jnp
from jax import lax
from jax.experimental import pallas as pl
from jax.experimental.pallas import tpu as pltpu
from jax.sharding import PartitionSpec as P

D = 2048
HEADS = 32
HEAD = 64
ROT = 16
LANGS = 7


EPS = 1e-05
BASE = 10000.0
NEG = -1e30


def contract(left, right, left_dim, right_dim):
    return lax.dot_general(
        left, right, (((left_dim,), (right_dim,)), ((), ())), preferred_element_type=jnp.float32
    )


def norm_forward(values, gain, bias):
    average = jnp.mean(values, axis=-1, keepdims=True)
    centered = values - average
    variance = jnp.mean(centered * centered, axis=-1, keepdims=True)
    inverse = lax.rsqrt(variance + EPS)
    scaled = centered * inverse
    return (scaled * gain + bias, scaled, inverse)


def norm_backward(grad_normed, scaled, inverse, gain):
    grad_scaled = grad_normed * gain
    grad_values = inverse * (
        grad_scaled
        - jnp.mean(grad_scaled, axis=-1, keepdims=True)
        - scaled * jnp.mean(grad_scaled * scaled, axis=-1, keepdims=True)
    )
    return (grad_values, jnp.sum(grad_normed * scaled, axis=0), jnp.sum(grad_normed, axis=0))


def row_tables(doc_lengths, length):
    ends = jnp.cumsum(doc_lengths)
    starts = ends - doc_lengths
    places = jnp.arange(length, dtype=jnp.int32)
    segment = jnp.sum((places[:, None] >= ends[None, :]).astype(jnp.int32), axis=1)
    member = segment[:, None] == jnp.arange(ends.shape[0], dtype=jnp.int32)[None, :]
    offsets = jnp.sum(jnp.where(member, starts[None, :], 0), axis=1)
    position = (places - offsets).astype(jnp.float32)
    half_rot = ROT // 2
    freq = BASE ** (-(2.0 * jnp.arange(half_rot, dtype=jnp.float32)) / ROT)
    angles = position[:, None] * freq[None, :]
    return (offsets, jnp.cos(angles), jnp.sin(angles))


def head_lanes(shape, dim, head):
    place = lax.broadcasted_iota(jnp.int32, shape, dim)
    return (place >= head * HEAD) & (place < (head + 1) * HEAD)


def turn(values, tables, direction):
    lanes = values.shape[1]
    cosines, sines_former, sines_latter = tables
    after = pltpu.roll(values, lanes - ROT // 2, 1)
    before = pltpu.roll(values, ROT // 2, 1)
    return values * cosines + direction * (before * sines_latter - after * sines_former)


def allowed_pairs(first_ref, start, block, keys):
    key_at = lax.broadcasted_iota(jnp.int32, (keys, block), 0)
    query_at = start + lax.broadcasted_iota(jnp.int32, (keys, block), 1)
    return (key_at >= first_ref[:, pl.ds(start, block)]) & (key_at <= query_at)


def over_blocks(length, block, step):
    count = length // block
    if count <= 4:
        for i in range(count):
            step(i * block, (i + 1) * block)
    else:

        def body(i, carry):
            step(pl.multiple_of(i * block, block), length)
            return carry

        lax.fori_loop(0, count, body, 0)


def forward_kernel(
    qkv_ref, cos_ref, former_ref, latter_ref, first_ref,
    query_ref, key_ref, context_ref, logsum_ref, value_t,
):
    length, width = query_ref.shape
    lanes = cos_ref.shape[1]
    block = min(256, length)
    tables = (cos_ref[...], former_ref[...], latter_ref[...])
    for group in range(width // lanes):
        part = slice(group * lanes, (group + 1) * lanes)

        def columns(c):
            begin = c * width + group * lanes
            return qkv_ref[:, begin : begin + lanes].astype(jnp.float32)

        query_ref[:, part] = turn(columns(0), tables, 1.0).astype(jnp.bfloat16)
        key_ref[:, part] = turn(columns(1), tables, 1.0).astype(jnp.bfloat16)
        value_t[...] = columns(2).T.astype(jnp.bfloat16)

        def step(start, keys):
            queries = query_ref[pl.ds(start, block), part].astype(jnp.float32) * HEAD ** (-0.5)
            allowed = allowed_pairs(first_ref, start, block, keys)
            found = []
            for head in range(lanes // HEAD):
                own = jnp.where(head_lanes(queries.shape, 1, head), queries, 0.0)
                scores = contract(key_ref[0:keys, part], own.astype(jnp.bfloat16), 1, 1)
                scores = jnp.where(allowed, scores, NEG)
                most = jnp.max(scores, axis=0, keepdims=True)
                weights = jnp.exp(scores - most)
                total = jnp.sum(weights, axis=0, keepdims=True)
                probs = (weights * (1.0 / total)).astype(jnp.bfloat16)
                logsum_ref[
                    pl.ds(group * (lanes // HEAD) + head, 1), pl.ds(start, block)
                ] = most + jnp.log(total)
                context = contract(value_t[:, 0:keys], probs, 1, 0)
                found.append(context[head * HEAD : (head + 1) * HEAD])
            context_ref[pl.ds(start, block), part] = (
                jnp.concatenate(found, axis=0).T.astype(jnp.bfloat16)
            )

        over_blocks(length, block, step)


def backward_kernel(
    query_ref, key_ref, qkv_ref, context_grad_ref, logsum_ref, cos_ref, former_ref, latter_ref,
    first_ref, grad_ref, key_t, grad_query, grad_key, grad_value,
):
    length, width = query_ref.shape
    lanes = cos_ref.shape[1]
    block = min(256, length)
    scale = HEAD ** (-0.5)
    tables = (cos_ref[...], former_ref[...], latter_ref[...])
    for group in range(width // lanes):
        part = slice(group * lanes, (group + 1) * lanes)
        value_part = slice(2 * width + group * lanes, 2 * width + (group + 1) * lanes)
        key_t[...] = key_ref[:, part].astype(jnp.float32).T.astype(jnp.bfloat16)
        grad_key[...] = jnp.zeros_like(grad_key)
        grad_value[...] = jnp.zeros_like(grad_value)

        def step(start, keys):
            queries = query_ref[pl.ds(start, block), part].astype(jnp.float32) * scale
            grads = context_grad_ref[pl.ds(start, block), part].astype(jnp.float32)
            allowed = allowed_pairs(first_ref, start, block, keys)
            found = []
            for head in range(lanes // HEAD):
                mine = head_lanes(queries.shape, 1, head)
                own_query = jnp.where(mine, queries, 0.0).astype(jnp.bfloat16)
                own_grad = jnp.where(mine, grads, 0.0).astype(jnp.bfloat16)
                scores = contract(key_ref[0:keys, part], own_query, 1, 1)
                logsum = logsum_ref[
                    pl.ds(group * (lanes // HEAD) + head, 1), pl.ds(start, block)
                ]
                soft = jnp.exp(jnp.where(allowed, scores, NEG) - logsum)
                grad_soft = contract(qkv_ref[0:keys, value_part], own_grad, 1, 1)
                weighed = soft * grad_soft
                delta = jnp.sum(weighed, axis=0, keepdims=True)
                grad_scores = (weighed - soft * delta).astype(jnp.bfloat16)
                grad_value[0:keys] += contract(soft.astype(jnp.bfloat16), own_grad, 1, 0)
                grad_key[0:keys] += contract(grad_scores, own_query, 1, 0)
                turned = contract(key_t[:, 0:keys], grad_scores, 1, 0)
                found.append(turned[head * HEAD : (head + 1) * HEAD])
            grad_query[pl.ds(start, block), :] = jnp.concatenate(found, axis=0).T * scale

        over_blocks(length, block, step)
        for c, grads in ((0, grad_query), (1, grad_key)):
            begin = c * width + group * lanes
            grad_ref[:, begin : begin + lanes] = turn(grads[...], tables, -1.0).astype(
                jnp.bfloat16
            )
        grad_ref[:, value_part] = grad_value[...].astype(jnp.bfloat16)


def columns_kernel(part_refs, out_ref, deal, width):
    row = 0
    for ref in part_refs:
        groups, rows = ref.shape[0], ref.shape[1]
        for c in range(3):
            for d in range(0, deal, 2):
                for s in range(0, groups, 2):
                    begin = c * deal * HEAD + d * HEAD
                    left = ref[s, :, begin : begin + 2 * HEAD].astype(jnp.float32)
                    right = ref[s + 1, :, begin : begin + 2 * HEAD].astype(jnp.float32)
                    lower = lax.broadcasted_iota(jnp.int32, left.shape, 1) < HEAD
                    out = c * width + d * groups * HEAD + s * HEAD
                    out_ref[row : row + rows, out : out + 2 * HEAD] = jnp.where(
                        lower, left, pltpu.roll(right, HEAD, 1)
                    )
                    out = out + groups * HEAD
                    out_ref[row : row + rows, out : out + 2 * HEAD] = jnp.where(
                        lower, pltpu.roll(left, HEAD, 1), right
                    )
        row += rows


def columns_in_place(parts, deal):
    rows = sum(part.shape[1] for part in parts)
    width = parts[0].shape[0] * deal * HEAD

    def kernel(*refs):
        columns_kernel(refs[:-1], refs[-1], deal, width)

    return pl.pallas_call(
        kernel,
        out_shape=jax.ShapeDtypeStruct((rows, 3 * width), jnp.float32),
        compiler_params=pltpu.CompilerParams(vmem_limit_bytes=VMEM_BYTES),
        name="columns_in_place",
    )(*parts)


def deal_kernel(weight_ref, riders_ref, out_ref, deal):
    groups = out_ref.shape[0]
    rows, width = weight_ref.shape[0], weight_ref.shape[1] // 3
    for c in range(3):
        for d in range(0, deal, 2):
            for s in range(0, groups, 2):
                begin = c * width + d * groups * HEAD + s * HEAD
                upper = weight_ref[:, begin : begin + 2 * HEAD].astype(jnp.float32)
                begin = begin + groups * HEAD
                after = weight_ref[:, begin : begin + 2 * HEAD].astype(jnp.float32)
                lower = lax.broadcasted_iota(jnp.int32, upper.shape, 1) < HEAD
                out = c * deal * HEAD + d * HEAD
                out_ref[s, 0:rows, out : out + 2 * HEAD] = jnp.where(
                    lower, upper, pltpu.roll(after, HEAD, 1)
                ).astype(jnp.bfloat16)
                out_ref[s + 1, 0:rows, out : out + 2 * HEAD] = jnp.where(
                    lower, pltpu.roll(upper, HEAD, 1), after
                ).astype(jnp.bfloat16)
    for s in range(groups):
        out_ref[s, rows:, :] = riders_ref[...]


def deal_columns(weight, riders, groups, deal):
    def kernel(*refs):
        deal_kernel(*refs, deal)

    return pl.pallas_call(
        kernel,
        out_shape=jax.ShapeDtypeStruct(
            (groups, weight.shape[0] + riders.shape[0], riders.shape[1]), jnp.bfloat16
        ),
        compiler_params=pltpu.CompilerParams(vmem_limit_bytes=VMEM_BYTES),
        name="deal_columns",
    )(weight, riders)


SMALL_COST = pl.CostEstimate(flops=1, bytes_accessed=1, transcendentals=1)


def norm_sums_kernel(values_ref, terms_ref, lang_ref, gain_ref, out_ref):
    @pl.when(pl.program_id(0) == 0)
    def clear():
        out_ref[...] = jnp.zeros_like(out_ref)

    values = values_ref[...].astype(jnp.float32) + lang_ref[...]
    terms = terms_ref[...].astype(jnp.float32)
    unused, scaled, inverse = norm_forward(values, 1.0, 0.0)
    grad_values, gain_sum, bias_sum = norm_backward(terms, scaled, inverse, gain_ref[...])
    out_ref[0:1] += gain_sum[None]
    out_ref[1:2] += bias_sum[None]
    out_ref[2:3] += jnp.sum(grad_values, axis=0, keepdims=True)


def norm_sums(values, terms, lang_row, gain):
    length, width = values.shape
    block = min(256, length)
    rows = pl.BlockSpec((block, width), lambda i: (i, 0))
    whole = pl.BlockSpec((1, width), lambda i: (0, 0))
    return pl.pallas_call(
        norm_sums_kernel,
        grid=(length // block,),
        in_specs=[rows, rows, whole, whole],
        out_specs=pl.BlockSpec((8, width), lambda i: (0, 0)),
        out_shape=jax.ShapeDtypeStruct((8, width), jnp.float32),
        compiler_params=pltpu.CompilerParams(vmem_limit_bytes=VMEM_BYTES),
        cost_estimate=SMALL_COST,
        name="norm_sums",
    )(values, terms, lang_row, gain[None])


def rotation_tables(cosines, sines, lanes):
    length = cosines.shape[0]
    rest = jnp.ones((length, HEAD - ROT), jnp.float32)
    none = jnp.zeros_like(sines)
    heads = lanes // HEAD
    return (
        jnp.tile(jnp.concatenate([cosines, cosines, rest], axis=1), (1, heads)),
        jnp.tile(jnp.concatenate([sines, none, 0.0 * rest], axis=1), (1, heads)),
        jnp.tile(jnp.concatenate([none, sines, 0.0 * rest], axis=1), (1, heads)),
    )


VMEM_BYTES = 48 * 1024 * 1024


def attention_forward(projected, tables, first):
    length, width = projected.shape[0], projected.shape[1] // 3
    lanes = tables[0].shape[1]
    rows = jax.ShapeDtypeStruct((length, width), jnp.bfloat16)
    return pl.pallas_call(
        forward_kernel,
        out_shape=(
            rows,
            rows,
            rows,
            jax.ShapeDtypeStruct((width // HEAD, length), jnp.float32),
        ),
        scratch_shapes=[pltpu.VMEM((lanes, length), jnp.bfloat16)],
        compiler_params=pltpu.CompilerParams(vmem_limit_bytes=VMEM_BYTES),
        cost_estimate=SMALL_COST,
        name="attention_forward",
    )(projected, *tables, first)


def attention_backward(queries, key_heads, projected, grad_context, logsum, tables, first):
    length, width = queries.shape
    lanes = tables[0].shape[1]
    return pl.pallas_call(
        backward_kernel,
        out_shape=jax.ShapeDtypeStruct((length, 3 * width), jnp.bfloat16),
        scratch_shapes=[
            pltpu.VMEM((lanes, length), jnp.bfloat16),
            pltpu.VMEM((length, lanes), jnp.float32),
            pltpu.VMEM((length, lanes), jnp.float32),
            pltpu.VMEM((length, lanes), jnp.float32),
        ],
        compiler_params=pltpu.CompilerParams(vmem_limit_bytes=VMEM_BYTES),
        cost_estimate=SMALL_COST,
        name="attention_backward",
    )(queries, key_heads, projected, grad_context, logsum, *tables, first)


def gate_backward(gate_values, up_values, grad_hidden):
    sigmoid_gate = jax.nn.sigmoid(gate_values)
    silu_gate = gate_values * sigmoid_gate
    grad_gate = (
        grad_hidden * up_values * sigmoid_gate * (1.0 + gate_values * (1.0 - sigmoid_gate))
    ).astype(jnp.bfloat16)
    grad_up = (grad_hidden * silu_gate).astype(jnp.bfloat16)
    return (grad_gate, grad_up)


def permute(value, axis, offset):
    size = lax.axis_size(axis)
    return lax.ppermute(value, axis, [(i, i ^ offset) for i in range(size)])


def gather_dp(piece):
    return [piece] + [permute(piece, "dp", k) for k in range(1, lax.axis_size("dp"))]


def scatter_dp(pieces):
    return total([pieces[0]] + [permute(pieces[k], "dp", k) for k in range(1, len(pieces))])


def near_dp(piece):
    return [piece, permute(piece, "dp", 1), permute(piece, "dp", 2)]


def corner_dp(pieces):
    middle = pieces[0].shape[0] // 2
    return jnp.concatenate(
        [permute(pieces[2][:middle], "dp", 1), permute(pieces[1][middle:], "dp", 2)], axis=0
    )


def send_corner(pieces):
    middle = pieces[0].shape[0] // 2
    return (permute(pieces[3][:middle], "dp", 2), permute(pieces[3][middle:], "dp", 1))


def add_corner(pieces, corner):
    middle = pieces[0].shape[0] // 2
    first = total([pieces[1][:middle], corner[0]]).astype(jnp.bfloat16)
    second = total([pieces[2][middle:], corner[1]]).astype(jnp.bfloat16)
    return [
        jnp.concatenate([first, pieces[1][middle:]], axis=0),
        jnp.concatenate([pieces[2][:middle], second], axis=0),
    ]


def send_near(pieces, corner):
    first, second = add_corner(pieces, corner)
    return [permute(first, "dp", 1), permute(second, "dp", 2)]


def total(parts):
    result = parts[0].astype(jnp.float32)
    for piece in parts[1:]:
        result = result + piece.astype(jnp.float32)
    return result


def gather_seq(piece):
    return lax.all_gather(piece, "seq", axis=0, tiled=True)


def scatter_seq(terms):
    return lax.psum_scatter(
        terms.astype(jnp.bfloat16), "seq", scatter_dimension=0, tiled=True
    ).astype(jnp.float32)


def after(value, *others):
    return lax.optimization_barrier((value,) + others)[0]


def place(pieces, index):
    block = pieces[0].shape[0]
    result = jnp.zeros((block * len(pieces),) + pieces[0].shape[1:], pieces[0].dtype)
    for k, piece in enumerate(pieces):
        result = lax.dynamic_update_slice_in_dim(result, piece, (index ^ k) * block, 0)
    return result


def per_device(
    layer_input,
    doc_lengths,
    language,
    lang_table,
    attn_norm_gain,
    attn_norm_bias,
    qkv_weight,
    qkv_bias,
    out_weight,
    mlp_norm_gain,
    mlp_norm_bias,
    gate_weight,
    up_weight,
    down_weight,
    cotangent,
):
    tokens = layer_input.shape[1]
    groups = lax.axis_size("seq")
    rows = lax.axis_size("dp")
    devices = rows * groups
    at_dp = lax.axis_index("dp")
    at_seq = lax.axis_index("seq")
    length = tokens * groups
    heads_here = HEADS // groups
    local_width = heads_here * HEAD
    own = D // devices
    whole_heads = own % HEAD == 0
    deal = (rows, groups, own) if whole_heads else (1, groups, local_width)
    at_deal = (0, 0, at_seq, 0)
    owner = [(i, (i % groups) * rows + i // groups) for i in range(devices)]
    back = [(b, a) for a, b in owner]

    def to_heads(values):
        count = values.shape[0]
        return lax.dynamic_slice(
            values.reshape((count,) + deal), at_deal, (count, deal[0], 1, deal[2])
        ).reshape(count, local_width)

    def from_heads(values):
        count = values.shape[0]
        return lax.dynamic_update_slice(
            jnp.zeros((count,) + deal, values.dtype),
            values.reshape(count, deal[0], 1, deal[2]),
            at_deal,
        ).reshape(count, D)

    phase = lax.optimization_barrier
    grad_out = cotangent[0]

    def dp_terms(terms):
        block = terms.shape[0] // rows
        return [
            lax.dynamic_slice_in_dim(terms, (at_dp ^ k) * block, block, 0) for k in range(rows)
        ]

    small = jnp.concatenate(
        [
            lang_table,
            attn_norm_gain[None],
            attn_norm_bias[None],
            mlp_norm_gain[None],
            mlp_norm_bias[None],
            qkv_bias,
        ],
        axis=0,
    )
    ride = 16
    riders = jnp.zeros((ride * 3 * local_width,), jnp.bfloat16)
    riders = lax.dynamic_update_slice(riders, small.reshape(-1), (0,))
    riders = riders.reshape(ride, 3 * local_width)
    if whole_heads and rows % 2 == 0:
        dealt = deal_columns(qkv_weight, riders, groups, rows)
    else:
        dealt = jnp.concatenate(
            [
                qkv_weight.reshape((own, 3) + deal)
                .transpose(3, 0, 1, 2, 4)
                .reshape(groups, own, 3 * local_width),
                jnp.broadcast_to(riders[None], (groups,) + riders.shape),
            ],
            axis=1,
        )
    part = lax.all_to_all(dealt, "seq", split_axis=0, concat_axis=0, tiled=True)
    chips = groups // 2
    input_all = gather_seq(layer_input[0])
    spread = place(gather_dp(part[:, own:].reshape(groups, -1)), at_dp)
    qkv_pieces = near_dp(part[:, :own].reshape(groups * own, 3 * local_width))
    input_all, spread, grad_far = phase((input_all, spread, grad_out))
    grad_pieces = [permute(grad_far, "seq", 2 * k) for k in range(2, chips)]
    spread = spread[:, : small.size].reshape((devices,) + small.shape)
    table = jnp.swapaxes(spread, 0, 1).reshape(small.shape[0], D).astype(jnp.float32)
    gain_attn = table[LANGS]
    bias_attn = table[LANGS + 1]
    gain_mlp = table[LANGS + 2]
    bias_mlp = table[LANGS + 3]
    bias_qkv = to_heads(table[LANGS + 4 : LANGS + 7]).reshape(3 * local_width)
    chooser = (jnp.arange(LANGS, dtype=jnp.int32) == language[0]).astype(jnp.float32)
    lang_row = jnp.sum(chooser[:, None] * table[:LANGS], axis=0)[None, :]
    offsets, cosines, sines = row_tables(doc_lengths[0], length)
    tables = rotation_tables(cosines, sines, min(128, local_width))
    first = offsets[None, :]
    resid_in = layer_input[0].astype(jnp.float32) + lang_row
    unused, scaled_attn, inverse_attn = norm_forward(resid_in, gain_attn, bias_attn)
    normed_all = norm_forward(input_all.astype(jnp.float32) + lang_row, gain_attn, bias_attn)[
        0
    ].astype(jnp.bfloat16)
    qkv_pieces, tables, first, resid_in = phase((qkv_pieces, tables, first, resid_in))
    head_qkv = place(qkv_pieces + [corner_dp(qkv_pieces)], at_dp)
    head_qkv, normed_all, out_rows = phase((head_qkv, normed_all, out_weight))
    if not whole_heads:
        out_rows = lax.ppermute(out_rows, ("dp", "seq"), back)
    head_out = place(gather_dp(out_rows), at_dp)
    projected = (
        jnp.dot(normed_all, head_qkv, preferred_element_type=jnp.float32) + bias_qkv
    ).astype(jnp.bfloat16)
    rot_query, rot_key, context_all, logsum = attention_forward(projected, tables, first)
    out_terms = jnp.dot(context_all, head_out, preferred_element_type=jnp.float32).astype(
        jnp.bfloat16
    )
    out_terms, grad_pieces, gate_rows, grad_near = phase(
        (out_terms, grad_pieces, gate_weight.T, grad_out)
    )
    attn_out = scatter_seq(out_terms)
    gate_pieces = near_dp(gate_rows)
    near = permute(grad_near, "seq", 2)
    gate_pieces, near, up_rows = phase((gate_pieces, near, up_weight.T))
    grad_pieces = [grad_out, near, *grad_pieces]
    gate_pieces = gate_pieces + [corner_dp(gate_pieces)]
    up_pieces = near_dp(up_rows)
    mates = permute(jnp.concatenate(grad_pieces, axis=0), "seq", 1)
    mates = jnp.split(mates, chips, axis=0)
    grad_all = place([piece for pair in zip(grad_pieces, mates) for piece in pair], at_seq)
    attn_out, gate_pieces, up_pieces, grad_all, down_rows = phase(
        (attn_out, gate_pieces, up_pieces, grad_all, down_weight)
    )
    resid_mid = resid_in + attn_out
    normed_mlp, scaled_mlp, inverse_mlp = norm_forward(resid_mid, gain_mlp, bias_mlp)
    rows_all = gather_seq(normed_mlp.astype(jnp.bfloat16))
    up_pieces = up_pieces + [corner_dp(up_pieces)]
    down_pieces = near_dp(down_rows)
    down_pieces, up_pieces = phase((down_pieces, up_pieces))
    cols_down = jnp.concatenate(down_pieces + [corner_dp(down_pieces)], axis=0)
    cols_gate = jnp.concatenate(gate_pieces, axis=0)
    cols_up = jnp.concatenate(up_pieces, axis=0)
    grad_hidden = contract(grad_all, cols_down, 1, 1)
    rows_all, cols_down, cols_gate, cols_up, grad_hidden = phase(
        (rows_all, cols_down, cols_gate, cols_up, grad_hidden)
    )
    gate_values = contract(rows_all, cols_gate, 1, 1)
    up_values = contract(rows_all, cols_up, 1, 1)
    hidden = (jax.nn.silu(gate_values) * up_values).astype(jnp.bfloat16)
    grad_gate, grad_up = gate_backward(gate_values, up_values, grad_hidden)
    grad_rows = (
        contract(grad_gate, cols_gate, 1, 0) + contract(grad_up, cols_up, 1, 0)
    ).astype(jnp.bfloat16)
    grad_rows, grad_gate, grad_up, hidden = phase((grad_rows, grad_gate, grad_up, hidden))
    grad_normed_mlp = scatter_seq(grad_rows)
    gate_terms = jnp.split(
        contract(grad_gate, rows_all, 0, 0).astype(jnp.bfloat16), rows, axis=0
    )
    gate_corner = send_corner(gate_terms)
    mlp_terms = contract(hidden, cols_down, 1, 0).astype(jnp.bfloat16)
    up_terms = contract(grad_up, rows_all, 0, 0).astype(jnp.bfloat16)
    gate_corner, gate_terms, mlp_terms, up_terms = phase(
        (gate_corner, gate_terms, mlp_terms, up_terms)
    )
    gate_near = send_near(gate_terms, gate_corner)
    down_terms = contract(hidden, grad_all, 0, 0).astype(jnp.bfloat16)
    grad_normed_mlp, gate_near, up_terms, mlp_terms, down_terms = phase(
        (grad_normed_mlp, gate_near, up_terms, mlp_terms, down_terms)
    )
    grad_mid_norm, grad_gain_mlp, grad_bias_mlp = norm_backward(
        grad_normed_mlp, scaled_mlp, inverse_mlp, gain_mlp
    )
    grad_mid = grad_out.astype(jnp.float32) + grad_mid_norm
    branch_all = gather_seq(grad_mid.astype(jnp.bfloat16))
    up_terms = jnp.split(up_terms, rows, axis=0)
    down_terms = jnp.split(down_terms, rows, axis=0)
    up_corner = send_corner(up_terms)
    up_corner, up_terms, down_terms = phase((up_corner, up_terms, down_terms))
    up_near = send_near(up_terms, up_corner)
    down_corner = send_corner(down_terms)
    down_terms = down_terms[:1] + add_corner(down_terms, down_corner)
    branch_all, up_near, mlp_terms, down_terms = phase(
        (branch_all, up_near, mlp_terms, down_terms)
    )
    mlp_out = scatter_seq(mlp_terms)
    down_near = [permute(down_terms[1], "dp", 1), permute(down_terms[2], "dp", 2)]
    grad_heads = contract(branch_all, head_out, 1, 1).astype(jnp.bfloat16)
    grad_stack = attention_backward(
        rot_query, rot_key, projected, grad_heads, logsum, tables, first
    )
    grad_stack, down_near = phase((grad_stack, down_near))
    slice_terms = contract(normed_all, grad_stack, 0, 0).astype(jnp.bfloat16)
    slice_pieces = dp_terms(slice_terms)
    grad_stack, slice_pieces = phase((grad_stack, slice_pieces))
    slice_near = [permute(slice_pieces[k], "dp", k) for k in range(1, rows - 1)]
    attn_terms = contract(grad_stack, head_qkv, 1, 1).astype(jnp.bfloat16)
    sums = norm_sums(input_all, attn_terms, lang_row, gain_attn)
    grad_bias_qkv = jnp.sum(grad_stack.astype(jnp.float32), axis=0).reshape(3, local_width)
    terms = jnp.concatenate(
        [
            sums[:2],
            grad_gain_mlp[None],
            grad_bias_mlp[None],
            from_heads(grad_bias_qkv),
            chooser[:, None] * (jnp.sum(grad_mid, axis=0) + sums[2])[None],
        ],
        axis=0,
    )
    count = terms.shape[0]

    def small_parts(values, index):
        return [
            lax.dynamic_index_in_dim(values, index ^ k, 0, keepdims=False)
            for k in range(values.shape[0])
        ]

    def small_sum(parts, axis):
        return total([parts[0]] + [permute(parts[k], axis, k) for k in range(1, len(parts))])

    terms = small_parts(terms.reshape(count, rows, groups, own).transpose(1, 2, 0, 3), at_dp)
    attn_terms, terms, slice_near, slice_pieces, branch_all, up_near, gate_near = phase(
        (attn_terms, terms, slice_near, slice_pieces, branch_all, up_near, gate_near)
    )
    grad_normed_attn = scatter_seq(attn_terms)
    slice_far = permute(slice_pieces[-1], "dp", rows - 1)
    terms = small_parts(small_sum(terms, "dp"), at_seq)
    out_pieces = dp_terms(contract(context_all, branch_all, 0, 0).astype(jnp.bfloat16))
    terms, slice_far, mlp_out, out_pieces, down_near, up_near, gate_near = phase(
        (terms, slice_far, mlp_out, out_pieces, down_near, up_near, gate_near)
    )
    home = (
        total([slice_pieces[0], *slice_near, slice_far])
        .astype(jnp.bfloat16)
        .reshape(groups, own, 3 * local_width)
    )
    home, terms, out_pieces, down_near, up_near, gate_near = phase(
        (home, terms, out_pieces, down_near, up_near, gate_near)
    )
    home = lax.all_to_all(home, "seq", split_axis=0, concat_axis=0, tiled=True)
    out_arrived = [permute(out_pieces[k], "dp", k) for k in range(1, rows)]
    summed = small_sum(terms, "seq")
    home, out_arrived, summed = phase((home, out_arrived, summed))
    out_proj = total([out_pieces[0], *out_arrived])
    out_gate = total([gate_terms[0], *gate_near])
    out_up = total([up_terms[0], *up_near])
    out_down = total([down_terms[0], *down_near])
    if whole_heads and rows % 2 == 0:
        grad_qkv_out = columns_in_place([home], rows)
    else:
        grad_qkv_out = (
            home.reshape(groups, own, 3, deal[0], deal[2])
            .transpose(1, 2, 3, 0, 4)
            .reshape(own, 3 * D)
            .astype(jnp.float32)
        )
    if not whole_heads:
        out_proj = lax.ppermute(out_proj, ("dp", "seq"), owner)
    layer_output = (resid_mid + mlp_out).astype(jnp.bfloat16)
    grad_normed_attn, grad_qkv_out, out_proj, out_gate, out_up, out_down, layer_output = phase(
        (grad_normed_attn, grad_qkv_out, out_proj, out_gate, out_up, out_down, layer_output)
    )
    grad_input = grad_mid + norm_backward(
        grad_normed_attn, scaled_attn, inverse_attn, gain_attn
    )[0]
    return (
        layer_output[None],
        grad_input[None],
        summed[7:],
        summed[0],
        summed[1],
        grad_qkv_out,
        summed[4:7],
        out_proj,
        summed[2],
        summed[3],
        out_gate.T,
        out_up.T,
        out_down,
    )


def solution(mesh):
    placed = (
        P("dp", "seq", None),
        P("dp", None),
        P("dp"),
        P(None, ("dp", "seq")),
        P(("dp", "seq")),
        P(("dp", "seq")),
        P(("dp", "seq"), None),
        P(None, ("dp", "seq")),
        P(("dp", "seq"), None),
        P(("dp", "seq")),
        P(("dp", "seq")),
        P(None, ("dp", "seq")),
        P(None, ("dp", "seq")),
        P(("dp", "seq"), None),
        P("dp", "seq", None),
    )
    return jax.shard_map(
        per_device,
        mesh=mesh,
        in_specs=placed,
        out_specs=(
            P("dp", "seq", None),
            P("dp", "seq", None),
            P(None, ("dp", "seq")),
            P(("dp", "seq")),
            P(("dp", "seq")),
            P(("dp", "seq"), None),
            P(None, ("dp", "seq")),
            P(("dp", "seq"), None),
            P(("dp", "seq")),
            P(("dp", "seq")),
            P(None, ("dp", "seq")),
            P(None, ("dp", "seq")),
            P(("dp", "seq"), None),
        ),
        check_vma=False,
    )
```

```python
import jax
import jax.numpy as jnp
from jax import lax
from jax.experimental import pallas as pl
from jax.experimental.pallas import tpu as pltpu
from jax.sharding import PartitionSpec as P

D = 2048
HEADS = 32
HEAD = 64
ROT = 16
LANGS = 7


EPS = 1e-05
BASE = 10000.0
NEG = -1e30


def contract(left, right, left_dim, right_dim):
    return lax.dot_general(
        left, right, (((left_dim,), (right_dim,)), ((), ())), preferred_element_type=jnp.float32
    )


def norm_forward(values, gain, bias):
    average = jnp.mean(values, axis=-1, keepdims=True)
    centered = values - average
    variance = jnp.mean(centered * centered, axis=-1, keepdims=True)
    inverse = lax.rsqrt(variance + EPS)
    scaled = centered * inverse
    return (scaled * gain + bias, scaled, inverse)


def norm_backward(grad_normed, scaled, inverse, gain):
    grad_scaled = grad_normed * gain
    grad_values = inverse * (
        grad_scaled
        - jnp.mean(grad_scaled, axis=-1, keepdims=True)
        - scaled * jnp.mean(grad_scaled * scaled, axis=-1, keepdims=True)
    )
    return (grad_values, jnp.sum(grad_normed * scaled, axis=0), jnp.sum(grad_normed, axis=0))


def row_tables(doc_lengths, length):
    ends = jnp.cumsum(doc_lengths)
    starts = ends - doc_lengths
    places = jnp.arange(length, dtype=jnp.int32)
    segment = jnp.sum((places[:, None] >= ends[None, :]).astype(jnp.int32), axis=1)
    member = segment[:, None] == jnp.arange(ends.shape[0], dtype=jnp.int32)[None, :]
    offsets = jnp.sum(jnp.where(member, starts[None, :], 0), axis=1)
    position = (places - offsets).astype(jnp.float32)
    half_rot = ROT // 2
    freq = BASE ** (-(2.0 * jnp.arange(half_rot, dtype=jnp.float32)) / ROT)
    angles = position[:, None] * freq[None, :]
    return (offsets, jnp.cos(angles), jnp.sin(angles))


def head_lanes(shape, dim, head):
    place = lax.broadcasted_iota(jnp.int32, shape, dim)
    return (place >= head * HEAD) & (place < (head + 1) * HEAD)


def turn(values, tables, direction):
    lanes = values.shape[1]
    cosines, sines_former, sines_latter = tables
    after = pltpu.roll(values, lanes - ROT // 2, 1)
    before = pltpu.roll(values, ROT // 2, 1)
    return values * cosines + direction * (before * sines_latter - after * sines_former)


def allowed_pairs(first_ref, start, block, keys):
    key_at = lax.broadcasted_iota(jnp.int32, (keys, block), 0)
    query_at = start + lax.broadcasted_iota(jnp.int32, (keys, block), 1)
    return (key_at >= first_ref[:, pl.ds(start, block)]) & (key_at <= query_at)


def over_blocks(length, block, step):
    count = length // block
    if count <= 4:
        for i in range(count):
            step(i * block, (i + 1) * block)
    else:

        def body(i, carry):
            step(pl.multiple_of(i * block, block), length)
            return carry

        lax.fori_loop(0, count, body, 0)


def forward_kernel(
    qkv_ref, cos_ref, former_ref, latter_ref, first_ref,
    query_ref, key_ref, context_ref, logsum_ref, value_t,
):
    length, width = query_ref.shape
    lanes = cos_ref.shape[1]
    block = min(256, length)
    tables = (cos_ref[...], former_ref[...], latter_ref[...])
    for group in range(width // lanes):
        part = slice(group * lanes, (group + 1) * lanes)

        def columns(c):
            begin = c * width + group * lanes
            return qkv_ref[:, begin : begin + lanes].astype(jnp.float32)

        query_ref[:, part] = turn(columns(0), tables, 1.0).astype(jnp.bfloat16)
        key_ref[:, part] = turn(columns(1), tables, 1.0).astype(jnp.bfloat16)
        value_t[...] = columns(2).T.astype(jnp.bfloat16)

        def step(start, keys):
            queries = query_ref[pl.ds(start, block), part].astype(jnp.float32) * HEAD ** (-0.5)
            allowed = allowed_pairs(first_ref, start, block, keys)
            found = []
            for head in range(lanes // HEAD):
                own = jnp.where(head_lanes(queries.shape, 1, head), queries, 0.0)
                scores = contract(key_ref[0:keys, part], own.astype(jnp.bfloat16), 1, 1)
                scores = jnp.where(allowed, scores, NEG)
                most = jnp.max(scores, axis=0, keepdims=True)
                weights = jnp.exp(scores - most)
                total = jnp.sum(weights, axis=0, keepdims=True)
                probs = (weights * (1.0 / total)).astype(jnp.bfloat16)
                logsum_ref[
                    pl.ds(group * (lanes // HEAD) + head, 1), pl.ds(start, block)
                ] = most + jnp.log(total)
                context = contract(value_t[:, 0:keys], probs, 1, 0)
                found.append(context[head * HEAD : (head + 1) * HEAD])
            context_ref[pl.ds(start, block), part] = (
                jnp.concatenate(found, axis=0).T.astype(jnp.bfloat16)
            )

        over_blocks(length, block, step)


def backward_kernel(
    query_ref, key_ref, qkv_ref, context_grad_ref, logsum_ref, cos_ref, former_ref, latter_ref,
    first_ref, grad_ref, key_t, grad_query, grad_key, grad_value,
):
    length, width = query_ref.shape
    lanes = cos_ref.shape[1]
    block = min(256, length)
    scale = HEAD ** (-0.5)
    tables = (cos_ref[...], former_ref[...], latter_ref[...])
    for group in range(width // lanes):
        part = slice(group * lanes, (group + 1) * lanes)
        value_part = slice(2 * width + group * lanes, 2 * width + (group + 1) * lanes)
        key_t[...] = key_ref[:, part].astype(jnp.float32).T.astype(jnp.bfloat16)
        grad_key[...] = jnp.zeros_like(grad_key)
        grad_value[...] = jnp.zeros_like(grad_value)

        def step(start, keys):
            queries = query_ref[pl.ds(start, block), part].astype(jnp.float32) * scale
            grads = context_grad_ref[pl.ds(start, block), part].astype(jnp.float32)
            allowed = allowed_pairs(first_ref, start, block, keys)
            found = []
            for head in range(lanes // HEAD):
                mine = head_lanes(queries.shape, 1, head)
                own_query = jnp.where(mine, queries, 0.0).astype(jnp.bfloat16)
                own_grad = jnp.where(mine, grads, 0.0).astype(jnp.bfloat16)
                scores = contract(key_ref[0:keys, part], own_query, 1, 1)
                logsum = logsum_ref[
                    pl.ds(group * (lanes // HEAD) + head, 1), pl.ds(start, block)
                ]
                soft = jnp.exp(jnp.where(allowed, scores, NEG) - logsum)
                grad_soft = contract(qkv_ref[0:keys, value_part], own_grad, 1, 1)
                weighed = soft * grad_soft
                delta = jnp.sum(weighed, axis=0, keepdims=True)
                grad_scores = (weighed - soft * delta).astype(jnp.bfloat16)
                grad_value[0:keys] += contract(soft.astype(jnp.bfloat16), own_grad, 1, 0)
                grad_key[0:keys] += contract(grad_scores, own_query, 1, 0)
                turned = contract(key_t[:, 0:keys], grad_scores, 1, 0)
                found.append(turned[head * HEAD : (head + 1) * HEAD])
            grad_query[pl.ds(start, block), :] = jnp.concatenate(found, axis=0).T * scale

        over_blocks(length, block, step)
        for c, grads in ((0, grad_query), (1, grad_key)):
            begin = c * width + group * lanes
            grad_ref[:, begin : begin + lanes] = turn(grads[...], tables, -1.0).astype(
                jnp.bfloat16
            )
        grad_ref[:, value_part] = grad_value[...].astype(jnp.bfloat16)


def columns_kernel(part_refs, out_ref, deal, width):
    row = 0
    for ref in part_refs:
        groups, rows = ref.shape[0], ref.shape[1]
        for c in range(3):
            for d in range(0, deal, 2):
                for s in range(0, groups, 2):
                    begin = c * deal * HEAD + d * HEAD
                    left = ref[s, :, begin : begin + 2 * HEAD].astype(jnp.float32)
                    right = ref[s + 1, :, begin : begin + 2 * HEAD].astype(jnp.float32)
                    lower = lax.broadcasted_iota(jnp.int32, left.shape, 1) < HEAD
                    out = c * width + d * groups * HEAD + s * HEAD
                    out_ref[row : row + rows, out : out + 2 * HEAD] = jnp.where(
                        lower, left, pltpu.roll(right, HEAD, 1)
                    )
                    out = out + groups * HEAD
                    out_ref[row : row + rows, out : out + 2 * HEAD] = jnp.where(
                        lower, pltpu.roll(left, HEAD, 1), right
                    )
        row += rows


def columns_in_place(parts, deal):
    rows = sum(part.shape[1] for part in parts)
    width = parts[0].shape[0] * deal * HEAD

    def kernel(*refs):
        columns_kernel(refs[:-1], refs[-1], deal, width)

    return pl.pallas_call(
        kernel,
        out_shape=jax.ShapeDtypeStruct((rows, 3 * width), jnp.float32),
        compiler_params=pltpu.CompilerParams(vmem_limit_bytes=VMEM_BYTES),
        name="columns_in_place",
    )(*parts)


def deal_kernel(weight_ref, riders_ref, out_ref, deal):
    groups = out_ref.shape[0]
    rows, width = weight_ref.shape[0], weight_ref.shape[1] // 3
    for c in range(3):
        for d in range(0, deal, 2):
            for s in range(0, groups, 2):
                begin = c * width + d * groups * HEAD + s * HEAD
                upper = weight_ref[:, begin : begin + 2 * HEAD].astype(jnp.float32)
                begin = begin + groups * HEAD
                after = weight_ref[:, begin : begin + 2 * HEAD].astype(jnp.float32)
                lower = lax.broadcasted_iota(jnp.int32, upper.shape, 1) < HEAD
                out = c * deal * HEAD + d * HEAD
                out_ref[s, 0:rows, out : out + 2 * HEAD] = jnp.where(
                    lower, upper, pltpu.roll(after, HEAD, 1)
                ).astype(jnp.bfloat16)
                out_ref[s + 1, 0:rows, out : out + 2 * HEAD] = jnp.where(
                    lower, pltpu.roll(upper, HEAD, 1), after
                ).astype(jnp.bfloat16)
    for s in range(groups):
        out_ref[s, rows:, :] = riders_ref[...]


def deal_columns(weight, riders, groups, deal):
    def kernel(*refs):
        deal_kernel(*refs, deal)

    return pl.pallas_call(
        kernel,
        out_shape=jax.ShapeDtypeStruct(
            (groups, weight.shape[0] + riders.shape[0], riders.shape[1]), jnp.bfloat16
        ),
        compiler_params=pltpu.CompilerParams(vmem_limit_bytes=VMEM_BYTES),
        name="deal_columns",
    )(weight, riders)


SMALL_COST = pl.CostEstimate(flops=1, bytes_accessed=1, transcendentals=1)


def norm_sums_kernel(values_ref, terms_ref, lang_ref, gain_ref, out_ref):
    @pl.when(pl.program_id(0) == 0)
    def clear():
        out_ref[...] = jnp.zeros_like(out_ref)

    values = values_ref[...].astype(jnp.float32) + lang_ref[...]
    terms = terms_ref[...].astype(jnp.float32)
    unused, scaled, inverse = norm_forward(values, 1.0, 0.0)
    grad_values, gain_sum, bias_sum = norm_backward(terms, scaled, inverse, gain_ref[...])
    out_ref[0:1] += gain_sum[None]
    out_ref[1:2] += bias_sum[None]
    out_ref[2:3] += jnp.sum(grad_values, axis=0, keepdims=True)


def norm_sums(values, terms, lang_row, gain):
    length, width = values.shape
    block = min(256, length)
    rows = pl.BlockSpec((block, width), lambda i: (i, 0))
    whole = pl.BlockSpec((1, width), lambda i: (0, 0))
    return pl.pallas_call(
        norm_sums_kernel,
        grid=(length // block,),
        in_specs=[rows, rows, whole, whole],
        out_specs=pl.BlockSpec((8, width), lambda i: (0, 0)),
        out_shape=jax.ShapeDtypeStruct((8, width), jnp.float32),
        compiler_params=pltpu.CompilerParams(vmem_limit_bytes=VMEM_BYTES),
        cost_estimate=SMALL_COST,
        name="norm_sums",
    )(values, terms, lang_row, gain[None])


def rotation_tables(cosines, sines, lanes):
    length = cosines.shape[0]
    rest = jnp.ones((length, HEAD - ROT), jnp.float32)
    none = jnp.zeros_like(sines)
    heads = lanes // HEAD
    return (
        jnp.tile(jnp.concatenate([cosines, cosines, rest], axis=1), (1, heads)),
        jnp.tile(jnp.concatenate([sines, none, 0.0 * rest], axis=1), (1, heads)),
        jnp.tile(jnp.concatenate([none, sines, 0.0 * rest], axis=1), (1, heads)),
    )


VMEM_BYTES = 48 * 1024 * 1024


def attention_forward(projected, tables, first):
    length, width = projected.shape[0], projected.shape[1] // 3
    lanes = tables[0].shape[1]
    rows = jax.ShapeDtypeStruct((length, width), jnp.bfloat16)
    return pl.pallas_call(
        forward_kernel,
        out_shape=(
            rows,
            rows,
            rows,
            jax.ShapeDtypeStruct((width // HEAD, length), jnp.float32),
        ),
        scratch_shapes=[pltpu.VMEM((lanes, length), jnp.bfloat16)],
        compiler_params=pltpu.CompilerParams(vmem_limit_bytes=VMEM_BYTES),
        cost_estimate=SMALL_COST,
        name="attention_forward",
    )(projected, *tables, first)


def attention_backward(queries, key_heads, projected, grad_context, logsum, tables, first):
    length, width = queries.shape
    lanes = tables[0].shape[1]
    return pl.pallas_call(
        backward_kernel,
        out_shape=jax.ShapeDtypeStruct((length, 3 * width), jnp.bfloat16),
        scratch_shapes=[
            pltpu.VMEM((lanes, length), jnp.bfloat16),
            pltpu.VMEM((length, lanes), jnp.float32),
            pltpu.VMEM((length, lanes), jnp.float32),
            pltpu.VMEM((length, lanes), jnp.float32),
        ],
        compiler_params=pltpu.CompilerParams(vmem_limit_bytes=VMEM_BYTES),
        cost_estimate=SMALL_COST,
        name="attention_backward",
    )(queries, key_heads, projected, grad_context, logsum, *tables, first)


def gate_backward(gate_values, up_values, grad_hidden):
    sigmoid_gate = jax.nn.sigmoid(gate_values)
    silu_gate = gate_values * sigmoid_gate
    grad_gate = (
        grad_hidden * up_values * sigmoid_gate * (1.0 + gate_values * (1.0 - sigmoid_gate))
    ).astype(jnp.bfloat16)
    grad_up = (grad_hidden * silu_gate).astype(jnp.bfloat16)
    return (grad_gate, grad_up)


def permute(value, axis, offset):
    size = lax.axis_size(axis)
    return lax.ppermute(value, axis, [(i, i ^ offset) for i in range(size)])


def gather_dp(piece):
    return [piece] + [permute(piece, "dp", k) for k in range(1, lax.axis_size("dp"))]


def scatter_dp(pieces):
    return total([pieces[0]] + [permute(pieces[k], "dp", k) for k in range(1, len(pieces))])


def near_dp(piece):
    return [piece, permute(piece, "dp", 1), permute(piece, "dp", 2)]


def corner_dp(pieces):
    middle = pieces[0].shape[0] // 2
    return jnp.concatenate(
        [permute(pieces[2][:middle], "dp", 1), permute(pieces[1][middle:], "dp", 2)], axis=0
    )


def send_corner(pieces):
    middle = pieces[0].shape[0] // 2
    return (permute(pieces[3][:middle], "dp", 2), permute(pieces[3][middle:], "dp", 1))


def add_corner(pieces, corner):
    middle = pieces[0].shape[0] // 2
    first = total([pieces[1][:middle], corner[0]]).astype(jnp.bfloat16)
    second = total([pieces[2][middle:], corner[1]]).astype(jnp.bfloat16)
    return [
        jnp.concatenate([first, pieces[1][middle:]], axis=0),
        jnp.concatenate([pieces[2][:middle], second], axis=0),
    ]


def send_near(pieces, corner):
    first, second = add_corner(pieces, corner)
    return [permute(first, "dp", 1), permute(second, "dp", 2)]


def total(parts):
    result = parts[0].astype(jnp.float32)
    for piece in parts[1:]:
        result = result + piece.astype(jnp.float32)
    return result


def gather_seq(piece):
    return lax.all_gather(piece, "seq", axis=0, tiled=True)


def scatter_seq(terms):
    return lax.psum_scatter(
        terms.astype(jnp.bfloat16), "seq", scatter_dimension=0, tiled=True
    ).astype(jnp.float32)


def after(value, *others):
    return lax.optimization_barrier((value,) + others)[0]


def place(pieces, index):
    block = pieces[0].shape[0]
    result = jnp.zeros((block * len(pieces),) + pieces[0].shape[1:], pieces[0].dtype)
    for k, piece in enumerate(pieces):
        result = lax.dynamic_update_slice_in_dim(result, piece, (index ^ k) * block, 0)
    return result


def per_device(
    layer_input,
    doc_lengths,
    language,
    lang_table,
    attn_norm_gain,
    attn_norm_bias,
    qkv_weight,
    qkv_bias,
    out_weight,
    mlp_norm_gain,
    mlp_norm_bias,
    gate_weight,
    up_weight,
    down_weight,
    cotangent,
):
    tokens = layer_input.shape[1]
    groups = lax.axis_size("seq")
    rows = lax.axis_size("dp")
    devices = rows * groups
    at_dp = lax.axis_index("dp")
    at_seq = lax.axis_index("seq")
    length = tokens * groups
    heads_here = HEADS // groups
    local_width = heads_here * HEAD
    own = D // devices
    whole_heads = own % HEAD == 0
    deal = (rows, groups, own) if whole_heads else (1, groups, local_width)
    at_deal = (0, 0, at_seq, 0)
    owner = [(i, (i % groups) * rows + i // groups) for i in range(devices)]
    back = [(b, a) for a, b in owner]

    def to_heads(values):
        count = values.shape[0]
        return lax.dynamic_slice(
            values.reshape((count,) + deal), at_deal, (count, deal[0], 1, deal[2])
        ).reshape(count, local_width)

    def from_heads(values):
        count = values.shape[0]
        return lax.dynamic_update_slice(
            jnp.zeros((count,) + deal, values.dtype),
            values.reshape(count, deal[0], 1, deal[2]),
            at_deal,
        ).reshape(count, D)

    phase = lax.optimization_barrier
    grad_out = cotangent[0]

    def dp_terms(terms):
        block = terms.shape[0] // rows
        return [
            lax.dynamic_slice_in_dim(terms, (at_dp ^ k) * block, block, 0) for k in range(rows)
        ]

    small = jnp.concatenate(
        [
            lang_table,
            attn_norm_gain[None],
            attn_norm_bias[None],
            mlp_norm_gain[None],
            mlp_norm_bias[None],
            qkv_bias,
        ],
        axis=0,
    )
    ride = 16
    riders = jnp.zeros((ride * 3 * local_width,), jnp.bfloat16)
    riders = lax.dynamic_update_slice(riders, small.reshape(-1), (0,))
    riders = riders.reshape(ride, 3 * local_width)
    if whole_heads and rows % 2 == 0:
        dealt = deal_columns(qkv_weight, riders, groups, rows)
    else:
        dealt = jnp.concatenate(
            [
                qkv_weight.reshape((own, 3) + deal)
                .transpose(3, 0, 1, 2, 4)
                .reshape(groups, own, 3 * local_width),
                jnp.broadcast_to(riders[None], (groups,) + riders.shape),
            ],
            axis=1,
        )
    part = lax.all_to_all(dealt, "seq", split_axis=0, concat_axis=0, tiled=True)
    out_rows = out_weight if whole_heads else lax.ppermute(out_weight, ("dp", "seq"), back)
    out_pieces = gather_dp(out_rows)
    gate_pieces = near_dp(gate_weight.T)
    part, out_pieces, gate_pieces = phase((part, out_pieces, gate_pieces))
    chips = groups // 2
    input_all = gather_seq(layer_input[0])
    spread = place(gather_dp(part[:, own:].reshape(groups, -1)), at_dp)
    qkv_pieces = near_dp(part[:, :own].reshape(groups * own, 3 * local_width))
    input_all, spread, grad_far = phase((input_all, spread, grad_out))
    grad_pieces = [permute(grad_far, "seq", 2 * k) for k in range(2, chips)]
    spread = spread[:, : small.size].reshape((devices,) + small.shape)
    table = jnp.swapaxes(spread, 0, 1).reshape(small.shape[0], D).astype(jnp.float32)
    gain_attn = table[LANGS]
    bias_attn = table[LANGS + 1]
    gain_mlp = table[LANGS + 2]
    bias_mlp = table[LANGS + 3]
    bias_qkv = to_heads(table[LANGS + 4 : LANGS + 7]).reshape(3 * local_width)
    chooser = (jnp.arange(LANGS, dtype=jnp.int32) == language[0]).astype(jnp.float32)
    lang_row = jnp.sum(chooser[:, None] * table[:LANGS], axis=0)[None, :]
    offsets, cosines, sines = row_tables(doc_lengths[0], length)
    tables = rotation_tables(cosines, sines, min(128, local_width))
    first = offsets[None, :]
    resid_in = layer_input[0].astype(jnp.float32) + lang_row
    unused, scaled_attn, inverse_attn = norm_forward(resid_in, gain_attn, bias_attn)
    normed_all = norm_forward(input_all.astype(jnp.float32) + lang_row, gain_attn, bias_attn)[
        0
    ].astype(jnp.bfloat16)
    qkv_pieces, tables, first, resid_in = phase((qkv_pieces, tables, first, resid_in))
    head_qkv = place(qkv_pieces + [corner_dp(qkv_pieces)], at_dp)
    head_qkv, normed_all, grad_near = phase((head_qkv, normed_all, grad_out))
    near = permute(grad_near, "seq", 2)
    head_out = place(out_pieces, at_dp)
    projected = (
        jnp.dot(normed_all, head_qkv, preferred_element_type=jnp.float32) + bias_qkv
    ).astype(jnp.bfloat16)
    rot_query, rot_key, context_all, logsum = attention_forward(projected, tables, first)
    out_terms = jnp.dot(context_all, head_out, preferred_element_type=jnp.float32).astype(
        jnp.bfloat16
    )
    out_terms, grad_pieces, near, up_rows = phase((out_terms, grad_pieces, near, up_weight.T))
    attn_out = scatter_seq(out_terms)
    grad_pieces = [grad_out, near, *grad_pieces]
    gate_pieces = gate_pieces + [corner_dp(gate_pieces)]
    up_pieces = near_dp(up_rows)
    mates = permute(jnp.concatenate(grad_pieces, axis=0), "seq", 1)
    mates = jnp.split(mates, chips, axis=0)
    grad_all = place([piece for pair in zip(grad_pieces, mates) for piece in pair], at_seq)
    attn_out, gate_pieces, up_pieces, grad_all, down_rows = phase(
        (attn_out, gate_pieces, up_pieces, grad_all, down_weight)
    )
    resid_mid = resid_in + attn_out
    normed_mlp, scaled_mlp, inverse_mlp = norm_forward(resid_mid, gain_mlp, bias_mlp)
    rows_all = gather_seq(normed_mlp.astype(jnp.bfloat16))
    up_pieces = up_pieces + [corner_dp(up_pieces)]
    down_pieces = near_dp(down_rows)
    down_pieces, up_pieces = phase((down_pieces, up_pieces))
    cols_down = jnp.concatenate(down_pieces + [corner_dp(down_pieces)], axis=0)
    cols_gate = jnp.concatenate(gate_pieces, axis=0)
    cols_up = jnp.concatenate(up_pieces, axis=0)
    grad_hidden = contract(grad_all, cols_down, 1, 1)
    rows_all, cols_down, cols_gate, cols_up, grad_hidden = phase(
        (rows_all, cols_down, cols_gate, cols_up, grad_hidden)
    )
    gate_values = contract(rows_all, cols_gate, 1, 1)
    up_values = contract(rows_all, cols_up, 1, 1)
    hidden = (jax.nn.silu(gate_values) * up_values).astype(jnp.bfloat16)
    grad_gate, grad_up = gate_backward(gate_values, up_values, grad_hidden)
    grad_rows = (
        contract(grad_gate, cols_gate, 1, 0) + contract(grad_up, cols_up, 1, 0)
    ).astype(jnp.bfloat16)
    grad_rows, grad_gate, grad_up, hidden = phase((grad_rows, grad_gate, grad_up, hidden))
    grad_normed_mlp = scatter_seq(grad_rows)
    gate_terms = jnp.split(
        contract(grad_gate, rows_all, 0, 0).astype(jnp.bfloat16), rows, axis=0
    )
    gate_corner = send_corner(gate_terms)
    mlp_terms = contract(hidden, cols_down, 1, 0).astype(jnp.bfloat16)
    up_terms = contract(grad_up, rows_all, 0, 0).astype(jnp.bfloat16)
    gate_corner, gate_terms, mlp_terms, up_terms = phase(
        (gate_corner, gate_terms, mlp_terms, up_terms)
    )
    gate_near = send_near(gate_terms, gate_corner)
    down_terms = contract(hidden, grad_all, 0, 0).astype(jnp.bfloat16)
    grad_normed_mlp, gate_near, up_terms, mlp_terms, down_terms = phase(
        (grad_normed_mlp, gate_near, up_terms, mlp_terms, down_terms)
    )
    grad_mid_norm, grad_gain_mlp, grad_bias_mlp = norm_backward(
        grad_normed_mlp, scaled_mlp, inverse_mlp, gain_mlp
    )
    grad_mid = grad_out.astype(jnp.float32) + grad_mid_norm
    branch_all = gather_seq(grad_mid.astype(jnp.bfloat16))
    up_terms = jnp.split(up_terms, rows, axis=0)
    down_terms = jnp.split(down_terms, rows, axis=0)
    up_corner = send_corner(up_terms)
    up_corner, up_terms, down_terms = phase((up_corner, up_terms, down_terms))
    up_near = send_near(up_terms, up_corner)
    down_corner = send_corner(down_terms)
    down_terms = down_terms[:1] + add_corner(down_terms, down_corner)
    branch_all, up_near, mlp_terms, down_terms = phase(
        (branch_all, up_near, mlp_terms, down_terms)
    )
    mlp_out = scatter_seq(mlp_terms)
    down_near = [permute(down_terms[1], "dp", 1), permute(down_terms[2], "dp", 2)]
    grad_heads = contract(branch_all, head_out, 1, 1).astype(jnp.bfloat16)
    grad_stack = attention_backward(
        rot_query, rot_key, projected, grad_heads, logsum, tables, first
    )
    grad_stack, down_near = phase((grad_stack, down_near))
    slice_terms = contract(normed_all, grad_stack, 0, 0).astype(jnp.bfloat16)
    slice_pieces = dp_terms(slice_terms)
    grad_stack, slice_pieces = phase((grad_stack, slice_pieces))
    slice_near = [permute(slice_pieces[k], "dp", k) for k in range(1, rows - 1)]
    attn_terms = contract(grad_stack, head_qkv, 1, 1).astype(jnp.bfloat16)
    sums = norm_sums(input_all, attn_terms, lang_row, gain_attn)
    grad_bias_qkv = jnp.sum(grad_stack.astype(jnp.float32), axis=0).reshape(3, local_width)
    terms = jnp.concatenate(
        [
            sums[:2],
            grad_gain_mlp[None],
            grad_bias_mlp[None],
            from_heads(grad_bias_qkv),
            chooser[:, None] * (jnp.sum(grad_mid, axis=0) + sums[2])[None],
        ],
        axis=0,
    )
    count = terms.shape[0]

    def small_parts(values, index):
        return [
            lax.dynamic_index_in_dim(values, index ^ k, 0, keepdims=False)
            for k in range(values.shape[0])
        ]

    def small_sum(parts, axis):
        return total([parts[0]] + [permute(parts[k], axis, k) for k in range(1, len(parts))])

    terms = small_parts(terms.reshape(count, rows, groups, own).transpose(1, 2, 0, 3), at_dp)
    attn_terms, terms, slice_near, slice_pieces, branch_all, up_near, gate_near = phase(
        (attn_terms, terms, slice_near, slice_pieces, branch_all, up_near, gate_near)
    )
    grad_normed_attn = scatter_seq(attn_terms)
    slice_far = permute(slice_pieces[-1], "dp", rows - 1)
    terms = small_parts(small_sum(terms, "dp"), at_seq)
    out_pieces = dp_terms(contract(context_all, branch_all, 0, 0).astype(jnp.bfloat16))
    terms, slice_far, mlp_out, out_pieces, down_near, up_near, gate_near = phase(
        (terms, slice_far, mlp_out, out_pieces, down_near, up_near, gate_near)
    )
    home = (
        total([slice_pieces[0], *slice_near, slice_far])
        .astype(jnp.bfloat16)
        .reshape(groups, own, 3 * local_width)
    )
    home, terms, out_pieces, down_near, up_near, gate_near = phase(
        (home, terms, out_pieces, down_near, up_near, gate_near)
    )
    home = lax.all_to_all(home, "seq", split_axis=0, concat_axis=0, tiled=True)
    out_arrived = [permute(out_pieces[k], "dp", k) for k in range(1, rows)]
    summed = small_sum(terms, "seq")
    home, out_arrived, summed = phase((home, out_arrived, summed))
    out_proj = total([out_pieces[0], *out_arrived])
    out_gate = total([gate_terms[0], *gate_near])
    out_up = total([up_terms[0], *up_near])
    out_down = total([down_terms[0], *down_near])
    if whole_heads and rows % 2 == 0:
        grad_qkv_out = columns_in_place([home], rows)
    else:
        grad_qkv_out = (
            home.reshape(groups, own, 3, deal[0], deal[2])
            .transpose(1, 2, 3, 0, 4)
            .reshape(own, 3 * D)
            .astype(jnp.float32)
        )
    if not whole_heads:
        out_proj = lax.ppermute(out_proj, ("dp", "seq"), owner)
    layer_output = (resid_mid + mlp_out).astype(jnp.bfloat16)
    grad_normed_attn, grad_qkv_out, out_proj, out_gate, out_up, out_down, layer_output = phase(
        (grad_normed_attn, grad_qkv_out, out_proj, out_gate, out_up, out_down, layer_output)
    )
    grad_input = grad_mid + norm_backward(
        grad_normed_attn, scaled_attn, inverse_attn, gain_attn
    )[0]
    return (
        layer_output[None],
        grad_input[None],
        summed[7:],
        summed[0],
        summed[1],
        grad_qkv_out,
        summed[4:7],
        out_proj,
        summed[2],
        summed[3],
        out_gate.T,
        out_up.T,
        out_down,
    )


def solution(mesh):
    placed = (
        P("dp", "seq", None),
        P("dp", None),
        P("dp"),
        P(None, ("dp", "seq")),
        P(("dp", "seq")),
        P(("dp", "seq")),
        P(("dp", "seq"), None),
        P(None, ("dp", "seq")),
        P(("dp", "seq"), None),
        P(("dp", "seq")),
        P(("dp", "seq")),
        P(None, ("dp", "seq")),
        P(None, ("dp", "seq")),
        P(("dp", "seq"), None),
        P("dp", "seq", None),
    )
    return jax.shard_map(
        per_device,
        mesh=mesh,
        in_specs=placed,
        out_specs=(
            P("dp", "seq", None),
            P("dp", "seq", None),
            P(None, ("dp", "seq")),
            P(("dp", "seq")),
            P(("dp", "seq")),
            P(("dp", "seq"), None),
            P(None, ("dp", "seq")),
            P(("dp", "seq"), None),
            P(("dp", "seq")),
            P(("dp", "seq")),
            P(None, ("dp", "seq")),
            P(None, ("dp", "seq")),
            P(("dp", "seq"), None),
        ),
        check_vma=False,
    )
```

```python
import jax
import jax.numpy as jnp
from jax import lax
from jax.experimental import pallas as pl
from jax.experimental.pallas import tpu as pltpu
from jax.sharding import PartitionSpec as P

D = 2048
HEADS = 32
HEAD = 64
ROT = 16
LANGS = 7


EPS = 1e-05
BASE = 10000.0
NEG = -1e30


def contract(left, right, left_dim, right_dim):
    return lax.dot_general(
        left, right, (((left_dim,), (right_dim,)), ((), ())), preferred_element_type=jnp.float32
    )


def norm_forward(values, gain, bias):
    average = jnp.mean(values, axis=-1, keepdims=True)
    centered = values - average
    variance = jnp.mean(centered * centered, axis=-1, keepdims=True)
    inverse = lax.rsqrt(variance + EPS)
    scaled = centered * inverse
    return (scaled * gain + bias, scaled, inverse)


def norm_backward(grad_normed, scaled, inverse, gain):
    grad_scaled = grad_normed * gain
    grad_values = inverse * (
        grad_scaled
        - jnp.mean(grad_scaled, axis=-1, keepdims=True)
        - scaled * jnp.mean(grad_scaled * scaled, axis=-1, keepdims=True)
    )
    return (grad_values, jnp.sum(grad_normed * scaled, axis=0), jnp.sum(grad_normed, axis=0))


def row_tables(doc_lengths, length):
    ends = jnp.cumsum(doc_lengths)
    starts = ends - doc_lengths
    places = jnp.arange(length, dtype=jnp.int32)
    segment = jnp.sum((places[:, None] >= ends[None, :]).astype(jnp.int32), axis=1)
    member = segment[:, None] == jnp.arange(ends.shape[0], dtype=jnp.int32)[None, :]
    offsets = jnp.sum(jnp.where(member, starts[None, :], 0), axis=1)
    position = (places - offsets).astype(jnp.float32)
    half_rot = ROT // 2
    freq = BASE ** (-(2.0 * jnp.arange(half_rot, dtype=jnp.float32)) / ROT)
    angles = position[:, None] * freq[None, :]
    return (offsets, jnp.cos(angles), jnp.sin(angles))


def head_lanes(shape, dim, head):
    place = lax.broadcasted_iota(jnp.int32, shape, dim)
    return (place >= head * HEAD) & (place < (head + 1) * HEAD)


def turn(values, tables, direction):
    lanes = values.shape[1]
    cosines, sines_former, sines_latter = tables
    after = pltpu.roll(values, lanes - ROT // 2, 1)
    before = pltpu.roll(values, ROT // 2, 1)
    return values * cosines + direction * (before * sines_latter - after * sines_former)


def allowed_pairs(first_ref, start, block, keys):
    key_at = lax.broadcasted_iota(jnp.int32, (keys, block), 0)
    query_at = start + lax.broadcasted_iota(jnp.int32, (keys, block), 1)
    return (key_at >= first_ref[:, pl.ds(start, block)]) & (key_at <= query_at)


def over_blocks(length, block, step):
    count = length // block
    if count <= 4:
        for i in range(count):
            step(i * block, (i + 1) * block)
    else:

        def body(i, carry):
            step(pl.multiple_of(i * block, block), length)
            return carry

        lax.fori_loop(0, count, body, 0)


def forward_kernel(
    qkv_ref, cos_ref, former_ref, latter_ref, first_ref,
    query_ref, key_ref, context_ref, logsum_ref, value_t,
):
    length, width = query_ref.shape
    lanes = cos_ref.shape[1]
    block = min(256, length)
    tables = (cos_ref[...], former_ref[...], latter_ref[...])
    for group in range(width // lanes):
        part = slice(group * lanes, (group + 1) * lanes)

        def columns(c):
            begin = c * width + group * lanes
            return qkv_ref[:, begin : begin + lanes].astype(jnp.float32)

        query_ref[:, part] = turn(columns(0), tables, 1.0).astype(jnp.bfloat16)
        key_ref[:, part] = turn(columns(1), tables, 1.0).astype(jnp.bfloat16)
        value_t[...] = columns(2).T.astype(jnp.bfloat16)

        def step(start, keys):
            queries = query_ref[pl.ds(start, block), part].astype(jnp.float32) * HEAD ** (-0.5)
            allowed = allowed_pairs(first_ref, start, block, keys)
            found = []
            for head in range(lanes // HEAD):
                own = jnp.where(head_lanes(queries.shape, 1, head), queries, 0.0)
                scores = contract(key_ref[0:keys, part], own.astype(jnp.bfloat16), 1, 1)
                scores = jnp.where(allowed, scores, NEG)
                most = jnp.max(scores, axis=0, keepdims=True)
                weights = jnp.exp(scores - most)
                total = jnp.sum(weights, axis=0, keepdims=True)
                probs = (weights * (1.0 / total)).astype(jnp.bfloat16)
                logsum_ref[
                    pl.ds(group * (lanes // HEAD) + head, 1), pl.ds(start, block)
                ] = most + jnp.log(total)
                context = contract(value_t[:, 0:keys], probs, 1, 0)
                found.append(context[head * HEAD : (head + 1) * HEAD])
            context_ref[pl.ds(start, block), part] = (
                jnp.concatenate(found, axis=0).T.astype(jnp.bfloat16)
            )

        over_blocks(length, block, step)


def backward_kernel(
    query_ref, key_ref, qkv_ref, context_grad_ref, logsum_ref, cos_ref, former_ref, latter_ref,
    first_ref, grad_ref, key_t, grad_query, grad_key, grad_value,
):
    length, width = query_ref.shape
    lanes = cos_ref.shape[1]
    block = min(256, length)
    scale = HEAD ** (-0.5)
    tables = (cos_ref[...], former_ref[...], latter_ref[...])
    for group in range(width // lanes):
        part = slice(group * lanes, (group + 1) * lanes)
        value_part = slice(2 * width + group * lanes, 2 * width + (group + 1) * lanes)
        key_t[...] = key_ref[:, part].astype(jnp.float32).T.astype(jnp.bfloat16)
        grad_key[...] = jnp.zeros_like(grad_key)
        grad_value[...] = jnp.zeros_like(grad_value)

        def step(start, keys):
            queries = query_ref[pl.ds(start, block), part].astype(jnp.float32) * scale
            grads = context_grad_ref[pl.ds(start, block), part].astype(jnp.float32)
            allowed = allowed_pairs(first_ref, start, block, keys)
            found = []
            for head in range(lanes // HEAD):
                mine = head_lanes(queries.shape, 1, head)
                own_query = jnp.where(mine, queries, 0.0).astype(jnp.bfloat16)
                own_grad = jnp.where(mine, grads, 0.0).astype(jnp.bfloat16)
                scores = contract(key_ref[0:keys, part], own_query, 1, 1)
                logsum = logsum_ref[
                    pl.ds(group * (lanes // HEAD) + head, 1), pl.ds(start, block)
                ]
                soft = jnp.exp(jnp.where(allowed, scores, NEG) - logsum)
                grad_soft = contract(qkv_ref[0:keys, value_part], own_grad, 1, 1)
                weighed = soft * grad_soft
                delta = jnp.sum(weighed, axis=0, keepdims=True)
                grad_scores = (weighed - soft * delta).astype(jnp.bfloat16)
                grad_value[0:keys] += contract(soft.astype(jnp.bfloat16), own_grad, 1, 0)
                grad_key[0:keys] += contract(grad_scores, own_query, 1, 0)
                turned = contract(key_t[:, 0:keys], grad_scores, 1, 0)
                found.append(turned[head * HEAD : (head + 1) * HEAD])
            grad_query[pl.ds(start, block), :] = jnp.concatenate(found, axis=0).T * scale

        over_blocks(length, block, step)
        for c, grads in ((0, grad_query), (1, grad_key)):
            begin = c * width + group * lanes
            grad_ref[:, begin : begin + lanes] = turn(grads[...], tables, -1.0).astype(
                jnp.bfloat16
            )
        grad_ref[:, value_part] = grad_value[...].astype(jnp.bfloat16)


def columns_kernel(part_refs, out_ref, deal, width):
    row = 0
    for ref in part_refs:
        groups, rows = ref.shape[0], ref.shape[1]
        for c in range(3):
            for d in range(0, deal, 2):
                for s in range(0, groups, 2):
                    begin = c * deal * HEAD + d * HEAD
                    left = ref[s, :, begin : begin + 2 * HEAD].astype(jnp.float32)
                    right = ref[s + 1, :, begin : begin + 2 * HEAD].astype(jnp.float32)
                    lower = lax.broadcasted_iota(jnp.int32, left.shape, 1) < HEAD
                    out = c * width + d * groups * HEAD + s * HEAD
                    out_ref[row : row + rows, out : out + 2 * HEAD] = jnp.where(
                        lower, left, pltpu.roll(right, HEAD, 1)
                    )
                    out = out + groups * HEAD
                    out_ref[row : row + rows, out : out + 2 * HEAD] = jnp.where(
                        lower, pltpu.roll(left, HEAD, 1), right
                    )
        row += rows


def columns_in_place(parts, deal):
    rows = sum(part.shape[1] for part in parts)
    width = parts[0].shape[0] * deal * HEAD

    def kernel(*refs):
        columns_kernel(refs[:-1], refs[-1], deal, width)

    return pl.pallas_call(
        kernel,
        out_shape=jax.ShapeDtypeStruct((rows, 3 * width), jnp.float32),
        compiler_params=pltpu.CompilerParams(vmem_limit_bytes=VMEM_BYTES),
        name="columns_in_place",
    )(*parts)


def deal_kernel(weight_ref, riders_ref, out_ref, deal):
    groups = out_ref.shape[0]
    rows, width = weight_ref.shape[0], weight_ref.shape[1] // 3
    for c in range(3):
        for d in range(0, deal, 2):
            for s in range(0, groups, 2):
                begin = c * width + d * groups * HEAD + s * HEAD
                upper = weight_ref[:, begin : begin + 2 * HEAD].astype(jnp.float32)
                begin = begin + groups * HEAD
                after = weight_ref[:, begin : begin + 2 * HEAD].astype(jnp.float32)
                lower = lax.broadcasted_iota(jnp.int32, upper.shape, 1) < HEAD
                out = c * deal * HEAD + d * HEAD
                out_ref[s, 0:rows, out : out + 2 * HEAD] = jnp.where(
                    lower, upper, pltpu.roll(after, HEAD, 1)
                ).astype(jnp.bfloat16)
                out_ref[s + 1, 0:rows, out : out + 2 * HEAD] = jnp.where(
                    lower, pltpu.roll(upper, HEAD, 1), after
                ).astype(jnp.bfloat16)
    for s in range(groups):
        out_ref[s, rows:, :] = riders_ref[...]


def deal_columns(weight, riders, groups, deal):
    def kernel(*refs):
        deal_kernel(*refs, deal)

    return pl.pallas_call(
        kernel,
        out_shape=jax.ShapeDtypeStruct(
            (groups, weight.shape[0] + riders.shape[0], riders.shape[1]), jnp.bfloat16
        ),
        compiler_params=pltpu.CompilerParams(vmem_limit_bytes=VMEM_BYTES),
        name="deal_columns",
    )(weight, riders)


SMALL_COST = pl.CostEstimate(flops=1, bytes_accessed=1, transcendentals=1)


def middle_kernel(resid_ref, terms_ref, gain_ref, bias_ref, sum_ref, normed_ref):
    values = resid_ref[...] + terms_ref[...].astype(jnp.float32)
    sum_ref[...] = values
    normed_ref[...] = norm_forward(values, gain_ref[...], bias_ref[...])[0].astype(jnp.bfloat16)


def middle_norm(resid, terms, gain, bias):
    return pl.pallas_call(
        middle_kernel,
        out_shape=(
            jax.ShapeDtypeStruct(resid.shape, jnp.float32),
            jax.ShapeDtypeStruct(resid.shape, jnp.bfloat16),
        ),
        compiler_params=pltpu.CompilerParams(vmem_limit_bytes=VMEM_BYTES),
        cost_estimate=SMALL_COST,
        name="middle_norm",
    )(resid, terms, gain[None], bias[None])


def branch_kernel(base_ref, terms_ref, values_ref, gain_ref, grad_ref, branch_ref, sums_ref):
    unused, scaled, inverse = norm_forward(values_ref[...], 1.0, 0.0)
    grad_values, gain_sum, bias_sum = norm_backward(
        terms_ref[...].astype(jnp.float32), scaled, inverse, gain_ref[...]
    )
    grads = base_ref[...].astype(jnp.float32) + grad_values
    grad_ref[...] = grads
    branch_ref[...] = grads.astype(jnp.bfloat16)
    sums_ref[0:1] = gain_sum[None]
    sums_ref[1:2] = bias_sum[None]


def branch_norm(base, terms, values, gain):
    return pl.pallas_call(
        branch_kernel,
        out_shape=(
            jax.ShapeDtypeStruct(values.shape, jnp.float32),
            jax.ShapeDtypeStruct(values.shape, jnp.bfloat16),
            jax.ShapeDtypeStruct((2, values.shape[1]), jnp.float32),
        ),
        compiler_params=pltpu.CompilerParams(vmem_limit_bytes=VMEM_BYTES),
        cost_estimate=SMALL_COST,
        name="branch_norm",
    )(base, terms, values, gain[None])


def norm_sums_kernel(values_ref, terms_ref, lang_ref, gain_ref, out_ref):
    @pl.when(pl.program_id(0) == 0)
    def clear():
        out_ref[...] = jnp.zeros_like(out_ref)

    values = values_ref[...].astype(jnp.float32) + lang_ref[...]
    terms = terms_ref[...].astype(jnp.float32)
    unused, scaled, inverse = norm_forward(values, 1.0, 0.0)
    grad_values, gain_sum, bias_sum = norm_backward(terms, scaled, inverse, gain_ref[...])
    out_ref[0:1] += gain_sum[None]
    out_ref[1:2] += bias_sum[None]
    out_ref[2:3] += jnp.sum(grad_values, axis=0, keepdims=True)


def norm_sums(values, terms, lang_row, gain):
    length, width = values.shape
    block = min(256, length)
    rows = pl.BlockSpec((block, width), lambda i: (i, 0))
    whole = pl.BlockSpec((1, width), lambda i: (0, 0))
    return pl.pallas_call(
        norm_sums_kernel,
        grid=(length // block,),
        in_specs=[rows, rows, whole, whole],
        out_specs=pl.BlockSpec((8, width), lambda i: (0, 0)),
        out_shape=jax.ShapeDtypeStruct((8, width), jnp.float32),
        compiler_params=pltpu.CompilerParams(vmem_limit_bytes=VMEM_BYTES),
        cost_estimate=SMALL_COST,
        name="norm_sums",
    )(values, terms, lang_row, gain[None])


def rotation_tables(cosines, sines, lanes):
    length = cosines.shape[0]
    rest = jnp.ones((length, HEAD - ROT), jnp.float32)
    none = jnp.zeros_like(sines)
    heads = lanes // HEAD
    return (
        jnp.tile(jnp.concatenate([cosines, cosines, rest], axis=1), (1, heads)),
        jnp.tile(jnp.concatenate([sines, none, 0.0 * rest], axis=1), (1, heads)),
        jnp.tile(jnp.concatenate([none, sines, 0.0 * rest], axis=1), (1, heads)),
    )


VMEM_BYTES = 48 * 1024 * 1024


def attention_forward(projected, tables, first):
    length, width = projected.shape[0], projected.shape[1] // 3
    lanes = tables[0].shape[1]
    rows = jax.ShapeDtypeStruct((length, width), jnp.bfloat16)
    return pl.pallas_call(
        forward_kernel,
        out_shape=(
            rows,
            rows,
            rows,
            jax.ShapeDtypeStruct((width // HEAD, length), jnp.float32),
        ),
        scratch_shapes=[pltpu.VMEM((lanes, length), jnp.bfloat16)],
        compiler_params=pltpu.CompilerParams(vmem_limit_bytes=VMEM_BYTES),
        cost_estimate=SMALL_COST,
        name="attention_forward",
    )(projected, *tables, first)


def attention_backward(queries, key_heads, projected, grad_context, logsum, tables, first):
    length, width = queries.shape
    lanes = tables[0].shape[1]
    return pl.pallas_call(
        backward_kernel,
        out_shape=jax.ShapeDtypeStruct((length, 3 * width), jnp.bfloat16),
        scratch_shapes=[
            pltpu.VMEM((lanes, length), jnp.bfloat16),
            pltpu.VMEM((length, lanes), jnp.float32),
            pltpu.VMEM((length, lanes), jnp.float32),
            pltpu.VMEM((length, lanes), jnp.float32),
        ],
        compiler_params=pltpu.CompilerParams(vmem_limit_bytes=VMEM_BYTES),
        cost_estimate=SMALL_COST,
        name="attention_backward",
    )(queries, key_heads, projected, grad_context, logsum, *tables, first)


def gate_backward(gate_values, up_values, grad_hidden):
    sigmoid_gate = jax.nn.sigmoid(gate_values)
    silu_gate = gate_values * sigmoid_gate
    grad_gate = (
        grad_hidden * up_values * sigmoid_gate * (1.0 + gate_values * (1.0 - sigmoid_gate))
    ).astype(jnp.bfloat16)
    grad_up = (grad_hidden * silu_gate).astype(jnp.bfloat16)
    return (grad_gate, grad_up)


def permute(value, axis, offset):
    size = lax.axis_size(axis)
    return lax.ppermute(value, axis, [(i, i ^ offset) for i in range(size)])


def gather_dp(piece):
    return [piece] + [permute(piece, "dp", k) for k in range(1, lax.axis_size("dp"))]


def scatter_dp(pieces):
    return total([pieces[0]] + [permute(pieces[k], "dp", k) for k in range(1, len(pieces))])


def near_dp(piece):
    return [piece, permute(piece, "dp", 1), permute(piece, "dp", 2)]


def corner_dp(pieces):
    middle = pieces[0].shape[0] // 2
    return jnp.concatenate(
        [permute(pieces[2][:middle], "dp", 1), permute(pieces[1][middle:], "dp", 2)], axis=0
    )


def send_corner(pieces):
    middle = pieces[0].shape[0] // 2
    return (permute(pieces[3][:middle], "dp", 2), permute(pieces[3][middle:], "dp", 1))


def add_corner(pieces, corner):
    middle = pieces[0].shape[0] // 2
    first = total([pieces[1][:middle], corner[0]]).astype(jnp.bfloat16)
    second = total([pieces[2][middle:], corner[1]]).astype(jnp.bfloat16)
    return [
        jnp.concatenate([first, pieces[1][middle:]], axis=0),
        jnp.concatenate([pieces[2][:middle], second], axis=0),
    ]


def send_near(pieces, corner):
    first, second = add_corner(pieces, corner)
    return [permute(first, "dp", 1), permute(second, "dp", 2)]


def total(parts):
    result = parts[0].astype(jnp.float32)
    for piece in parts[1:]:
        result = result + piece.astype(jnp.float32)
    return result


def gather_seq(piece):
    return lax.all_gather(piece, "seq", axis=0, tiled=True)


def scatter_seq(terms):
    return lax.psum_scatter(
        terms.astype(jnp.bfloat16), "seq", scatter_dimension=0, tiled=True
    )


def after(value, *others):
    return lax.optimization_barrier((value,) + others)[0]


def place(pieces, index):
    block = pieces[0].shape[0]
    result = jnp.zeros((block * len(pieces),) + pieces[0].shape[1:], pieces[0].dtype)
    for k, piece in enumerate(pieces):
        result = lax.dynamic_update_slice_in_dim(result, piece, (index ^ k) * block, 0)
    return result


def per_device(
    layer_input,
    doc_lengths,
    language,
    lang_table,
    attn_norm_gain,
    attn_norm_bias,
    qkv_weight,
    qkv_bias,
    out_weight,
    mlp_norm_gain,
    mlp_norm_bias,
    gate_weight,
    up_weight,
    down_weight,
    cotangent,
):
    tokens = layer_input.shape[1]
    groups = lax.axis_size("seq")
    rows = lax.axis_size("dp")
    devices = rows * groups
    at_dp = lax.axis_index("dp")
    at_seq = lax.axis_index("seq")
    length = tokens * groups
    heads_here = HEADS // groups
    local_width = heads_here * HEAD
    own = D // devices
    whole_heads = own % HEAD == 0
    deal = (rows, groups, own) if whole_heads else (1, groups, local_width)
    at_deal = (0, 0, at_seq, 0)
    owner = [(i, (i % groups) * rows + i // groups) for i in range(devices)]
    back = [(b, a) for a, b in owner]

    def to_heads(values):
        count = values.shape[0]
        return lax.dynamic_slice(
            values.reshape((count,) + deal), at_deal, (count, deal[0], 1, deal[2])
        ).reshape(count, local_width)

    def from_heads(values):
        count = values.shape[0]
        return lax.dynamic_update_slice(
            jnp.zeros((count,) + deal, values.dtype),
            values.reshape(count, deal[0], 1, deal[2]),
            at_deal,
        ).reshape(count, D)

    phase = lax.optimization_barrier
    grad_out = cotangent[0]

    def dp_terms(terms):
        block = terms.shape[0] // rows
        return [
            lax.dynamic_slice_in_dim(terms, (at_dp ^ k) * block, block, 0) for k in range(rows)
        ]

    small = jnp.concatenate(
        [
            lang_table,
            attn_norm_gain[None],
            attn_norm_bias[None],
            mlp_norm_gain[None],
            mlp_norm_bias[None],
            qkv_bias,
        ],
        axis=0,
    )
    ride = 16
    riders = jnp.zeros((ride * 3 * local_width,), jnp.bfloat16)
    riders = lax.dynamic_update_slice(riders, small.reshape(-1), (0,))
    riders = riders.reshape(ride, 3 * local_width)
    if whole_heads and rows % 2 == 0:
        dealt = deal_columns(qkv_weight, riders, groups, rows)
    else:
        dealt = jnp.concatenate(
            [
                qkv_weight.reshape((own, 3) + deal)
                .transpose(3, 0, 1, 2, 4)
                .reshape(groups, own, 3 * local_width),
                jnp.broadcast_to(riders[None], (groups,) + riders.shape),
            ],
            axis=1,
        )
    part = lax.all_to_all(dealt, "seq", split_axis=0, concat_axis=0, tiled=True)
    out_rows = out_weight if whole_heads else lax.ppermute(out_weight, ("dp", "seq"), back)
    out_pieces = gather_dp(out_rows)
    gate_pieces = near_dp(gate_weight.T)
    part, out_pieces, gate_pieces = phase((part, out_pieces, gate_pieces))
    chips = groups // 2
    input_all = gather_seq(layer_input[0])
    spread = place(gather_dp(part[:, own:].reshape(groups, -1)), at_dp)
    qkv_pieces = near_dp(part[:, :own].reshape(groups * own, 3 * local_width))
    input_all, spread, grad_far = phase((input_all, spread, grad_out))
    grad_pieces = [permute(grad_far, "seq", 2 * k) for k in range(2, chips)]
    spread = spread[:, : small.size].reshape((devices,) + small.shape)
    table = jnp.swapaxes(spread, 0, 1).reshape(small.shape[0], D).astype(jnp.float32)
    gain_attn = table[LANGS]
    bias_attn = table[LANGS + 1]
    gain_mlp = table[LANGS + 2]
    bias_mlp = table[LANGS + 3]
    bias_qkv = to_heads(table[LANGS + 4 : LANGS + 7]).reshape(3 * local_width)
    chooser = (jnp.arange(LANGS, dtype=jnp.int32) == language[0]).astype(jnp.float32)
    lang_row = jnp.sum(chooser[:, None] * table[:LANGS], axis=0)[None, :]
    offsets, cosines, sines = row_tables(doc_lengths[0], length)
    tables = rotation_tables(cosines, sines, min(128, local_width))
    first = offsets[None, :]
    resid_in = layer_input[0].astype(jnp.float32) + lang_row
    normed_all = norm_forward(input_all.astype(jnp.float32) + lang_row, gain_attn, bias_attn)[
        0
    ].astype(jnp.bfloat16)
    qkv_pieces, tables, first, resid_in = phase((qkv_pieces, tables, first, resid_in))
    head_qkv = place(qkv_pieces + [corner_dp(qkv_pieces)], at_dp)
    head_qkv, normed_all, grad_near = phase((head_qkv, normed_all, grad_out))
    near = permute(grad_near, "seq", 2)
    head_out = place(out_pieces, at_dp)
    projected = (
        jnp.dot(normed_all, head_qkv, preferred_element_type=jnp.float32) + bias_qkv
    ).astype(jnp.bfloat16)
    rot_query, rot_key, context_all, logsum = attention_forward(projected, tables, first)
    out_terms = jnp.dot(context_all, head_out, preferred_element_type=jnp.float32).astype(
        jnp.bfloat16
    )
    out_terms, grad_pieces, near, up_rows = phase((out_terms, grad_pieces, near, up_weight.T))
    attn_out = scatter_seq(out_terms)
    grad_pieces = [grad_out, near, *grad_pieces]
    gate_pieces = gate_pieces + [corner_dp(gate_pieces)]
    up_pieces = near_dp(up_rows)
    mates = permute(jnp.concatenate(grad_pieces, axis=0), "seq", 1)
    mates = jnp.split(mates, chips, axis=0)
    grad_all = place([piece for pair in zip(grad_pieces, mates) for piece in pair], at_seq)
    attn_out, gate_pieces, up_pieces, grad_all, down_rows = phase(
        (attn_out, gate_pieces, up_pieces, grad_all, down_weight)
    )
    resid_mid, normed_mlp = middle_norm(resid_in, attn_out, gain_mlp, bias_mlp)
    rows_all = gather_seq(normed_mlp)
    up_pieces = up_pieces + [corner_dp(up_pieces)]
    down_pieces = near_dp(down_rows)
    down_pieces, up_pieces = phase((down_pieces, up_pieces))
    cols_down = jnp.concatenate(down_pieces + [corner_dp(down_pieces)], axis=0)
    cols_gate = jnp.concatenate(gate_pieces, axis=0)
    cols_up = jnp.concatenate(up_pieces, axis=0)
    grad_hidden = contract(grad_all, cols_down, 1, 1)
    rows_all, cols_down, cols_gate, cols_up, grad_hidden = phase(
        (rows_all, cols_down, cols_gate, cols_up, grad_hidden)
    )
    gate_values = contract(rows_all, cols_gate, 1, 1)
    up_values = contract(rows_all, cols_up, 1, 1)
    hidden = (jax.nn.silu(gate_values) * up_values).astype(jnp.bfloat16)
    grad_gate, grad_up = gate_backward(gate_values, up_values, grad_hidden)
    grad_rows = (
        contract(grad_gate, cols_gate, 1, 0) + contract(grad_up, cols_up, 1, 0)
    ).astype(jnp.bfloat16)
    grad_rows, grad_gate, grad_up, hidden = phase((grad_rows, grad_gate, grad_up, hidden))
    grad_normed_mlp = scatter_seq(grad_rows)
    gate_terms = jnp.split(
        contract(grad_gate, rows_all, 0, 0).astype(jnp.bfloat16), rows, axis=0
    )
    gate_corner = send_corner(gate_terms)
    mlp_terms = contract(hidden, cols_down, 1, 0).astype(jnp.bfloat16)
    up_terms = contract(grad_up, rows_all, 0, 0).astype(jnp.bfloat16)
    gate_corner, gate_terms, mlp_terms, up_terms = phase(
        (gate_corner, gate_terms, mlp_terms, up_terms)
    )
    gate_near = send_near(gate_terms, gate_corner)
    down_terms = contract(hidden, grad_all, 0, 0).astype(jnp.bfloat16)
    grad_normed_mlp, gate_near, up_terms, mlp_terms, down_terms = phase(
        (grad_normed_mlp, gate_near, up_terms, mlp_terms, down_terms)
    )
    grad_mid, grad_branch, mlp_norm_sums = branch_norm(
        grad_out, grad_normed_mlp, resid_mid, gain_mlp
    )
    branch_all = gather_seq(grad_branch)
    up_terms = jnp.split(up_terms, rows, axis=0)
    down_terms = jnp.split(down_terms, rows, axis=0)
    up_corner = send_corner(up_terms)
    up_corner, up_terms, down_terms = phase((up_corner, up_terms, down_terms))
    up_near = send_near(up_terms, up_corner)
    down_corner = send_corner(down_terms)
    down_terms = down_terms[:1] + add_corner(down_terms, down_corner)
    branch_all, up_near, mlp_terms, down_terms = phase(
        (branch_all, up_near, mlp_terms, down_terms)
    )
    mlp_out = scatter_seq(mlp_terms)
    down_near = [permute(down_terms[1], "dp", 1), permute(down_terms[2], "dp", 2)]
    grad_heads = contract(branch_all, head_out, 1, 1).astype(jnp.bfloat16)
    grad_stack = attention_backward(
        rot_query, rot_key, projected, grad_heads, logsum, tables, first
    )
    grad_stack, down_near = phase((grad_stack, down_near))
    slice_terms = contract(normed_all, grad_stack, 0, 0).astype(jnp.bfloat16)
    slice_pieces = dp_terms(slice_terms)
    grad_stack, slice_pieces = phase((grad_stack, slice_pieces))
    slice_near = [permute(slice_pieces[k], "dp", k) for k in range(1, rows - 1)]
    attn_terms = contract(grad_stack, head_qkv, 1, 1).astype(jnp.bfloat16)
    sums = norm_sums(input_all, attn_terms, lang_row, gain_attn)
    attn_terms, sums, slice_near, slice_pieces, branch_all, up_near, gate_near, grad_stack = phase(
        (attn_terms, sums, slice_near, slice_pieces, branch_all, up_near, gate_near, grad_stack)
    )
    grad_normed_attn = scatter_seq(attn_terms)
    slice_far = permute(slice_pieces[-1], "dp", rows - 1)
    grad_bias_qkv = jnp.sum(grad_stack.astype(jnp.float32), axis=0).reshape(3, local_width)
    terms = jnp.concatenate(
        [
            sums[:2],
            mlp_norm_sums,
            from_heads(grad_bias_qkv),
            chooser[:, None] * (jnp.sum(grad_mid, axis=0) + sums[2])[None],
        ],
        axis=0,
    )
    count = terms.shape[0]

    def small_parts(values, index):
        return [
            lax.dynamic_index_in_dim(values, index ^ k, 0, keepdims=False)
            for k in range(values.shape[0])
        ]

    def small_sum(parts, axis):
        return total([parts[0]] + [permute(parts[k], axis, k) for k in range(1, len(parts))])

    terms = small_parts(terms.reshape(count, rows, groups, own).transpose(1, 2, 0, 3), at_dp)
    terms = small_parts(small_sum(terms, "dp"), at_seq)
    out_pieces = dp_terms(contract(context_all, branch_all, 0, 0).astype(jnp.bfloat16))
    terms, slice_far, mlp_out, out_pieces, down_near, up_near, gate_near = phase(
        (terms, slice_far, mlp_out, out_pieces, down_near, up_near, gate_near)
    )
    home = (
        total([slice_pieces[0], *slice_near, slice_far])
        .astype(jnp.bfloat16)
        .reshape(groups, own, 3 * local_width)
    )
    home, terms, out_pieces, down_near, up_near, gate_near = phase(
        (home, terms, out_pieces, down_near, up_near, gate_near)
    )
    home = lax.all_to_all(home, "seq", split_axis=0, concat_axis=0, tiled=True)
    out_arrived = [permute(out_pieces[k], "dp", k) for k in range(1, rows)]
    summed = small_sum(terms, "seq")
    home, out_arrived, summed = phase((home, out_arrived, summed))
    out_proj = total([out_pieces[0], *out_arrived])
    out_gate = total([gate_terms[0], *gate_near])
    out_up = total([up_terms[0], *up_near])
    out_down = total([down_terms[0], *down_near])
    if whole_heads and rows % 2 == 0:
        grad_qkv_out = columns_in_place([home], rows)
    else:
        grad_qkv_out = (
            home.reshape(groups, own, 3, deal[0], deal[2])
            .transpose(1, 2, 3, 0, 4)
            .reshape(own, 3 * D)
            .astype(jnp.float32)
        )
    if not whole_heads:
        out_proj = lax.ppermute(out_proj, ("dp", "seq"), owner)
    layer_output = (resid_mid + mlp_out).astype(jnp.bfloat16)
    grad_normed_attn, grad_qkv_out, out_proj, out_gate, out_up, out_down, layer_output = phase(
        (grad_normed_attn, grad_qkv_out, out_proj, out_gate, out_up, out_down, layer_output)
    )
    grad_input = branch_norm(grad_mid, grad_normed_attn, resid_in, gain_attn)[0]
    return (
        layer_output[None],
        grad_input[None],
        summed[7:],
        summed[0],
        summed[1],
        grad_qkv_out,
        summed[4:7],
        out_proj,
        summed[2],
        summed[3],
        out_gate.T,
        out_up.T,
        out_down,
    )


def solution(mesh):
    placed = (
        P("dp", "seq", None),
        P("dp", None),
        P("dp"),
        P(None, ("dp", "seq")),
        P(("dp", "seq")),
        P(("dp", "seq")),
        P(("dp", "seq"), None),
        P(None, ("dp", "seq")),
        P(("dp", "seq"), None),
        P(("dp", "seq")),
        P(("dp", "seq")),
        P(None, ("dp", "seq")),
        P(None, ("dp", "seq")),
        P(("dp", "seq"), None),
        P("dp", "seq", None),
    )
    return jax.shard_map(
        per_device,
        mesh=mesh,
        in_specs=placed,
        out_specs=(
            P("dp", "seq", None),
            P("dp", "seq", None),
            P(None, ("dp", "seq")),
            P(("dp", "seq")),
            P(("dp", "seq")),
            P(("dp", "seq"), None),
            P(None, ("dp", "seq")),
            P(("dp", "seq"), None),
            P(("dp", "seq")),
            P(("dp", "seq")),
            P(None, ("dp", "seq")),
            P(None, ("dp", "seq")),
            P(("dp", "seq"), None),
        ),
        check_vma=False,
    )
```

```python
import jax
import jax.numpy as jnp
from jax import lax
from jax.experimental import pallas as pl
from jax.experimental.pallas import tpu as pltpu
from jax.sharding import PartitionSpec as P

D = 2048
HEADS = 32
HEAD = 64
ROT = 16
LANGS = 7


EPS = 1e-05
BASE = 10000.0
NEG = -1e30


def contract(left, right, left_dim, right_dim):
    return lax.dot_general(
        left, right, (((left_dim,), (right_dim,)), ((), ())), preferred_element_type=jnp.float32
    )


def norm_forward(values, gain, bias):
    average = jnp.mean(values, axis=-1, keepdims=True)
    centered = values - average
    variance = jnp.mean(centered * centered, axis=-1, keepdims=True)
    inverse = lax.rsqrt(variance + EPS)
    scaled = centered * inverse
    return (scaled * gain + bias, scaled, inverse)


def norm_backward(grad_normed, scaled, inverse, gain):
    grad_scaled = grad_normed * gain
    grad_values = inverse * (
        grad_scaled
        - jnp.mean(grad_scaled, axis=-1, keepdims=True)
        - scaled * jnp.mean(grad_scaled * scaled, axis=-1, keepdims=True)
    )
    return (grad_values, jnp.sum(grad_normed * scaled, axis=0), jnp.sum(grad_normed, axis=0))


def row_tables(doc_lengths, length):
    ends = jnp.cumsum(doc_lengths)
    starts = ends - doc_lengths
    places = jnp.arange(length, dtype=jnp.int32)
    segment = jnp.sum((places[:, None] >= ends[None, :]).astype(jnp.int32), axis=1)
    member = segment[:, None] == jnp.arange(ends.shape[0], dtype=jnp.int32)[None, :]
    offsets = jnp.sum(jnp.where(member, starts[None, :], 0), axis=1)
    position = (places - offsets).astype(jnp.float32)
    half_rot = ROT // 2
    freq = BASE ** (-(2.0 * jnp.arange(half_rot, dtype=jnp.float32)) / ROT)
    angles = position[:, None] * freq[None, :]
    return (offsets, jnp.cos(angles), jnp.sin(angles))


def head_lanes(shape, dim, head):
    place = lax.broadcasted_iota(jnp.int32, shape, dim)
    return (place >= head * HEAD) & (place < (head + 1) * HEAD)


def turn(values, tables, direction):
    lanes = values.shape[1]
    cosines, sines_former, sines_latter = tables
    after = pltpu.roll(values, lanes - ROT // 2, 1)
    before = pltpu.roll(values, ROT // 2, 1)
    return values * cosines + direction * (before * sines_latter - after * sines_former)


def allowed_pairs(first_ref, start, block, keys):
    key_at = lax.broadcasted_iota(jnp.int32, (keys, block), 0)
    query_at = start + lax.broadcasted_iota(jnp.int32, (keys, block), 1)
    return (key_at >= first_ref[:, pl.ds(start, block)]) & (key_at <= query_at)


def over_blocks(length, block, step):
    count = length // block
    if count <= 8:
        for i in range(count):
            step(i * block, (i + 1) * block)
    else:

        def body(i, carry):
            step(pl.multiple_of(i * block, block), length)
            return carry

        lax.fori_loop(0, count, body, 0)


def forward_kernel(
    qkv_ref, cos_ref, former_ref, latter_ref, first_ref,
    query_ref, key_ref, context_ref, logsum_ref, value_t,
):
    length, width = query_ref.shape
    lanes = cos_ref.shape[1]
    block = min(128, length)
    tables = (cos_ref[...], former_ref[...], latter_ref[...])
    for group in range(width // lanes):
        part = slice(group * lanes, (group + 1) * lanes)

        def columns(c):
            begin = c * width + group * lanes
            return qkv_ref[:, begin : begin + lanes].astype(jnp.float32)

        query_ref[:, part] = turn(columns(0), tables, 1.0).astype(jnp.bfloat16)
        key_ref[:, part] = turn(columns(1), tables, 1.0).astype(jnp.bfloat16)
        value_t[...] = columns(2).T.astype(jnp.bfloat16)

        def step(start, keys):
            queries = query_ref[pl.ds(start, block), part].astype(jnp.float32) * HEAD ** (-0.5)
            allowed = allowed_pairs(first_ref, start, block, keys)
            found = []
            for head in range(lanes // HEAD):
                own = jnp.where(head_lanes(queries.shape, 1, head), queries, 0.0)
                scores = contract(key_ref[0:keys, part], own.astype(jnp.bfloat16), 1, 1)
                scores = jnp.where(allowed, scores, NEG)
                most = jnp.max(scores, axis=0, keepdims=True)
                weights = jnp.exp(scores - most)
                total = jnp.sum(weights, axis=0, keepdims=True)
                probs = (weights * (1.0 / total)).astype(jnp.bfloat16)
                logsum_ref[
                    pl.ds(group * (lanes // HEAD) + head, 1), pl.ds(start, block)
                ] = most + jnp.log(total)
                context = contract(value_t[:, 0:keys], probs, 1, 0)
                found.append(context[head * HEAD : (head + 1) * HEAD])
            context_ref[pl.ds(start, block), part] = (
                jnp.concatenate(found, axis=0).T.astype(jnp.bfloat16)
            )

        over_blocks(length, block, step)


def backward_kernel(
    query_ref, key_ref, qkv_ref, context_grad_ref, logsum_ref, cos_ref, former_ref, latter_ref,
    first_ref, grad_ref, key_t, grad_query, grad_key, grad_value,
):
    length, width = query_ref.shape
    lanes = cos_ref.shape[1]
    block = min(256, length)
    scale = HEAD ** (-0.5)
    tables = (cos_ref[...], former_ref[...], latter_ref[...])
    for group in range(width // lanes):
        part = slice(group * lanes, (group + 1) * lanes)
        value_part = slice(2 * width + group * lanes, 2 * width + (group + 1) * lanes)
        key_t[...] = key_ref[:, part].astype(jnp.float32).T.astype(jnp.bfloat16)
        grad_key[...] = jnp.zeros_like(grad_key)
        grad_value[...] = jnp.zeros_like(grad_value)

        def step(start, keys):
            queries = query_ref[pl.ds(start, block), part].astype(jnp.float32) * scale
            grads = context_grad_ref[pl.ds(start, block), part].astype(jnp.float32)
            allowed = allowed_pairs(first_ref, start, block, keys)
            found = []
            for head in range(lanes // HEAD):
                mine = head_lanes(queries.shape, 1, head)
                own_query = jnp.where(mine, queries, 0.0).astype(jnp.bfloat16)
                own_grad = jnp.where(mine, grads, 0.0).astype(jnp.bfloat16)
                scores = contract(key_ref[0:keys, part], own_query, 1, 1)
                logsum = logsum_ref[
                    pl.ds(group * (lanes // HEAD) + head, 1), pl.ds(start, block)
                ]
                soft = jnp.exp(jnp.where(allowed, scores, NEG) - logsum)
                grad_soft = contract(qkv_ref[0:keys, value_part], own_grad, 1, 1)
                weighed = soft * grad_soft
                delta = jnp.sum(weighed, axis=0, keepdims=True)
                grad_scores = (weighed - soft * delta).astype(jnp.bfloat16)
                grad_value[0:keys] += contract(soft.astype(jnp.bfloat16), own_grad, 1, 0)
                grad_key[0:keys] += contract(grad_scores, own_query, 1, 0)
                turned = contract(key_t[:, 0:keys], grad_scores, 1, 0)
                found.append(turned[head * HEAD : (head + 1) * HEAD])
            grad_query[pl.ds(start, block), :] = jnp.concatenate(found, axis=0).T * scale

        over_blocks(length, block, step)
        for c, grads in ((0, grad_query), (1, grad_key)):
            begin = c * width + group * lanes
            grad_ref[:, begin : begin + lanes] = turn(grads[...], tables, -1.0).astype(
                jnp.bfloat16
            )
        grad_ref[:, value_part] = grad_value[...].astype(jnp.bfloat16)


def columns_kernel(part_refs, out_ref, deal, width):
    row = 0
    for ref in part_refs:
        groups, rows = ref.shape[0], ref.shape[1]
        for c in range(3):
            for d in range(0, deal, 2):
                for s in range(0, groups, 2):
                    begin = c * deal * HEAD + d * HEAD
                    left = ref[s, :, begin : begin + 2 * HEAD].astype(jnp.float32)
                    right = ref[s + 1, :, begin : begin + 2 * HEAD].astype(jnp.float32)
                    lower = lax.broadcasted_iota(jnp.int32, left.shape, 1) < HEAD
                    out = c * width + d * groups * HEAD + s * HEAD
                    out_ref[row : row + rows, out : out + 2 * HEAD] = jnp.where(
                        lower, left, pltpu.roll(right, HEAD, 1)
                    )
                    out = out + groups * HEAD
                    out_ref[row : row + rows, out : out + 2 * HEAD] = jnp.where(
                        lower, pltpu.roll(left, HEAD, 1), right
                    )
        row += rows


def columns_in_place(parts, deal):
    rows = sum(part.shape[1] for part in parts)
    width = parts[0].shape[0] * deal * HEAD

    def kernel(*refs):
        columns_kernel(refs[:-1], refs[-1], deal, width)

    return pl.pallas_call(
        kernel,
        out_shape=jax.ShapeDtypeStruct((rows, 3 * width), jnp.float32),
        compiler_params=pltpu.CompilerParams(vmem_limit_bytes=VMEM_BYTES),
        name="columns_in_place",
    )(*parts)


def deal_kernel(weight_ref, riders_ref, out_ref, deal):
    groups = out_ref.shape[0]
    rows, width = weight_ref.shape[0], weight_ref.shape[1] // 3
    for c in range(3):
        for d in range(0, deal, 2):
            for s in range(0, groups, 2):
                begin = c * width + d * groups * HEAD + s * HEAD
                upper = weight_ref[:, begin : begin + 2 * HEAD].astype(jnp.float32)
                begin = begin + groups * HEAD
                after = weight_ref[:, begin : begin + 2 * HEAD].astype(jnp.float32)
                lower = lax.broadcasted_iota(jnp.int32, upper.shape, 1) < HEAD
                out = c * deal * HEAD + d * HEAD
                out_ref[s, 0:rows, out : out + 2 * HEAD] = jnp.where(
                    lower, upper, pltpu.roll(after, HEAD, 1)
                ).astype(jnp.bfloat16)
                out_ref[s + 1, 0:rows, out : out + 2 * HEAD] = jnp.where(
                    lower, pltpu.roll(upper, HEAD, 1), after
                ).astype(jnp.bfloat16)
    for s in range(groups):
        out_ref[s, rows:, :] = riders_ref[...]


def deal_columns(weight, riders, groups, deal):
    def kernel(*refs):
        deal_kernel(*refs, deal)

    return pl.pallas_call(
        kernel,
        out_shape=jax.ShapeDtypeStruct(
            (groups, weight.shape[0] + riders.shape[0], riders.shape[1]), jnp.bfloat16
        ),
        compiler_params=pltpu.CompilerParams(vmem_limit_bytes=VMEM_BYTES),
        name="deal_columns",
    )(weight, riders)


SMALL_COST = pl.CostEstimate(flops=1, bytes_accessed=1, transcendentals=1)


def middle_kernel(resid_ref, terms_ref, gain_ref, bias_ref, sum_ref, normed_ref):
    values = resid_ref[...] + terms_ref[...].astype(jnp.float32)
    sum_ref[...] = values
    normed_ref[...] = norm_forward(values, gain_ref[...], bias_ref[...])[0].astype(jnp.bfloat16)


def middle_norm(resid, terms, gain, bias):
    return pl.pallas_call(
        middle_kernel,
        out_shape=(
            jax.ShapeDtypeStruct(resid.shape, jnp.float32),
            jax.ShapeDtypeStruct(resid.shape, jnp.bfloat16),
        ),
        compiler_params=pltpu.CompilerParams(vmem_limit_bytes=VMEM_BYTES),
        cost_estimate=SMALL_COST,
        name="middle_norm",
    )(resid, terms, gain[None], bias[None])


def branch_kernel(base_ref, terms_ref, values_ref, gain_ref, grad_ref, branch_ref, sums_ref):
    unused, scaled, inverse = norm_forward(values_ref[...], 1.0, 0.0)
    grad_values, gain_sum, bias_sum = norm_backward(
        terms_ref[...].astype(jnp.float32), scaled, inverse, gain_ref[...]
    )
    grads = base_ref[...].astype(jnp.float32) + grad_values
    grad_ref[...] = grads
    branch_ref[...] = grads.astype(jnp.bfloat16)
    sums_ref[0:1] = gain_sum[None]
    sums_ref[1:2] = bias_sum[None]


def branch_norm(base, terms, values, gain):
    return pl.pallas_call(
        branch_kernel,
        out_shape=(
            jax.ShapeDtypeStruct(values.shape, jnp.float32),
            jax.ShapeDtypeStruct(values.shape, jnp.bfloat16),
            jax.ShapeDtypeStruct((2, values.shape[1]), jnp.float32),
        ),
        compiler_params=pltpu.CompilerParams(vmem_limit_bytes=VMEM_BYTES),
        cost_estimate=SMALL_COST,
        name="branch_norm",
    )(base, terms, values, gain[None])


def norm_sums_kernel(values_ref, terms_ref, lang_ref, gain_ref, out_ref):
    @pl.when(pl.program_id(0) == 0)
    def clear():
        out_ref[...] = jnp.zeros_like(out_ref)

    values = values_ref[...].astype(jnp.float32) + lang_ref[...]
    terms = terms_ref[...].astype(jnp.float32)
    unused, scaled, inverse = norm_forward(values, 1.0, 0.0)
    grad_values, gain_sum, bias_sum = norm_backward(terms, scaled, inverse, gain_ref[...])
    out_ref[0:1] += gain_sum[None]
    out_ref[1:2] += bias_sum[None]
    out_ref[2:3] += jnp.sum(grad_values, axis=0, keepdims=True)


def norm_sums(values, terms, lang_row, gain):
    length, width = values.shape
    block = min(256, length)
    rows = pl.BlockSpec((block, width), lambda i: (i, 0))
    whole = pl.BlockSpec((1, width), lambda i: (0, 0))
    return pl.pallas_call(
        norm_sums_kernel,
        grid=(length // block,),
        in_specs=[rows, rows, whole, whole],
        out_specs=pl.BlockSpec((8, width), lambda i: (0, 0)),
        out_shape=jax.ShapeDtypeStruct((8, width), jnp.float32),
        compiler_params=pltpu.CompilerParams(vmem_limit_bytes=VMEM_BYTES),
        cost_estimate=SMALL_COST,
        name="norm_sums",
    )(values, terms, lang_row, gain[None])


def rotation_tables(cosines, sines, lanes):
    length = cosines.shape[0]
    rest = jnp.ones((length, HEAD - ROT), jnp.float32)
    none = jnp.zeros_like(sines)
    heads = lanes // HEAD
    return (
        jnp.tile(jnp.concatenate([cosines, cosines, rest], axis=1), (1, heads)),
        jnp.tile(jnp.concatenate([sines, none, 0.0 * rest], axis=1), (1, heads)),
        jnp.tile(jnp.concatenate([none, sines, 0.0 * rest], axis=1), (1, heads)),
    )


VMEM_BYTES = 48 * 1024 * 1024


def attention_forward(projected, tables, first):
    length, width = projected.shape[0], projected.shape[1] // 3
    lanes = tables[0].shape[1]
    rows = jax.ShapeDtypeStruct((length, width), jnp.bfloat16)
    return pl.pallas_call(
        forward_kernel,
        out_shape=(
            rows,
            rows,
            rows,
            jax.ShapeDtypeStruct((width // HEAD, length), jnp.float32),
        ),
        scratch_shapes=[pltpu.VMEM((lanes, length), jnp.bfloat16)],
        compiler_params=pltpu.CompilerParams(vmem_limit_bytes=VMEM_BYTES),
        cost_estimate=SMALL_COST,
        name="attention_forward",
    )(projected, *tables, first)


def attention_backward(queries, key_heads, projected, grad_context, logsum, tables, first):
    length, width = queries.shape
    lanes = tables[0].shape[1]
    return pl.pallas_call(
        backward_kernel,
        out_shape=jax.ShapeDtypeStruct((length, 3 * width), jnp.bfloat16),
        scratch_shapes=[
            pltpu.VMEM((lanes, length), jnp.bfloat16),
            pltpu.VMEM((length, lanes), jnp.float32),
            pltpu.VMEM((length, lanes), jnp.float32),
            pltpu.VMEM((length, lanes), jnp.float32),
        ],
        compiler_params=pltpu.CompilerParams(vmem_limit_bytes=VMEM_BYTES),
        cost_estimate=SMALL_COST,
        name="attention_backward",
    )(queries, key_heads, projected, grad_context, logsum, *tables, first)


def gate_backward(gate_values, up_values, grad_hidden):
    sigmoid_gate = jax.nn.sigmoid(gate_values)
    silu_gate = gate_values * sigmoid_gate
    grad_gate = (
        grad_hidden * up_values * sigmoid_gate * (1.0 + gate_values * (1.0 - sigmoid_gate))
    ).astype(jnp.bfloat16)
    grad_up = (grad_hidden * silu_gate).astype(jnp.bfloat16)
    return (grad_gate, grad_up)


def permute(value, axis, offset):
    size = lax.axis_size(axis)
    return lax.ppermute(value, axis, [(i, i ^ offset) for i in range(size)])


def gather_dp(piece):
    return [piece] + [permute(piece, "dp", k) for k in range(1, lax.axis_size("dp"))]


def scatter_dp(pieces):
    return total([pieces[0]] + [permute(pieces[k], "dp", k) for k in range(1, len(pieces))])


def near_dp(piece):
    return [piece, permute(piece, "dp", 1), permute(piece, "dp", 2)]


def corner_dp(pieces):
    middle = pieces[0].shape[0] // 2
    return jnp.concatenate(
        [permute(pieces[2][:middle], "dp", 1), permute(pieces[1][middle:], "dp", 2)], axis=0
    )


def send_corner(pieces):
    middle = pieces[0].shape[0] // 2
    return (permute(pieces[3][:middle], "dp", 2), permute(pieces[3][middle:], "dp", 1))


def add_corner(pieces, corner):
    middle = pieces[0].shape[0] // 2
    first = total([pieces[1][:middle], corner[0]]).astype(jnp.bfloat16)
    second = total([pieces[2][middle:], corner[1]]).astype(jnp.bfloat16)
    return [
        jnp.concatenate([first, pieces[1][middle:]], axis=0),
        jnp.concatenate([pieces[2][:middle], second], axis=0),
    ]


def send_near(pieces, corner):
    first, second = add_corner(pieces, corner)
    return [permute(first, "dp", 1), permute(second, "dp", 2)]


def total(parts):
    result = parts[0].astype(jnp.float32)
    for piece in parts[1:]:
        result = result + piece.astype(jnp.float32)
    return result


def gather_seq(piece):
    return lax.all_gather(piece, "seq", axis=0, tiled=True)


def scatter_seq(terms):
    return lax.psum_scatter(
        terms.astype(jnp.bfloat16), "seq", scatter_dimension=0, tiled=True
    )


def after(value, *others):
    return lax.optimization_barrier((value,) + others)[0]


def place(pieces, index):
    block = pieces[0].shape[0]
    result = jnp.zeros((block * len(pieces),) + pieces[0].shape[1:], pieces[0].dtype)
    for k, piece in enumerate(pieces):
        result = lax.dynamic_update_slice_in_dim(result, piece, (index ^ k) * block, 0)
    return result


def per_device(
    layer_input,
    doc_lengths,
    language,
    lang_table,
    attn_norm_gain,
    attn_norm_bias,
    qkv_weight,
    qkv_bias,
    out_weight,
    mlp_norm_gain,
    mlp_norm_bias,
    gate_weight,
    up_weight,
    down_weight,
    cotangent,
):
    tokens = layer_input.shape[1]
    groups = lax.axis_size("seq")
    rows = lax.axis_size("dp")
    devices = rows * groups
    at_dp = lax.axis_index("dp")
    at_seq = lax.axis_index("seq")
    length = tokens * groups
    heads_here = HEADS // groups
    local_width = heads_here * HEAD
    own = D // devices
    whole_heads = own % HEAD == 0
    deal = (rows, groups, own) if whole_heads else (1, groups, local_width)
    at_deal = (0, 0, at_seq, 0)
    owner = [(i, (i % groups) * rows + i // groups) for i in range(devices)]
    back = [(b, a) for a, b in owner]

    def to_heads(values):
        count = values.shape[0]
        return lax.dynamic_slice(
            values.reshape((count,) + deal), at_deal, (count, deal[0], 1, deal[2])
        ).reshape(count, local_width)

    def from_heads(values):
        count = values.shape[0]
        return lax.dynamic_update_slice(
            jnp.zeros((count,) + deal, values.dtype),
            values.reshape(count, deal[0], 1, deal[2]),
            at_deal,
        ).reshape(count, D)

    phase = lax.optimization_barrier
    grad_out = cotangent[0]

    def dp_terms(terms):
        block = terms.shape[0] // rows
        return [
            lax.dynamic_slice_in_dim(terms, (at_dp ^ k) * block, block, 0) for k in range(rows)
        ]

    small = jnp.concatenate(
        [
            lang_table,
            attn_norm_gain[None],
            attn_norm_bias[None],
            mlp_norm_gain[None],
            mlp_norm_bias[None],
            qkv_bias,
        ],
        axis=0,
    )
    ride = 16
    riders = jnp.zeros((ride * 3 * local_width,), jnp.bfloat16)
    riders = lax.dynamic_update_slice(riders, small.reshape(-1), (0,))
    riders = riders.reshape(ride, 3 * local_width)
    if whole_heads and rows % 2 == 0:
        dealt = deal_columns(qkv_weight, riders, groups, rows)
    else:
        dealt = jnp.concatenate(
            [
                qkv_weight.reshape((own, 3) + deal)
                .transpose(3, 0, 1, 2, 4)
                .reshape(groups, own, 3 * local_width),
                jnp.broadcast_to(riders[None], (groups,) + riders.shape),
            ],
            axis=1,
        )
    part = lax.all_to_all(dealt, "seq", split_axis=0, concat_axis=0, tiled=True)
    out_rows = out_weight if whole_heads else lax.ppermute(out_weight, ("dp", "seq"), back)
    out_pieces = gather_dp(out_rows)
    gate_pieces = near_dp(gate_weight.T)
    part, out_pieces, gate_pieces = phase((part, out_pieces, gate_pieces))
    chips = groups // 2
    input_all = gather_seq(layer_input[0])
    spread = place(gather_dp(part[:, own:].reshape(groups, -1)), at_dp)
    qkv_pieces = near_dp(part[:, :own].reshape(groups * own, 3 * local_width))
    input_all, spread, grad_far = phase((input_all, spread, grad_out))
    grad_pieces = [permute(grad_far, "seq", 2 * k) for k in range(2, chips)]
    spread = spread[:, : small.size].reshape((devices,) + small.shape)
    table = jnp.swapaxes(spread, 0, 1).reshape(small.shape[0], D).astype(jnp.float32)
    gain_attn = table[LANGS]
    bias_attn = table[LANGS + 1]
    gain_mlp = table[LANGS + 2]
    bias_mlp = table[LANGS + 3]
    bias_qkv = to_heads(table[LANGS + 4 : LANGS + 7]).reshape(3 * local_width)
    chooser = (jnp.arange(LANGS, dtype=jnp.int32) == language[0]).astype(jnp.float32)
    lang_row = jnp.sum(chooser[:, None] * table[:LANGS], axis=0)[None, :]
    offsets, cosines, sines = row_tables(doc_lengths[0], length)
    tables = rotation_tables(cosines, sines, min(128, local_width))
    first = offsets[None, :]
    resid_in = layer_input[0].astype(jnp.float32) + lang_row
    normed_all = norm_forward(input_all.astype(jnp.float32) + lang_row, gain_attn, bias_attn)[
        0
    ].astype(jnp.bfloat16)
    qkv_pieces, tables, first, resid_in = phase((qkv_pieces, tables, first, resid_in))
    head_qkv = place(qkv_pieces + [corner_dp(qkv_pieces)], at_dp)
    head_qkv, normed_all, grad_near = phase((head_qkv, normed_all, grad_out))
    near = permute(grad_near, "seq", 2)
    head_out = place(out_pieces, at_dp)
    projected = (
        jnp.dot(normed_all, head_qkv, preferred_element_type=jnp.float32) + bias_qkv
    ).astype(jnp.bfloat16)
    rot_query, rot_key, context_all, logsum = attention_forward(projected, tables, first)
    out_terms = jnp.dot(context_all, head_out, preferred_element_type=jnp.float32).astype(
        jnp.bfloat16
    )
    out_terms, grad_pieces, near, up_rows = phase((out_terms, grad_pieces, near, up_weight.T))
    attn_out = scatter_seq(out_terms)
    grad_pieces = [grad_out, near, *grad_pieces]
    gate_pieces = gate_pieces + [corner_dp(gate_pieces)]
    up_pieces = near_dp(up_rows)
    mates = permute(jnp.concatenate(grad_pieces, axis=0), "seq", 1)
    mates = jnp.split(mates, chips, axis=0)
    grad_all = place([piece for pair in zip(grad_pieces, mates) for piece in pair], at_seq)
    attn_out, gate_pieces, up_pieces, grad_all, down_rows = phase(
        (attn_out, gate_pieces, up_pieces, grad_all, down_weight)
    )
    resid_mid, normed_mlp = middle_norm(resid_in, attn_out, gain_mlp, bias_mlp)
    rows_all = gather_seq(normed_mlp)
    up_pieces = up_pieces + [corner_dp(up_pieces)]
    down_pieces = near_dp(down_rows)
    down_pieces, up_pieces = phase((down_pieces, up_pieces))
    cols_down = jnp.concatenate(down_pieces + [corner_dp(down_pieces)], axis=0)
    cols_gate = jnp.concatenate(gate_pieces, axis=0)
    cols_up = jnp.concatenate(up_pieces, axis=0)
    grad_hidden = contract(grad_all, cols_down, 1, 1)
    rows_all, cols_down, cols_gate, cols_up, grad_hidden = phase(
        (rows_all, cols_down, cols_gate, cols_up, grad_hidden)
    )
    gate_values = contract(rows_all, cols_gate, 1, 1)
    up_values = contract(rows_all, cols_up, 1, 1)
    hidden = (jax.nn.silu(gate_values) * up_values).astype(jnp.bfloat16)
    grad_gate, grad_up = gate_backward(gate_values, up_values, grad_hidden)
    grad_rows = (
        contract(grad_gate, cols_gate, 1, 0) + contract(grad_up, cols_up, 1, 0)
    ).astype(jnp.bfloat16)
    grad_rows, grad_gate, grad_up, hidden = phase((grad_rows, grad_gate, grad_up, hidden))
    grad_normed_mlp = scatter_seq(grad_rows)
    gate_terms = jnp.split(
        contract(grad_gate, rows_all, 0, 0).astype(jnp.bfloat16), rows, axis=0
    )
    gate_corner = send_corner(gate_terms)
    mlp_terms = contract(hidden, cols_down, 1, 0).astype(jnp.bfloat16)
    up_terms = contract(grad_up, rows_all, 0, 0).astype(jnp.bfloat16)
    gate_corner, gate_terms, mlp_terms, up_terms = phase(
        (gate_corner, gate_terms, mlp_terms, up_terms)
    )
    gate_near = send_near(gate_terms, gate_corner)
    down_terms = contract(hidden, grad_all, 0, 0).astype(jnp.bfloat16)
    grad_normed_mlp, gate_near, up_terms, mlp_terms, down_terms = phase(
        (grad_normed_mlp, gate_near, up_terms, mlp_terms, down_terms)
    )
    grad_mid, grad_branch, mlp_norm_sums = branch_norm(
        grad_out, grad_normed_mlp, resid_mid, gain_mlp
    )
    branch_all = gather_seq(grad_branch)
    up_terms = jnp.split(up_terms, rows, axis=0)
    down_terms = jnp.split(down_terms, rows, axis=0)
    up_corner = send_corner(up_terms)
    up_corner, up_terms, down_terms = phase((up_corner, up_terms, down_terms))
    up_near = send_near(up_terms, up_corner)
    down_corner = send_corner(down_terms)
    down_terms = down_terms[:1] + add_corner(down_terms, down_corner)
    branch_all, up_near, mlp_terms, down_terms = phase(
        (branch_all, up_near, mlp_terms, down_terms)
    )
    mlp_out = scatter_seq(mlp_terms)
    down_near = [permute(down_terms[1], "dp", 1), permute(down_terms[2], "dp", 2)]
    grad_heads = contract(branch_all, head_out, 1, 1).astype(jnp.bfloat16)
    grad_stack = attention_backward(
        rot_query, rot_key, projected, grad_heads, logsum, tables, first
    )
    grad_stack, down_near = phase((grad_stack, down_near))
    slice_terms = contract(normed_all, grad_stack, 0, 0).astype(jnp.bfloat16)
    slice_pieces = dp_terms(slice_terms)
    grad_stack, slice_pieces = phase((grad_stack, slice_pieces))
    slice_near = [permute(slice_pieces[k], "dp", k) for k in range(1, rows - 1)]
    attn_terms = contract(grad_stack, head_qkv, 1, 1).astype(jnp.bfloat16)
    sums = norm_sums(input_all, attn_terms, lang_row, gain_attn)
    attn_terms, sums, slice_near, slice_pieces, branch_all, up_near, gate_near, grad_stack = phase(
        (attn_terms, sums, slice_near, slice_pieces, branch_all, up_near, gate_near, grad_stack)
    )
    grad_normed_attn = scatter_seq(attn_terms)
    slice_far = permute(slice_pieces[-1], "dp", rows - 1)
    grad_bias_qkv = jnp.sum(grad_stack.astype(jnp.float32), axis=0).reshape(3, local_width)
    terms = jnp.concatenate(
        [
            sums[:2],
            mlp_norm_sums,
            from_heads(grad_bias_qkv),
            chooser[:, None] * (jnp.sum(grad_mid, axis=0) + sums[2])[None],
        ],
        axis=0,
    )
    count = terms.shape[0]

    def small_parts(values, index):
        return [
            lax.dynamic_index_in_dim(values, index ^ k, 0, keepdims=False)
            for k in range(values.shape[0])
        ]

    def small_sum(parts, axis):
        return total([parts[0]] + [permute(parts[k], axis, k) for k in range(1, len(parts))])

    terms = small_parts(terms.reshape(count, rows, groups, own).transpose(1, 2, 0, 3), at_dp)
    terms = small_parts(small_sum(terms, "dp"), at_seq)
    out_pieces = dp_terms(contract(context_all, branch_all, 0, 0).astype(jnp.bfloat16))
    terms, slice_far, mlp_out, out_pieces, down_near, up_near, gate_near = phase(
        (terms, slice_far, mlp_out, out_pieces, down_near, up_near, gate_near)
    )
    home = (
        total([slice_pieces[0], *slice_near, slice_far])
        .astype(jnp.bfloat16)
        .reshape(groups, own, 3 * local_width)
    )
    home, terms, out_pieces, down_near, up_near, gate_near = phase(
        (home, terms, out_pieces, down_near, up_near, gate_near)
    )
    home = lax.all_to_all(home, "seq", split_axis=0, concat_axis=0, tiled=True)
    out_arrived = [permute(out_pieces[k], "dp", k) for k in range(1, rows)]
    summed = small_sum(terms, "seq")
    home, out_arrived, summed = phase((home, out_arrived, summed))
    out_proj = total([out_pieces[0], *out_arrived])
    out_gate = total([gate_terms[0], *gate_near])
    out_up = total([up_terms[0], *up_near])
    out_down = total([down_terms[0], *down_near])
    if whole_heads and rows % 2 == 0:
        grad_qkv_out = columns_in_place([home], rows)
    else:
        grad_qkv_out = (
            home.reshape(groups, own, 3, deal[0], deal[2])
            .transpose(1, 2, 3, 0, 4)
            .reshape(own, 3 * D)
            .astype(jnp.float32)
        )
    if not whole_heads:
        out_proj = lax.ppermute(out_proj, ("dp", "seq"), owner)
    layer_output = (resid_mid + mlp_out).astype(jnp.bfloat16)
    grad_normed_attn, grad_qkv_out, out_proj, out_gate, out_up, out_down, layer_output = phase(
        (grad_normed_attn, grad_qkv_out, out_proj, out_gate, out_up, out_down, layer_output)
    )
    grad_input = branch_norm(grad_mid, grad_normed_attn, resid_in, gain_attn)[0]
    return (
        layer_output[None],
        grad_input[None],
        summed[7:],
        summed[0],
        summed[1],
        grad_qkv_out,
        summed[4:7],
        out_proj,
        summed[2],
        summed[3],
        out_gate.T,
        out_up.T,
        out_down,
    )


def solution(mesh):
    placed = (
        P("dp", "seq", None),
        P("dp", None),
        P("dp"),
        P(None, ("dp", "seq")),
        P(("dp", "seq")),
        P(("dp", "seq")),
        P(("dp", "seq"), None),
        P(None, ("dp", "seq")),
        P(("dp", "seq"), None),
        P(("dp", "seq")),
        P(("dp", "seq")),
        P(None, ("dp", "seq")),
        P(None, ("dp", "seq")),
        P(("dp", "seq"), None),
        P("dp", "seq", None),
    )
    return jax.shard_map(
        per_device,
        mesh=mesh,
        in_specs=placed,
        out_specs=(
            P("dp", "seq", None),
            P("dp", "seq", None),
            P(None, ("dp", "seq")),
            P(("dp", "seq")),
            P(("dp", "seq")),
            P(("dp", "seq"), None),
            P(None, ("dp", "seq")),
            P(("dp", "seq"), None),
            P(("dp", "seq")),
            P(("dp", "seq")),
            P(None, ("dp", "seq")),
            P(None, ("dp", "seq")),
            P(("dp", "seq"), None),
        ),
        check_vma=False,
    )
```

```python
import jax
import jax.numpy as jnp
from jax import lax
from jax.experimental import pallas as pl
from jax.experimental.pallas import tpu as pltpu
from jax.sharding import PartitionSpec as P

D = 2048
HEADS = 32
HEAD = 64
ROT = 16
LANGS = 7


EPS = 1e-05
BASE = 10000.0
NEG = -1e30


def contract(left, right, left_dim, right_dim):
    return lax.dot_general(
        left, right, (((left_dim,), (right_dim,)), ((), ())), preferred_element_type=jnp.float32
    )


def norm_forward(values, gain, bias):
    average = jnp.mean(values, axis=-1, keepdims=True)
    centered = values - average
    variance = jnp.mean(centered * centered, axis=-1, keepdims=True)
    inverse = lax.rsqrt(variance + EPS)
    scaled = centered * inverse
    return (scaled * gain + bias, scaled, inverse)


def norm_backward(grad_normed, scaled, inverse, gain):
    grad_scaled = grad_normed * gain
    grad_values = inverse * (
        grad_scaled
        - jnp.mean(grad_scaled, axis=-1, keepdims=True)
        - scaled * jnp.mean(grad_scaled * scaled, axis=-1, keepdims=True)
    )
    return (grad_values, jnp.sum(grad_normed * scaled, axis=0), jnp.sum(grad_normed, axis=0))


def row_tables(doc_lengths, length):
    ends = jnp.cumsum(doc_lengths)
    starts = ends - doc_lengths
    places = jnp.arange(length, dtype=jnp.int32)
    segment = jnp.sum((places[:, None] >= ends[None, :]).astype(jnp.int32), axis=1)
    member = segment[:, None] == jnp.arange(ends.shape[0], dtype=jnp.int32)[None, :]
    offsets = jnp.sum(jnp.where(member, starts[None, :], 0), axis=1)
    position = (places - offsets).astype(jnp.float32)
    half_rot = ROT // 2
    freq = BASE ** (-(2.0 * jnp.arange(half_rot, dtype=jnp.float32)) / ROT)
    angles = position[:, None] * freq[None, :]
    return (offsets, jnp.cos(angles), jnp.sin(angles))


def head_lanes(shape, dim, head):
    place = lax.broadcasted_iota(jnp.int32, shape, dim)
    return (place >= head * HEAD) & (place < (head + 1) * HEAD)


def turn(values, tables, direction):
    lanes = values.shape[1]
    cosines, sines_former, sines_latter = tables
    after = pltpu.roll(values, lanes - ROT // 2, 1)
    before = pltpu.roll(values, ROT // 2, 1)
    return values * cosines + direction * (before * sines_latter - after * sines_former)


def allowed_pairs(first_ref, start, block, keys):
    key_at = lax.broadcasted_iota(jnp.int32, (keys, block), 0)
    query_at = start + lax.broadcasted_iota(jnp.int32, (keys, block), 1)
    return (key_at >= first_ref[:, pl.ds(start, block)]) & (key_at <= query_at)


def over_blocks(length, block, step):
    count = length // block
    if count <= 8:
        for i in range(count):
            step(i * block, (i + 1) * block)
    else:

        def body(i, carry):
            step(pl.multiple_of(i * block, block), length)
            return carry

        lax.fori_loop(0, count, body, 0)


def forward_kernel(
    qkv_ref, cos_ref, former_ref, latter_ref, first_ref,
    query_ref, key_ref, context_ref, logsum_ref, value_t,
):
    length, width = query_ref.shape
    lanes = cos_ref.shape[1]
    block = min(128, length)
    tables = (cos_ref[...], former_ref[...], latter_ref[...])
    for group in range(width // lanes):
        part = slice(group * lanes, (group + 1) * lanes)

        def columns(c):
            begin = c * width + group * lanes
            return qkv_ref[:, begin : begin + lanes].astype(jnp.float32)

        query_ref[:, part] = turn(columns(0), tables, 1.0).astype(jnp.bfloat16)
        key_ref[:, part] = turn(columns(1), tables, 1.0).astype(jnp.bfloat16)
        value_t[...] = columns(2).T.astype(jnp.bfloat16)

        def step(start, keys):
            queries = query_ref[pl.ds(start, block), part].astype(jnp.float32) * HEAD ** (-0.5)
            allowed = allowed_pairs(first_ref, start, block, keys)
            found = []
            for head in range(lanes // HEAD):
                own = jnp.where(head_lanes(queries.shape, 1, head), queries, 0.0)
                scores = contract(key_ref[0:keys, part], own.astype(jnp.bfloat16), 1, 1)
                scores = jnp.where(allowed, scores, NEG)
                most = jnp.max(scores, axis=0, keepdims=True)
                weights = jnp.exp(scores - most)
                total = jnp.sum(weights, axis=0, keepdims=True)
                probs = (weights * (1.0 / total)).astype(jnp.bfloat16)
                logsum_ref[
                    pl.ds(group * (lanes // HEAD) + head, 1), pl.ds(start, block)
                ] = most + jnp.log(total)
                context = contract(value_t[:, 0:keys], probs, 1, 0)
                found.append(context[head * HEAD : (head + 1) * HEAD])
            context_ref[pl.ds(start, block), part] = (
                jnp.concatenate(found, axis=0).T.astype(jnp.bfloat16)
            )

        over_blocks(length, block, step)


def backward_kernel(
    query_ref, key_ref, qkv_ref, context_grad_ref, logsum_ref, cos_ref, former_ref, latter_ref,
    first_ref, grad_ref, key_t, grad_query, grad_key, grad_value,
):
    length, width = query_ref.shape
    lanes = cos_ref.shape[1]
    block = min(128, length)
    scale = HEAD ** (-0.5)
    tables = (cos_ref[...], former_ref[...], latter_ref[...])
    for group in range(width // lanes):
        part = slice(group * lanes, (group + 1) * lanes)
        value_part = slice(2 * width + group * lanes, 2 * width + (group + 1) * lanes)
        key_t[...] = key_ref[:, part].astype(jnp.float32).T.astype(jnp.bfloat16)
        grad_key[...] = jnp.zeros_like(grad_key)
        grad_value[...] = jnp.zeros_like(grad_value)

        def step(start, keys):
            queries = query_ref[pl.ds(start, block), part].astype(jnp.float32) * scale
            grads = context_grad_ref[pl.ds(start, block), part].astype(jnp.float32)
            allowed = allowed_pairs(first_ref, start, block, keys)
            found = []
            for head in range(lanes // HEAD):
                mine = head_lanes(queries.shape, 1, head)
                own_query = jnp.where(mine, queries, 0.0).astype(jnp.bfloat16)
                own_grad = jnp.where(mine, grads, 0.0).astype(jnp.bfloat16)
                scores = contract(key_ref[0:keys, part], own_query, 1, 1)
                logsum = logsum_ref[
                    pl.ds(group * (lanes // HEAD) + head, 1), pl.ds(start, block)
                ]
                soft = jnp.exp(jnp.where(allowed, scores, NEG) - logsum)
                grad_soft = contract(qkv_ref[0:keys, value_part], own_grad, 1, 1)
                weighed = soft * grad_soft
                delta = jnp.sum(weighed, axis=0, keepdims=True)
                grad_scores = (weighed - soft * delta).astype(jnp.bfloat16)
                grad_value[0:keys] += contract(soft.astype(jnp.bfloat16), own_grad, 1, 0)
                grad_key[0:keys] += contract(grad_scores, own_query, 1, 0)
                turned = contract(key_t[:, 0:keys], grad_scores, 1, 0)
                found.append(turned[head * HEAD : (head + 1) * HEAD])
            grad_query[pl.ds(start, block), :] = jnp.concatenate(found, axis=0).T * scale

        over_blocks(length, block, step)
        for c, grads in ((0, grad_query), (1, grad_key)):
            begin = c * width + group * lanes
            grad_ref[:, begin : begin + lanes] = turn(grads[...], tables, -1.0).astype(
                jnp.bfloat16
            )
        grad_ref[:, value_part] = grad_value[...].astype(jnp.bfloat16)


def columns_kernel(part_refs, out_ref, deal, width):
    row = 0
    for ref in part_refs:
        groups, rows = ref.shape[0], ref.shape[1]
        for c in range(3):
            for d in range(0, deal, 2):
                for s in range(0, groups, 2):
                    begin = c * deal * HEAD + d * HEAD
                    left = ref[s, :, begin : begin + 2 * HEAD].astype(jnp.float32)
                    right = ref[s + 1, :, begin : begin + 2 * HEAD].astype(jnp.float32)
                    lower = lax.broadcasted_iota(jnp.int32, left.shape, 1) < HEAD
                    out = c * width + d * groups * HEAD + s * HEAD
                    out_ref[row : row + rows, out : out + 2 * HEAD] = jnp.where(
                        lower, left, pltpu.roll(right, HEAD, 1)
                    )
                    out = out + groups * HEAD
                    out_ref[row : row + rows, out : out + 2 * HEAD] = jnp.where(
                        lower, pltpu.roll(left, HEAD, 1), right
                    )
        row += rows


def columns_in_place(parts, deal):
    rows = sum(part.shape[1] for part in parts)
    width = parts[0].shape[0] * deal * HEAD

    def kernel(*refs):
        columns_kernel(refs[:-1], refs[-1], deal, width)

    return pl.pallas_call(
        kernel,
        out_shape=jax.ShapeDtypeStruct((rows, 3 * width), jnp.float32),
        compiler_params=pltpu.CompilerParams(vmem_limit_bytes=VMEM_BYTES),
        name="columns_in_place",
    )(*parts)


def deal_kernel(weight_ref, riders_ref, out_ref, deal):
    groups = out_ref.shape[0]
    rows, width = weight_ref.shape[0], weight_ref.shape[1] // 3
    for c in range(3):
        for d in range(0, deal, 2):
            for s in range(0, groups, 2):
                begin = c * width + d * groups * HEAD + s * HEAD
                upper = weight_ref[:, begin : begin + 2 * HEAD].astype(jnp.float32)
                begin = begin + groups * HEAD
                after = weight_ref[:, begin : begin + 2 * HEAD].astype(jnp.float32)
                lower = lax.broadcasted_iota(jnp.int32, upper.shape, 1) < HEAD
                out = c * deal * HEAD + d * HEAD
                out_ref[s, 0:rows, out : out + 2 * HEAD] = jnp.where(
                    lower, upper, pltpu.roll(after, HEAD, 1)
                ).astype(jnp.bfloat16)
                out_ref[s + 1, 0:rows, out : out + 2 * HEAD] = jnp.where(
                    lower, pltpu.roll(upper, HEAD, 1), after
                ).astype(jnp.bfloat16)
    for s in range(groups):
        out_ref[s, rows:, :] = riders_ref[...]


def deal_columns(weight, riders, groups, deal):
    def kernel(*refs):
        deal_kernel(*refs, deal)

    return pl.pallas_call(
        kernel,
        out_shape=jax.ShapeDtypeStruct(
            (groups, weight.shape[0] + riders.shape[0], riders.shape[1]), jnp.bfloat16
        ),
        compiler_params=pltpu.CompilerParams(vmem_limit_bytes=VMEM_BYTES),
        name="deal_columns",
    )(weight, riders)


SMALL_COST = pl.CostEstimate(flops=1, bytes_accessed=1, transcendentals=1)


def middle_kernel(resid_ref, terms_ref, gain_ref, bias_ref, sum_ref, normed_ref):
    values = resid_ref[...] + terms_ref[...].astype(jnp.float32)
    sum_ref[...] = values
    normed_ref[...] = norm_forward(values, gain_ref[...], bias_ref[...])[0].astype(jnp.bfloat16)


def middle_norm(resid, terms, gain, bias):
    return pl.pallas_call(
        middle_kernel,
        out_shape=(
            jax.ShapeDtypeStruct(resid.shape, jnp.float32),
            jax.ShapeDtypeStruct(resid.shape, jnp.bfloat16),
        ),
        compiler_params=pltpu.CompilerParams(vmem_limit_bytes=VMEM_BYTES),
        cost_estimate=SMALL_COST,
        name="middle_norm",
    )(resid, terms, gain[None], bias[None])


def branch_kernel(base_ref, terms_ref, values_ref, gain_ref, grad_ref, branch_ref, sums_ref):
    unused, scaled, inverse = norm_forward(values_ref[...], 1.0, 0.0)
    grad_values, gain_sum, bias_sum = norm_backward(
        terms_ref[...].astype(jnp.float32), scaled, inverse, gain_ref[...]
    )
    grads = base_ref[...].astype(jnp.float32) + grad_values
    grad_ref[...] = grads
    branch_ref[...] = grads.astype(jnp.bfloat16)
    sums_ref[0:1] = gain_sum[None]
    sums_ref[1:2] = bias_sum[None]


def branch_norm(base, terms, values, gain):
    return pl.pallas_call(
        branch_kernel,
        out_shape=(
            jax.ShapeDtypeStruct(values.shape, jnp.float32),
            jax.ShapeDtypeStruct(values.shape, jnp.bfloat16),
            jax.ShapeDtypeStruct((2, values.shape[1]), jnp.float32),
        ),
        compiler_params=pltpu.CompilerParams(vmem_limit_bytes=VMEM_BYTES),
        cost_estimate=SMALL_COST,
        name="branch_norm",
    )(base, terms, values, gain[None])


def norm_sums_kernel(values_ref, terms_ref, lang_ref, gain_ref, out_ref):
    @pl.when(pl.program_id(0) == 0)
    def clear():
        out_ref[...] = jnp.zeros_like(out_ref)

    values = values_ref[...].astype(jnp.float32) + lang_ref[...]
    terms = terms_ref[...].astype(jnp.float32)
    unused, scaled, inverse = norm_forward(values, 1.0, 0.0)
    grad_values, gain_sum, bias_sum = norm_backward(terms, scaled, inverse, gain_ref[...])
    out_ref[0:1] += gain_sum[None]
    out_ref[1:2] += bias_sum[None]
    out_ref[2:3] += jnp.sum(grad_values, axis=0, keepdims=True)


def norm_sums(values, terms, lang_row, gain):
    length, width = values.shape
    block = min(256, length)
    rows = pl.BlockSpec((block, width), lambda i: (i, 0))
    whole = pl.BlockSpec((1, width), lambda i: (0, 0))
    return pl.pallas_call(
        norm_sums_kernel,
        grid=(length // block,),
        in_specs=[rows, rows, whole, whole],
        out_specs=pl.BlockSpec((8, width), lambda i: (0, 0)),
        out_shape=jax.ShapeDtypeStruct((8, width), jnp.float32),
        compiler_params=pltpu.CompilerParams(vmem_limit_bytes=VMEM_BYTES),
        cost_estimate=SMALL_COST,
        name="norm_sums",
    )(values, terms, lang_row, gain[None])


def rotation_tables(cosines, sines, lanes):
    length = cosines.shape[0]
    rest = jnp.ones((length, HEAD - ROT), jnp.float32)
    none = jnp.zeros_like(sines)
    heads = lanes // HEAD
    return (
        jnp.tile(jnp.concatenate([cosines, cosines, rest], axis=1), (1, heads)),
        jnp.tile(jnp.concatenate([sines, none, 0.0 * rest], axis=1), (1, heads)),
        jnp.tile(jnp.concatenate([none, sines, 0.0 * rest], axis=1), (1, heads)),
    )


VMEM_BYTES = 48 * 1024 * 1024


def attention_forward(projected, tables, first):
    length, width = projected.shape[0], projected.shape[1] // 3
    lanes = tables[0].shape[1]
    rows = jax.ShapeDtypeStruct((length, width), jnp.bfloat16)
    return pl.pallas_call(
        forward_kernel,
        out_shape=(
            rows,
            rows,
            rows,
            jax.ShapeDtypeStruct((width // HEAD, length), jnp.float32),
        ),
        scratch_shapes=[pltpu.VMEM((lanes, length), jnp.bfloat16)],
        compiler_params=pltpu.CompilerParams(vmem_limit_bytes=VMEM_BYTES),
        cost_estimate=SMALL_COST,
        name="attention_forward",
    )(projected, *tables, first)


def attention_backward(queries, key_heads, projected, grad_context, logsum, tables, first):
    length, width = queries.shape
    lanes = tables[0].shape[1]
    return pl.pallas_call(
        backward_kernel,
        out_shape=jax.ShapeDtypeStruct((length, 3 * width), jnp.bfloat16),
        scratch_shapes=[
            pltpu.VMEM((lanes, length), jnp.bfloat16),
            pltpu.VMEM((length, lanes), jnp.float32),
            pltpu.VMEM((length, lanes), jnp.float32),
            pltpu.VMEM((length, lanes), jnp.float32),
        ],
        compiler_params=pltpu.CompilerParams(vmem_limit_bytes=VMEM_BYTES),
        cost_estimate=SMALL_COST,
        name="attention_backward",
    )(queries, key_heads, projected, grad_context, logsum, *tables, first)


def gate_backward(gate_values, up_values, grad_hidden):
    sigmoid_gate = jax.nn.sigmoid(gate_values)
    silu_gate = gate_values * sigmoid_gate
    grad_gate = (
        grad_hidden * up_values * sigmoid_gate * (1.0 + gate_values * (1.0 - sigmoid_gate))
    ).astype(jnp.bfloat16)
    grad_up = (grad_hidden * silu_gate).astype(jnp.bfloat16)
    return (grad_gate, grad_up)


def permute(value, axis, offset):
    size = lax.axis_size(axis)
    return lax.ppermute(value, axis, [(i, i ^ offset) for i in range(size)])


def gather_dp(piece):
    return [piece] + [permute(piece, "dp", k) for k in range(1, lax.axis_size("dp"))]


def scatter_dp(pieces):
    return total([pieces[0]] + [permute(pieces[k], "dp", k) for k in range(1, len(pieces))])


def near_dp(piece):
    return [piece, permute(piece, "dp", 1), permute(piece, "dp", 2)]


def corner_dp(pieces):
    middle = pieces[0].shape[0] // 2
    return jnp.concatenate(
        [permute(pieces[2][:middle], "dp", 1), permute(pieces[1][middle:], "dp", 2)], axis=0
    )


def send_corner(pieces):
    middle = pieces[0].shape[0] // 2
    return (permute(pieces[3][:middle], "dp", 2), permute(pieces[3][middle:], "dp", 1))


def add_corner(pieces, corner):
    middle = pieces[0].shape[0] // 2
    first = total([pieces[1][:middle], corner[0]]).astype(jnp.bfloat16)
    second = total([pieces[2][middle:], corner[1]]).astype(jnp.bfloat16)
    return [
        jnp.concatenate([first, pieces[1][middle:]], axis=0),
        jnp.concatenate([pieces[2][:middle], second], axis=0),
    ]


def send_near(pieces, corner):
    first, second = add_corner(pieces, corner)
    return [permute(first, "dp", 1), permute(second, "dp", 2)]


def total(parts):
    result = parts[0].astype(jnp.float32)
    for piece in parts[1:]:
        result = result + piece.astype(jnp.float32)
    return result


def gather_seq(piece):
    return lax.all_gather(piece, "seq", axis=0, tiled=True)


def scatter_seq(terms):
    return lax.psum_scatter(
        terms.astype(jnp.bfloat16), "seq", scatter_dimension=0, tiled=True
    )


def after(value, *others):
    return lax.optimization_barrier((value,) + others)[0]


def place(pieces, index):
    block = pieces[0].shape[0]
    result = jnp.zeros((block * len(pieces),) + pieces[0].shape[1:], pieces[0].dtype)
    for k, piece in enumerate(pieces):
        result = lax.dynamic_update_slice_in_dim(result, piece, (index ^ k) * block, 0)
    return result


def per_device(
    layer_input,
    doc_lengths,
    language,
    lang_table,
    attn_norm_gain,
    attn_norm_bias,
    qkv_weight,
    qkv_bias,
    out_weight,
    mlp_norm_gain,
    mlp_norm_bias,
    gate_weight,
    up_weight,
    down_weight,
    cotangent,
):
    tokens = layer_input.shape[1]
    groups = lax.axis_size("seq")
    rows = lax.axis_size("dp")
    devices = rows * groups
    at_dp = lax.axis_index("dp")
    at_seq = lax.axis_index("seq")
    length = tokens * groups
    heads_here = HEADS // groups
    local_width = heads_here * HEAD
    own = D // devices
    whole_heads = own % HEAD == 0
    deal = (rows, groups, own) if whole_heads else (1, groups, local_width)
    at_deal = (0, 0, at_seq, 0)
    owner = [(i, (i % groups) * rows + i // groups) for i in range(devices)]
    back = [(b, a) for a, b in owner]

    def to_heads(values):
        count = values.shape[0]
        return lax.dynamic_slice(
            values.reshape((count,) + deal), at_deal, (count, deal[0], 1, deal[2])
        ).reshape(count, local_width)

    def from_heads(values):
        count = values.shape[0]
        return lax.dynamic_update_slice(
            jnp.zeros((count,) + deal, values.dtype),
            values.reshape(count, deal[0], 1, deal[2]),
            at_deal,
        ).reshape(count, D)

    phase = lax.optimization_barrier
    grad_out = cotangent[0]

    def dp_terms(terms):
        block = terms.shape[0] // rows
        return [
            lax.dynamic_slice_in_dim(terms, (at_dp ^ k) * block, block, 0) for k in range(rows)
        ]

    small = jnp.concatenate(
        [
            lang_table,
            attn_norm_gain[None],
            attn_norm_bias[None],
            mlp_norm_gain[None],
            mlp_norm_bias[None],
            qkv_bias,
        ],
        axis=0,
    )
    ride = 16
    riders = jnp.zeros((ride * 3 * local_width,), jnp.bfloat16)
    riders = lax.dynamic_update_slice(riders, small.reshape(-1), (0,))
    riders = riders.reshape(ride, 3 * local_width)
    if whole_heads and rows % 2 == 0:
        dealt = deal_columns(qkv_weight, riders, groups, rows)
    else:
        dealt = jnp.concatenate(
            [
                qkv_weight.reshape((own, 3) + deal)
                .transpose(3, 0, 1, 2, 4)
                .reshape(groups, own, 3 * local_width),
                jnp.broadcast_to(riders[None], (groups,) + riders.shape),
            ],
            axis=1,
        )
    part = lax.all_to_all(dealt, "seq", split_axis=0, concat_axis=0, tiled=True)
    out_rows = out_weight if whole_heads else lax.ppermute(out_weight, ("dp", "seq"), back)
    out_pieces = gather_dp(out_rows)
    gate_pieces = near_dp(gate_weight.T)
    part, out_pieces, gate_pieces = phase((part, out_pieces, gate_pieces))
    chips = groups // 2
    input_all = gather_seq(layer_input[0])
    spread = place(gather_dp(part[:, own:].reshape(groups, -1)), at_dp)
    qkv_pieces = near_dp(part[:, :own].reshape(groups * own, 3 * local_width))
    input_all, spread, grad_far = phase((input_all, spread, grad_out))
    grad_pieces = [permute(grad_far, "seq", 2 * k) for k in range(2, chips)]
    spread = spread[:, : small.size].reshape((devices,) + small.shape)
    table = jnp.swapaxes(spread, 0, 1).reshape(small.shape[0], D).astype(jnp.float32)
    gain_attn = table[LANGS]
    bias_attn = table[LANGS + 1]
    gain_mlp = table[LANGS + 2]
    bias_mlp = table[LANGS + 3]
    bias_qkv = to_heads(table[LANGS + 4 : LANGS + 7]).reshape(3 * local_width)
    chooser = (jnp.arange(LANGS, dtype=jnp.int32) == language[0]).astype(jnp.float32)
    lang_row = jnp.sum(chooser[:, None] * table[:LANGS], axis=0)[None, :]
    offsets, cosines, sines = row_tables(doc_lengths[0], length)
    tables = rotation_tables(cosines, sines, min(128, local_width))
    first = offsets[None, :]
    resid_in = layer_input[0].astype(jnp.float32) + lang_row
    normed_all = norm_forward(input_all.astype(jnp.float32) + lang_row, gain_attn, bias_attn)[
        0
    ].astype(jnp.bfloat16)
    qkv_pieces, tables, first, resid_in = phase((qkv_pieces, tables, first, resid_in))
    head_qkv = place(qkv_pieces + [corner_dp(qkv_pieces)], at_dp)
    head_qkv, normed_all, grad_near = phase((head_qkv, normed_all, grad_out))
    near = permute(grad_near, "seq", 2)
    head_out = place(out_pieces, at_dp)
    projected = (
        jnp.dot(normed_all, head_qkv, preferred_element_type=jnp.float32) + bias_qkv
    ).astype(jnp.bfloat16)
    rot_query, rot_key, context_all, logsum = attention_forward(projected, tables, first)
    out_terms = jnp.dot(context_all, head_out, preferred_element_type=jnp.float32).astype(
        jnp.bfloat16
    )
    out_terms, grad_pieces, near, up_rows = phase((out_terms, grad_pieces, near, up_weight.T))
    attn_out = scatter_seq(out_terms)
    grad_pieces = [grad_out, near, *grad_pieces]
    gate_pieces = gate_pieces + [corner_dp(gate_pieces)]
    up_pieces = near_dp(up_rows)
    mates = permute(jnp.concatenate(grad_pieces, axis=0), "seq", 1)
    mates = jnp.split(mates, chips, axis=0)
    grad_all = place([piece for pair in zip(grad_pieces, mates) for piece in pair], at_seq)
    attn_out, gate_pieces, up_pieces, grad_all, down_rows = phase(
        (attn_out, gate_pieces, up_pieces, grad_all, down_weight)
    )
    resid_mid, normed_mlp = middle_norm(resid_in, attn_out, gain_mlp, bias_mlp)
    rows_all = gather_seq(normed_mlp)
    up_pieces = up_pieces + [corner_dp(up_pieces)]
    down_pieces = near_dp(down_rows)
    down_pieces, up_pieces = phase((down_pieces, up_pieces))
    cols_down = jnp.concatenate(down_pieces + [corner_dp(down_pieces)], axis=0)
    cols_gate = jnp.concatenate(gate_pieces, axis=0)
    cols_up = jnp.concatenate(up_pieces, axis=0)
    grad_hidden = contract(grad_all, cols_down, 1, 1)
    rows_all, cols_down, cols_gate, cols_up, grad_hidden = phase(
        (rows_all, cols_down, cols_gate, cols_up, grad_hidden)
    )
    gate_values = contract(rows_all, cols_gate, 1, 1)
    up_values = contract(rows_all, cols_up, 1, 1)
    hidden = (jax.nn.silu(gate_values) * up_values).astype(jnp.bfloat16)
    grad_gate, grad_up = gate_backward(gate_values, up_values, grad_hidden)
    grad_rows = (
        contract(grad_gate, cols_gate, 1, 0) + contract(grad_up, cols_up, 1, 0)
    ).astype(jnp.bfloat16)
    grad_rows, grad_gate, grad_up, hidden = phase((grad_rows, grad_gate, grad_up, hidden))
    grad_normed_mlp = scatter_seq(grad_rows)
    gate_terms = jnp.split(
        contract(grad_gate, rows_all, 0, 0).astype(jnp.bfloat16), rows, axis=0
    )
    gate_corner = send_corner(gate_terms)
    mlp_terms = contract(hidden, cols_down, 1, 0).astype(jnp.bfloat16)
    up_terms = contract(grad_up, rows_all, 0, 0).astype(jnp.bfloat16)
    gate_corner, gate_terms, mlp_terms, up_terms = phase(
        (gate_corner, gate_terms, mlp_terms, up_terms)
    )
    gate_near = send_near(gate_terms, gate_corner)
    down_terms = contract(hidden, grad_all, 0, 0).astype(jnp.bfloat16)
    grad_normed_mlp, gate_near, up_terms, mlp_terms, down_terms = phase(
        (grad_normed_mlp, gate_near, up_terms, mlp_terms, down_terms)
    )
    grad_mid, grad_branch, mlp_norm_sums = branch_norm(
        grad_out, grad_normed_mlp, resid_mid, gain_mlp
    )
    branch_all = gather_seq(grad_branch)
    up_terms = jnp.split(up_terms, rows, axis=0)
    down_terms = jnp.split(down_terms, rows, axis=0)
    up_corner = send_corner(up_terms)
    up_corner, up_terms, down_terms = phase((up_corner, up_terms, down_terms))
    up_near = send_near(up_terms, up_corner)
    down_corner = send_corner(down_terms)
    down_terms = down_terms[:1] + add_corner(down_terms, down_corner)
    branch_all, up_near, mlp_terms, down_terms = phase(
        (branch_all, up_near, mlp_terms, down_terms)
    )
    mlp_out = scatter_seq(mlp_terms)
    down_near = [permute(down_terms[1], "dp", 1), permute(down_terms[2], "dp", 2)]
    grad_heads = contract(branch_all, head_out, 1, 1).astype(jnp.bfloat16)
    grad_stack = attention_backward(
        rot_query, rot_key, projected, grad_heads, logsum, tables, first
    )
    grad_stack, down_near = phase((grad_stack, down_near))
    slice_terms = contract(normed_all, grad_stack, 0, 0).astype(jnp.bfloat16)
    slice_pieces = dp_terms(slice_terms)
    grad_stack, slice_pieces = phase((grad_stack, slice_pieces))
    slice_near = [permute(slice_pieces[k], "dp", k) for k in range(1, rows - 1)]
    attn_terms = contract(grad_stack, head_qkv, 1, 1).astype(jnp.bfloat16)
    sums = norm_sums(input_all, attn_terms, lang_row, gain_attn)
    attn_terms, sums, slice_near, slice_pieces, branch_all, up_near, gate_near, grad_stack = phase(
        (attn_terms, sums, slice_near, slice_pieces, branch_all, up_near, gate_near, grad_stack)
    )
    grad_normed_attn = scatter_seq(attn_terms)
    slice_far = permute(slice_pieces[-1], "dp", rows - 1)
    grad_bias_qkv = jnp.sum(grad_stack.astype(jnp.float32), axis=0).reshape(3, local_width)
    terms = jnp.concatenate(
        [
            sums[:2],
            mlp_norm_sums,
            from_heads(grad_bias_qkv),
            chooser[:, None] * (jnp.sum(grad_mid, axis=0) + sums[2])[None],
        ],
        axis=0,
    )
    count = terms.shape[0]

    def small_parts(values, index):
        return [
            lax.dynamic_index_in_dim(values, index ^ k, 0, keepdims=False)
            for k in range(values.shape[0])
        ]

    def small_sum(parts, axis):
        return total([parts[0]] + [permute(parts[k], axis, k) for k in range(1, len(parts))])

    terms = small_parts(terms.reshape(count, rows, groups, own).transpose(1, 2, 0, 3), at_dp)
    terms = small_parts(small_sum(terms, "dp"), at_seq)
    out_pieces = dp_terms(contract(context_all, branch_all, 0, 0).astype(jnp.bfloat16))
    terms, slice_far, mlp_out, out_pieces, down_near, up_near, gate_near = phase(
        (terms, slice_far, mlp_out, out_pieces, down_near, up_near, gate_near)
    )
    home = (
        total([slice_pieces[0], *slice_near, slice_far])
        .astype(jnp.bfloat16)
        .reshape(groups, own, 3 * local_width)
    )
    home, terms, out_pieces, down_near, up_near, gate_near = phase(
        (home, terms, out_pieces, down_near, up_near, gate_near)
    )
    home = lax.all_to_all(home, "seq", split_axis=0, concat_axis=0, tiled=True)
    out_arrived = [permute(out_pieces[k], "dp", k) for k in range(1, rows)]
    summed = small_sum(terms, "seq")
    home, out_arrived, summed = phase((home, out_arrived, summed))
    out_proj = total([out_pieces[0], *out_arrived])
    out_gate = total([gate_terms[0], *gate_near])
    out_up = total([up_terms[0], *up_near])
    out_down = total([down_terms[0], *down_near])
    if whole_heads and rows % 2 == 0:
        grad_qkv_out = columns_in_place([home], rows)
    else:
        grad_qkv_out = (
            home.reshape(groups, own, 3, deal[0], deal[2])
            .transpose(1, 2, 3, 0, 4)
            .reshape(own, 3 * D)
            .astype(jnp.float32)
        )
    if not whole_heads:
        out_proj = lax.ppermute(out_proj, ("dp", "seq"), owner)
    layer_output = (resid_mid + mlp_out).astype(jnp.bfloat16)
    grad_normed_attn, grad_qkv_out, out_proj, out_gate, out_up, out_down, layer_output = phase(
        (grad_normed_attn, grad_qkv_out, out_proj, out_gate, out_up, out_down, layer_output)
    )
    grad_input = branch_norm(grad_mid, grad_normed_attn, resid_in, gain_attn)[0]
    return (
        layer_output[None],
        grad_input[None],
        summed[7:],
        summed[0],
        summed[1],
        grad_qkv_out,
        summed[4:7],
        out_proj,
        summed[2],
        summed[3],
        out_gate.T,
        out_up.T,
        out_down,
    )


def solution(mesh):
    placed = (
        P("dp", "seq", None),
        P("dp", None),
        P("dp"),
        P(None, ("dp", "seq")),
        P(("dp", "seq")),
        P(("dp", "seq")),
        P(("dp", "seq"), None),
        P(None, ("dp", "seq")),
        P(("dp", "seq"), None),
        P(("dp", "seq")),
        P(("dp", "seq")),
        P(None, ("dp", "seq")),
        P(None, ("dp", "seq")),
        P(("dp", "seq"), None),
        P("dp", "seq", None),
    )
    return jax.shard_map(
        per_device,
        mesh=mesh,
        in_specs=placed,
        out_specs=(
            P("dp", "seq", None),
            P("dp", "seq", None),
            P(None, ("dp", "seq")),
            P(("dp", "seq")),
            P(("dp", "seq")),
            P(("dp", "seq"), None),
            P(None, ("dp", "seq")),
            P(("dp", "seq"), None),
            P(("dp", "seq")),
            P(("dp", "seq")),
            P(None, ("dp", "seq")),
            P(None, ("dp", "seq")),
            P(("dp", "seq"), None),
        ),
        check_vma=False,
    )
```
